32 devices in a mesh: gx: 2 (over core), gy: 4 (over y, x), gz: 4 (over z).
Axes of the slice: x: 2, y: 2, z: 4, core: 2. Of those that a mesh axis runs over, the one named last changes fastest.
Arguments:
- snapshots: float32 [16, 32, 128, 1024], P(None, 'gx', 'gy', 'gz'), as said below
- diffusivity: float32 [32, 128, 1024], P('gx', 'gy', 'gz'), may hold values from 0.02 to 0.16
Outputs:
- shifted: float32 [16, 32, 128, 1024], P(None, 'gx', 'gy', 'gz')
- reduced: float32 [16, 16], replicated
- sigmas: float32 [16], replicated
The draws below stay inside these ranges and needn't reach their ends.
Inputs may be any that keep to these rules, and one draw needn't show every extreme that they name: `snapshots`: real values.
All inputs are finite; a program needn't handle non-finite values.
Results may differ from the reference program's by a relative error of at most 0.0003.
Values sent between devices are 32-bit elements; how exact they have to be, the bound alone decides.
No kernel may reach another device: no remote copies, remote signals or barrier semaphores. Data moves between devices by JAX's collectives and lax.ppermute only.
A program may use at most 128 MiB of HBM per device.

```python
import math
import jax
import jax.numpy as jnp
import numpy as np
from jax import lax

SNAPS = 16
RANK = 12
SWEEPS = 6
NX = 32
NY = 128
NZ = 1024


def draw_snapshots(key, part):
    key_noise, key_mix = jax.random.split(jax.random.fold_in(key, 17))
    shape = (SNAPS, NX, NY, NZ)
    noise = jnp.clip(jax.random.normal(key_noise, shape, jnp.float32), -6.0, 6.0)
    slope = 2.0
    for axis_pos in (1, 2, 3):
        noise = (noise + jnp.roll(noise, 1, axis=axis_pos)) * 0.70710678
    reflect = jax.random.normal(key_mix, (SNAPS, SNAPS), jnp.float32)
    rotation = jnp.eye(SNAPS, dtype=jnp.float32)
    for reflect_pos in range(SNAPS):
        vector = reflect[reflect_pos]
        image = jnp.dot(rotation, vector, precision=lax.Precision.HIGHEST)
        rotation = rotation - 2.0 / jnp.sum(vector * vector) * (image[:, None] * vector[None, :])
    index = jnp.arange(SNAPS).astype(jnp.float32)
    scales = jnp.where(index < RANK, 3.0 * 0.9 ** index, 0.3 * 0.8 ** (index - RANK))
    mixing = rotation * scales[None, :]
    fields = jnp.einsum('kj,jxyz->kxyz', mixing, noise, precision=lax.Precision.HIGHEST)
    envelope = 1.0 + slope * jnp.arange(NX).astype(jnp.float32) / max(NX - 1, 1)
    return fields * envelope[None, :, None, None]


def steps_of(own_key, dims, cuts, least, largest):
    def one(axis_at, shards_of):
        heights = jax.random.uniform(jax.random.fold_in(jax.random.fold_in(own_key, 6), axis_at), (shards_of,), jnp.float32, least / len(cuts), largest / len(cuts))
        return jnp.repeat(jnp.exp(heights), dims[axis_at] // shards_of).reshape((-1,) + (1,) * (len(dims) - axis_at - 1))

    gain = one(*cuts[0])
    for cut in cuts[1:]:
        gain = gain * one(*cut)
    return gain


def setup_inputs(seed: int = 0) -> dict:
    splits = jax.random.split(jax.random.key(seed), 3)
    return {
        "snapshots": draw_snapshots(jax.random.fold_in(splits[2], 71), 0),
        "diffusivity": jnp.clip(jnp.exp(math.log(0.16) - 2.0794415 * jax.random.uniform(splits[1], (NX, NY, NZ), jnp.float32) ** steps_of(splits[1], (NX, NY, NZ), ((0, 2), (1, 4), (2, 4)), -0.2, 0.2)), 0.02, 0.16),
    }


def round_pairs(count):
    players = list(range(count))
    firsts = []
    seconds = []
    for turn in range(count - 1):
        firsts.append([players[i] for i in range(count // 2)])
        seconds.append([players[count - 1 - i] for i in range(count // 2)])
        players = [players[0]] + [players[-1]] + players[1:-1]
    return (np.array(firsts, dtype=np.int32), np.array(seconds, dtype=np.int32))

def jacobi_eigen(small):
    count = small.shape[0]
    first_np, second_np = round_pairs(count)
    firsts = jnp.asarray(first_np)
    seconds = jnp.asarray(second_np)
    eye = jnp.eye(count, dtype=jnp.float32)
    high = lax.Precision.HIGHEST

    def turn(step, carry):
        mat, vecs = carry
        row = step % (count - 1)
        pidx = firsts[row]
        qidx = seconds[row]
        app = mat[pidx, pidx]
        aqq = mat[qidx, qidx]
        apq = mat[pidx, qidx]
        tau = aqq - app
        sgn = jnp.where(tau >= 0, 1.0, -1.0).astype(jnp.float32)
        denom = jnp.abs(tau) + jnp.sqrt(tau * tau + 4.0 * apq * apq)
        tangent = jnp.where(denom > 0, 2.0 * apq * sgn / jnp.where(denom > 0, denom, 1.0), 0.0)
        cosine = 1.0 / jnp.sqrt(1.0 + tangent * tangent)
        sine = tangent * cosine
        onep = jax.nn.one_hot(pidx, count, dtype=jnp.float32)
        oneq = jax.nn.one_hot(qidx, count, dtype=jnp.float32)
        rot = eye + jnp.dot(onep.T, (cosine - 1.0)[:, None] * onep, precision=high)
        rot = rot + jnp.dot(oneq.T, (cosine - 1.0)[:, None] * oneq, precision=high)
        rot = rot + jnp.dot(onep.T, sine[:, None] * oneq, precision=high)
        rot = rot - jnp.dot(oneq.T, sine[:, None] * onep, precision=high)
        mat = jnp.dot(jnp.dot(rot.T, mat, precision=high), rot, precision=high)
        vecs = jnp.dot(vecs, rot, precision=high)
        return (mat, vecs)
    mat, vecs = lax.fori_loop(0, SWEEPS * (count - 1), turn, (small, eye))
    return (jnp.diagonal(mat), vecs)

def factor_pair(gram, cross):
    lower = jnp.linalg.cholesky(gram)
    proj = lax.linalg.triangular_solve(lower, cross, left_side=True, lower=True)
    return (lower.T, proj)

def finish(upper, proj, ncell):
    high = lax.Precision.HIGHEST
    small = jnp.dot(upper, upper.T, precision=high) / ncell
    lam, vecs = jacobi_eigen(small)
    ordered = jnp.sort(lam)[::-1]
    sigmas = jnp.sqrt(ordered)
    keep = (lam >= ordered[RANK - 1]).astype(jnp.float32)
    projector = jnp.dot(vecs * keep[None, :], vecs.T, precision=high)
    inverse = jnp.dot(vecs * (keep / lam)[None, :], vecs.T, precision=high) / ncell
    reduced = jnp.dot(jnp.dot(projector, proj, precision=high), upper.T, precision=high)
    reduced = jnp.dot(reduced, inverse, precision=high)
    return (reduced, sigmas)

def advance_field(field, diffusivity):

    def near(offset, dim):
        return jnp.roll(field, -offset, axis=dim)
    lap = -6.0 * field
    for dim in range(3):
        lap = lap + near(1, dim) + near(-1, dim)

    def slope(dim):
        return (8.0 * (near(1, dim) - near(-1, dim)) - (near(2, dim) - near(-2, dim))) / 12.0
    return field + diffusivity * lap - (0.3 + 0.02 * field) * slope(2) - 0.2 * slope(0) - 0.15 * slope(1)

def reference(snapshots, diffusivity):
    high = lax.Precision.HIGHEST
    shifted = lax.map(lambda field: advance_field(field, diffusivity), snapshots)
    flat_x = snapshots.reshape(SNAPS, -1)
    flat_y = shifted.reshape(SNAPS, -1)
    gram = jnp.dot(flat_x, flat_x.T, precision=high)
    cross = jnp.dot(flat_x, flat_y.T, precision=high)
    upper, proj = factor_pair(gram, cross)
    reduced, sigmas = finish(upper, proj, float(NX * NY * NZ))
    return (shifted, reduced, sigmas)
```

```python
import functools

import jax
import jax.numpy as jnp
from jax import lax
from jax.experimental import pallas as pl
from jax.experimental.pallas import tpu as pltpu
from jax.sharding import PartitionSpec as P

RANK = 12
SWEEPS = 6
ROWS = 8
LANES = 128
AXES = ("gx", "gy", "gz")
HIGH = lax.Precision.HIGHEST
LAST = (((1,), (1,)), ((), ()))
FIRST = (((0,), (0,)), ((), ()))


def neighbours(low_edge, high_edge, axis):
    count = lax.axis_size(axis)
    forward = [(i, (i + 1) % count) for i in range(count)]
    backward = [(target, source) for source, target in forward]
    return lax.ppermute(high_edge, axis, forward), lax.ppermute(low_edge, axis, backward)


def iota(dim):
    return lax.broadcasted_iota(jnp.int32, (ROWS, LANES), dim)


def pack_kernel(x_ref, low_ref, high_ref):
    snaps, _, ny, nz = x_ref.shape
    tiles = ny // ROWS
    lane = iota(1)
    for group in range(low_ref.shape[1]):
        low = jnp.zeros((ROWS, LANES), jnp.float32)
        high = jnp.zeros((ROWS, LANES), jnp.float32)
        for place in range(min(LANES // 2, snaps * tiles - group * (LANES // 2))):
            snap, tile = divmod(group * (LANES // 2) + place, tiles)
            rows = slice(tile * ROWS, tile * ROWS + ROWS)
            here = (lane >> 1) == place
            low = jnp.where(here, pltpu.roll(x_ref[snap, 0, rows, :LANES], 2 * place, 1), low)
            turn = (2 * place + 2) % LANES
            high = jnp.where(here, pltpu.roll(x_ref[snap, 0, rows, nz - LANES :], turn, 1), high)
        low_ref[0, group] = low
        high_ref[0, group] = high


def pack_edges(x):
    snaps, nx, ny, nz = x.shape
    groups = -(-snaps * (ny // ROWS) * 2 // LANES)
    shape = jax.ShapeDtypeStruct((nx, groups, ROWS, LANES), jnp.float32)
    spec = pl.BlockSpec((1, groups, ROWS, LANES), lambda i: (i, 0, 0, 0))
    return pl.pallas_call(
        pack_kernel,
        grid=(nx,),
        in_specs=[pl.BlockSpec((snaps, 1, ny, nz), lambda i: (0, i, 0, 0))],
        out_specs=[spec, spec],
        out_shape=[shape, shape],
        compiler_params=pltpu.CompilerParams(vmem_limit_bytes=16 << 20),
        cost_estimate=pl.CostEstimate(flops=x.size, bytes_accessed=4 * x.size, transcendentals=0),
        name="pack_edges",
    )(x)


def step_kernel(
    x_hbm, xlow_hbm, xhigh_hbm, ylow_ref, yhigh_ref, zlow_ref, zhigh_ref, diff_ref,
    out_ref, sums_ref, planes, left, right, acc, sems,
):
    snaps, _, ny, nz = out_ref.shape
    nx = pl.num_programs(0)
    step = pl.program_id(0)
    tiles, cols = ny // ROWS, nz // LANES
    half = snaps * ROWS
    total = planes.shape[0]
    row, lane = iota(0), iota(1)

    def fetch(i):
        if i < 2:
            source = xlow_hbm.at[:, i]
        elif i < total - 2:
            source = x_hbm.at[:, i - 2]
        else:
            source = xhigh_hbm.at[:, i - total + 2]
        return pltpu.make_async_copy(source, planes.at[i], sems.at[i])

    @pl.when(step == 0)
    def _():
        for i in range(total):
            fetch(i).start()
        for i in range(4):
            fetch(i).wait()
        acc[...] = jnp.zeros_like(acc)

    pltpu.make_async_copy(x_hbm.at[:, 0], planes.at[step + 4], sems.at[step + 4]).wait()

    def advance(snap):
        def tile(plane, t, c):
            return planes[step + plane, snap, t * ROWS : (t + 1) * ROWS, c * LANES : (c + 1) * LANES]

        centre = [[tile(2, t, c) for c in range(cols)] for t in range(tiles)]
        blank = jnp.zeros((ROWS - 2, nz), jnp.float32)
        under = jnp.concatenate([blank, ylow_ref[snap, 0]], axis=0)
        over = jnp.concatenate([yhigh_ref[snap, 0], blank], axis=0)
        results = []
        for t in range(tiles):
            group, place = divmod(snap * tiles + t, LANES // 2)
            rim = jnp.where(
                lane < LANES // 2,
                pltpu.roll(zhigh_ref[0, group], (LANES - 2 * place) % LANES, 1),
                pltpu.roll(zlow_ref[0, group], (LANES - 2 * place - 2) % LANES, 1),
            )
            ring = centre[t] + [rim]
            for c in range(cols):
                part = slice(c * LANES, (c + 1) * LANES)
                u = centre[t][c]
                above = over[:, part] if t == tiles - 1 else centre[t + 1][c]
                below = under[:, part] if t == 0 else centre[t - 1][c]
                after, before = ring[c + 1], ring[c - 1]
                yp1 = pltpu.roll(jnp.where(row == 0, above, u), ROWS - 1, 0)
                yp2 = pltpu.roll(jnp.where(row < 2, above, u), ROWS - 2, 0)
                ym1 = pltpu.roll(jnp.where(row == ROWS - 1, below, u), 1, 0)
                ym2 = pltpu.roll(jnp.where(row >= ROWS - 2, below, u), 2, 0)
                zp1 = pltpu.roll(jnp.where(lane == 0, after, u), LANES - 1, 1)
                zp2 = pltpu.roll(jnp.where(lane < 2, after, u), LANES - 2, 1)
                zm1 = pltpu.roll(jnp.where(lane == LANES - 1, before, u), 1, 1)
                zm2 = pltpu.roll(jnp.where(lane >= LANES - 2, before, u), 2, 1)
                xp1, xp2, xm1, xm2 = tile(3, t, c), tile(4, t, c), tile(1, t, c), tile(0, t, c)
                lap = (xp1 + xm1) + (yp1 + ym1) + (zp1 + zm1) - 6.0 * u
                zd = 8.0 * (zp1 - zm1) - (zp2 - zm2)
                xyd = 8.0 * ((xp1 - xm1) + 0.75 * (yp1 - ym1)) - ((xp2 - xm2) + 0.75 * (yp2 - ym2))
                diff = diff_ref[0, t * ROWS : (t + 1) * ROWS, part]
                new = (u + diff * lap) - ((0.3 / 12 + 0.02 / 12 * u) * zd + (0.2 / 12) * xyd)
                out_ref[snap, 0, t * ROWS : (t + 1) * ROWS, part] = new
                results.append((t, c, u, new))
        return results

    def split(first, second):
        both = jnp.concatenate([first, second], axis=0)
        high = both.astype(jnp.bfloat16)
        return high, (both - high.astype(jnp.float32)).astype(jnp.bfloat16)

    for pair in range(snaps // 2):
        rows = slice(pair * 2 * ROWS, (pair + 1) * 2 * ROWS)
        low_rows = slice(half + pair * 2 * ROWS, half + (pair + 1) * 2 * ROWS)
        first, second = advance(2 * pair), advance(2 * pair + 1)
        for (t, c, u0, v0), (_, _, u1, v1) in zip(first, second):
            at = slice(t * nz + c * LANES, t * nz + (c + 1) * LANES)
            right[rows, at], right[low_rows, at] = split(u0, u1)
            left[rows, at], left[low_rows, at] = split(v0, v1)

    both = right[...]
    acc[:half] += lax.dot_general(both[:half], both, LAST, preferred_element_type=jnp.float32)
    acc[half:] += lax.dot_general(left[...], both, LAST, preferred_element_type=jnp.float32)

    @pl.when(step == nx - 1)
    def _():
        same = (
            lax.broadcasted_iota(jnp.int32, acc.shape, 0) % ROWS
            == lax.broadcasted_iota(jnp.int32, acc.shape, 1) % ROWS
        )
        folded = jnp.where(same, acc[...], 0.0).reshape(3 * snaps, ROWS, 2 * half).sum(axis=1)
        at = lax.broadcasted_iota(jnp.int32, (LANES, 2 * half), 1)
        to = lax.broadcasted_iota(jnp.int32, (LANES, 2 * half), 0)
        member = (at % half) // ROWS == to % snaps
        every = jnp.where(member, 1.0, 0.0)
        upper = jnp.where(member & (at < half), 1.0, 0.0)
        lower = jnp.where(member & (at >= half), 1.0, 0.0)

        def dot(a, b):
            return lax.dot_general(a, b, LAST, precision=HIGH, preferred_element_type=jnp.float32)

        def spread(a):
            return jnp.concatenate([a] * (LANES // snaps), axis=0)

        own, fresh, rest = folded[:snaps], folded[snaps : 2 * snaps], folded[2 * snaps :]
        gram = dot(own, every) + dot(lower[:snaps], spread(own))
        cross = dot(every[:snaps], spread(fresh)) + dot(upper[:snaps], spread(rest))
        blocks = [gram[i : i + ROWS] for i in range(0, snaps, ROWS)]
        blocks += [cross[i : i + ROWS] for i in range(0, snaps, ROWS)]
        packed = jnp.zeros((ROWS, LANES), jnp.float32)
        for i, block in enumerate(blocks):
            packed = jnp.where(lane // snaps == i, block, packed)
        sums_ref[...] = jnp.broadcast_to(packed[None], sums_ref.shape)


def step_and_sums(x, diff, x_halo, y_halo, z_halo, copies):
    snaps, nx, ny, nz = x.shape
    half = snaps * ROWS
    anywhere = pl.BlockSpec(memory_space=pl.ANY)
    y_spec = pl.BlockSpec((snaps, 1, 2, nz), lambda i: (0, i, 0, 0))
    z_spec = pl.BlockSpec((1,) + z_halo[0].shape[1:], lambda i: (i, 0, 0, 0))
    return pl.pallas_call(
        step_kernel,
        grid=(nx,),
        in_specs=[anywhere] * 3
        + [y_spec] * 2
        + [z_spec] * 2
        + [pl.BlockSpec((1, ny, nz), lambda i: (i, 0, 0))],
        out_specs=[
            pl.BlockSpec((snaps, 1, ny, nz), lambda i: (0, i, 0, 0)),
            pl.BlockSpec((copies, ROWS, LANES), lambda i: (0, 0, 0)),
        ],
        out_shape=[
            jax.ShapeDtypeStruct(x.shape, jnp.float32),
            jax.ShapeDtypeStruct((copies, ROWS, LANES), jnp.float32),
        ],
        scratch_shapes=[
            pltpu.VMEM((nx + 4, snaps, ny, nz), jnp.float32),
            pltpu.VMEM((2 * half, (ny // ROWS) * nz), jnp.bfloat16),
            pltpu.VMEM((2 * half, (ny // ROWS) * nz), jnp.bfloat16),
            pltpu.VMEM((3 * half, 2 * half), jnp.float32),
            pltpu.SemaphoreType.DMA((nx + 4,)),
        ],
        compiler_params=pltpu.CompilerParams(vmem_limit_bytes=48 << 20),
        name="step_and_sums",
    )(x, *x_halo, *y_halo, *z_halo, diff)


def spectral_kernel(ncell, sums_ref, reduced_ref, sigmas_ref):
    count = sigmas_ref.shape[1]
    slots = count // 2
    row, lane = iota(0), iota(1)
    total = sums_ref[0]
    for i in range(1, sums_ref.shape[0]):
        total = total + sums_ref[i]
    total = total * (1.0 / ncell)

    def whole(tile, at):
        return jnp.broadcast_to(tile[at : at + 1], (ROWS, LANES))

    def shift(x, turn):
        return pltpu.roll(x, turn % ROWS, 0)

    gram = [
        [jnp.broadcast_to(total[:, part * count + j : part * count + j + 1], (ROWS, LANES)) for part in range(2)]
        for j in range(count)
    ]
    rows = []
    inverse = [jnp.where(lane == row + count + part * ROWS, 1.0, 0.0) for part in range(2)]
    for j in range(count):
        part, at = divmod(j, ROWS)
        scale = 1.0 / jnp.sqrt(whole(gram[j][part], at))
        column = [jnp.where(row + i * ROWS >= j, gram[j][i] * scale, 0.0) for i in range(2)]
        for m in range(j + 1, count):
            factor = whole(column[m // ROWS], m % ROWS)
            gram[m] = [gram[m][i] - column[i] * factor for i in range(2)]
        line = whole(inverse[part], at) * scale
        for i in range(2):
            index = row + i * ROWS
            inverse[i] = jnp.where(
                index == j, line, inverse[i] - jnp.where(index > j, column[i], 0.0) * line
            )
        rows += column

    back = jnp.zeros((ROWS, LANES), jnp.float32)
    for i in range(slots):
        back = jnp.where(row == i, whole(inverse[1], ROWS - 1 - i), back)
    first = jnp.where(lane < count, jnp.where(lane == row, 1.0, 0.0), inverse[0])
    second = jnp.where(lane < count, jnp.where(lane == count - 1 - row, 1.0, 0.0), back)

    def join(a, b, turn):
        mask = (row & turn) == 0
        return jnp.where(mask, a, b) + jnp.where(mask, shift(a, -turn), shift(b, turn))

    def gather(parts):
        level = [join(parts[i], parts[i + 4], 4) for i in range(4)]
        level = [join(level[i], level[i + 2], 2) for i in range(2)]
        return join(level[0], level[1], 1)

    def norms(rows, players):
        return gather([rows[2 * p] * rows[2 * p] + rows[2 * p + 1] * rows[2 * p + 1] for p in players])

    heads, tails = list(range(slots)), list(range(count - 1, slots - 1, -1))

    def move(top, low):
        return (
            jnp.where(row == 0, top, shift(jnp.where(row == 0, low, top), 1)),
            jnp.where(row == ROWS - 1, top, shift(low, -1)),
        )

    def sweep(_, carry):
        rows, first, second = list(carry[:-2]), carry[-2], carry[-1]
        players = list(range(count))
        app, aqq = norms(rows, heads), norms(rows, tails)
        for turn in range(count - 1):
            pairs = [(players[i], players[count - 1 - i]) for i in range(slots)]
            apq = gather(
                [rows[2 * p] * rows[2 * q] + rows[2 * p + 1] * rows[2 * q + 1] for p, q in pairs]
            )
            tau = aqq - app
            twice = 2.0 * apq
            denom = jnp.abs(tau) + jnp.sqrt(tau * tau + twice * twice)
            signed = jnp.where(tau >= 0, twice, -twice)
            tangent = jnp.where(denom > 0, signed / jnp.where(denom > 0, denom, 1.0), 0.0)
            cosine = lax.rsqrt(1.0 + tangent * tangent)
            sine = tangent * cosine
            for i, (p, q) in enumerate(pairs):
                c, s = whole(cosine, i), whole(sine, i)
                for k in range(2):
                    a, b = rows[2 * p + k], rows[2 * q + k]
                    rows[2 * p + k], rows[2 * q + k] = c * a - s * b, s * a + c * b
            first, second = move(cosine * first - sine * second, sine * first + cosine * second)
            app, aqq = move(app - tangent * apq, aqq + tangent * apq)
            players = [players[0], players[-1]] + players[1:-1]
        return (*rows, first, second)

    carry = lax.fori_loop(0, SWEEPS, sweep, (*rows, first, second))
    rows, first, second = carry[:-2], carry[-2], carry[-1]
    lam = [norms(rows, heads), norms(rows, tails)]
    index = [row, count - 1 - row]
    above = [jnp.zeros((ROWS, LANES), jnp.int32)] * 2
    ahead = [jnp.zeros((ROWS, LANES), jnp.int32)] * 2
    for p in range(count):
        other = whole(lam[0], p) if p < slots else whole(lam[1], count - 1 - p)
        for i in range(2):
            larger = other > lam[i]
            above[i] = above[i] + jnp.where(larger, 1, 0)
            ahead[i] = ahead[i] + jnp.where(larger | ((other == lam[i]) & (p < index[i])), 1, 0)
    keep = [jnp.where(a < RANK, 1.0, 0.0) for a in above]
    ordered = jnp.where(ahead[0] == lane, lam[0], 0.0) + jnp.where(ahead[1] == lane, lam[1], 0.0)
    ordered = jnp.sum(ordered, axis=0, keepdims=True)
    sigmas_ref[...] = jnp.sqrt(ordered)[:, :count]

    weight = [keep[i] / lam[i] for i in range(2)]
    weighted = [first * weight[0], second * weight[1]]
    tail = [jnp.zeros((ROWS, LANES), jnp.float32)] * 2
    for p in range(count):
        line = whole(weighted[0], p) if p < slots else whole(weighted[1], count - 1 - p)
        tail = [tail[k] + rows[2 * p + k] * line for k in range(2)]

    def dot(a, b, dims):
        return lax.dot_general(a, b, dims, precision=HIGH, preferred_element_type=jnp.float32)

    def tall(tiles, offset):
        blank = jnp.zeros((ROWS, LANES), jnp.float32)
        stack = [blank] * (offset // ROWS) + tiles
        return jnp.concatenate(stack + [blank] * (LANES // ROWS - len(stack)), axis=0)

    head = dot(
        jnp.concatenate([first, second], axis=0),
        jnp.concatenate([first * keep[0], second * keep[1]], axis=0),
        FIRST,
    )[:count]
    cross = [
        jnp.where(lane < count, pltpu.roll(total, LANES - (2 + i) * count, 1), 0.0) for i in range(2)
    ]
    plain = (((1,), (0,)), ((), ()))
    middle = dot(head, tall(cross, count), plain)
    reduced_ref[...] = dot(middle, tall(tail, 0), plain)[:, :count]


def spectral(sums, count, ncell):
    return pl.pallas_call(
        functools.partial(spectral_kernel, ncell),
        out_shape=[
            jax.ShapeDtypeStruct((count, count), jnp.float32),
            jax.ShapeDtypeStruct((1, count), jnp.float32),
        ],
        compiler_params=pltpu.CompilerParams(vmem_limit_bytes=16 << 20),
        name="spectral",
    )(sums)


def shards(snapshots, diffusivity):
    snaps, nx, ny, nz = snapshots.shape
    copies = lax.axis_size(AXES)
    x_halo = neighbours(snapshots[:, :2], snapshots[:, nx - 2 :], "gx")
    y_halo = neighbours(snapshots[:, :, :2], snapshots[:, :, ny - 2 :], "gy")
    z_halo = neighbours(*pack_edges(snapshots), "gz")
    shifted, sums = step_and_sums(snapshots, diffusivity, x_halo, y_halo, z_halo, copies)
    sums = lax.all_to_all(sums, AXES, 0, 0, tiled=True)
    ncell = float(nx * ny * nz * copies)
    reduced, sigmas = spectral(sums, snaps, ncell)
    return shifted, reduced, sigmas.reshape(snaps)


def solution(mesh):
    placed = (P(None, "gx", "gy", "gz"), P("gx", "gy", "gz"))
    return jax.shard_map(
        shards,
        mesh=mesh,
        in_specs=placed,
        out_specs=(P(None, "gx", "gy", "gz"), P(), P()),
        check_vma=False,
    )
```

```python
import functools

import jax
import jax.numpy as jnp
from jax import lax
from jax.experimental import pallas as pl
from jax.experimental.pallas import tpu as pltpu
from jax.sharding import PartitionSpec as P

RANK = 12
SWEEPS = 6
ROWS = 8
LANES = 128
AXES = ("gx", "gy", "gz")
HIGH = lax.Precision.HIGHEST
LAST = (((1,), (1,)), ((), ()))
FIRST = (((0,), (0,)), ((), ()))


def neighbours(low_edge, high_edge, axis):
    count = lax.axis_size(axis)
    forward = [(i, (i + 1) % count) for i in range(count)]
    backward = [(target, source) for source, target in forward]
    return lax.ppermute(high_edge, axis, forward), lax.ppermute(low_edge, axis, backward)


def iota(dim):
    return lax.broadcasted_iota(jnp.int32, (ROWS, LANES), dim)


def edges_kernel(x_hbm, xlow_hbm, xhigh_hbm, ylow_ref, yhigh_ref, zlow_ref, zhigh_ref, planes, sems):
    nx, snaps, ny, nz = planes.shape
    tiles = ny // ROWS
    row, lane = iota(0), iota(1)
    copies = [pltpu.make_async_copy(x_hbm.at[:, i], planes.at[i], sems.at[i]) for i in range(nx)]
    copies += [pltpu.make_async_copy(x_hbm.at[:, i], xlow_hbm.at[i], sems.at[nx + i]) for i in range(2)]
    copies += [
        pltpu.make_async_copy(x_hbm.at[:, nx - 2 + i], xhigh_hbm.at[i], sems.at[nx + 2 + i]) for i in range(2)
    ]
    for copy in copies:
        copy.start()

    def plane(x, _):
        pltpu.make_async_copy(x_hbm.at[:, 0], planes.at[x], sems.at[x]).wait()
        for group in range(zlow_ref.shape[1]):
            low = jnp.zeros((ROWS, LANES), jnp.float32)
            high = jnp.zeros((ROWS, LANES), jnp.float32)
            for place in range(min(LANES // 2, snaps * tiles - group * (LANES // 2))):
                snap, tile = divmod(group * (LANES // 2) + place, tiles)
                rows = slice(tile * ROWS, tile * ROWS + ROWS)
                here = (lane >> 1) == place
                low = jnp.where(here, pltpu.roll(planes[x, snap, rows, :LANES], 2 * place, 1), low)
                turn = (2 * place + 2) % LANES
                high = jnp.where(here, pltpu.roll(planes[x, snap, rows, nz - LANES :], turn, 1), high)
            zlow_ref[x, group] = low
            zhigh_ref[x, group] = high
        for group in range(snaps // 4):
            for c in range(nz // LANES):
                part = slice(c * LANES, (c + 1) * LANES)
                low = jnp.zeros((ROWS, LANES), jnp.float32)
                high = jnp.zeros((ROWS, LANES), jnp.float32)
                for place in range(4):
                    here = (row >> 1) == place
                    first = planes[x, 4 * group + place, :ROWS, part]
                    last = planes[x, 4 * group + place, ny - ROWS :, part]
                    low = jnp.where(here, pltpu.roll(first, 2 * place, 0), low)
                    high = jnp.where(here, pltpu.roll(last, (2 * place + 2) % ROWS, 0), high)
                ylow_ref[x, group, :, part] = low
                yhigh_ref[x, group, :, part] = high
        return 0

    lax.fori_loop(0, nx, plane, 0)
    for copy in copies[nx:]:
        copy.wait()


def pack_edges(x):
    snaps, nx, ny, nz = x.shape
    groups = -(-snaps * (ny // ROWS) * 2 // LANES)
    x_edge = jax.ShapeDtypeStruct((2, snaps, ny, nz), jnp.float32)
    y_edge = jax.ShapeDtypeStruct((nx, snaps // 4, ROWS, nz), jnp.float32)
    z_edge = jax.ShapeDtypeStruct((nx, groups, ROWS, LANES), jnp.float32)
    anywhere, inside = pl.BlockSpec(memory_space=pl.ANY), pl.BlockSpec(memory_space=pltpu.VMEM)
    return pl.pallas_call(
        edges_kernel,
        in_specs=[anywhere],
        out_specs=[anywhere] * 2 + [inside] * 4,
        out_shape=[x_edge, x_edge, y_edge, y_edge, z_edge, z_edge],
        scratch_shapes=[
            pltpu.VMEM((nx, snaps, ny, nz), jnp.float32),
            pltpu.SemaphoreType.DMA((nx + 4,)),
        ],
        compiler_params=pltpu.CompilerParams(vmem_limit_bytes=48 << 20),
        name="pack_edges",
    )(x)


def step_kernel(
    x_hbm, xlow_hbm, xhigh_hbm, zlow_hbm, zhigh_hbm, diff_hbm,
    out_hbm, edge, sums_ref, planes, zlow, zhigh, rims, diff, bare, out, left, right, acc, in_sems, out_sems,
):
    nx, _, snaps, _, nz = edge.shape
    ny = diff.shape[1]
    tiles, cols = ny // ROWS, nz // LANES
    half = snaps * ROWS
    total = planes.shape[0]
    per = snaps // tiles
    row, lane = iota(0), iota(1)

    def fetch(i):
        if i < 2:
            source = xlow_hbm.at[i]
        elif i < total - 2:
            source = x_hbm.at[:, i - 2]
        else:
            source = xhigh_hbm.at[i - total + 2]
        return pltpu.make_async_copy(source, planes.at[i], in_sems.at[i])

    small = [(zlow_hbm, zlow), (zhigh_hbm, zhigh), (diff_hbm, diff)]
    small = [pltpu.make_async_copy(a, b, in_sems.at[total + i]) for i, (a, b) in enumerate(small)]
    for copy in small:
        copy.start()
    for i in range(total):
        fetch(i).start()
    acc[...] = jnp.zeros_like(acc)
    left[1] = jnp.zeros_like(left[1])
    right[1] = jnp.zeros_like(right[1])
    for copy in small:
        copy.wait()
    bare[...] = 1.0 - 6.0 * diff[...]

    slots = LANES // 4
    at = lax.broadcasted_iota(jnp.int32, (LANES, LANES), 0)
    to = lax.broadcasted_iota(jnp.int32, (LANES, LANES), 1)
    for group in range(zlow.shape[1]):
        lows = zlow[:, group].reshape(nx * ROWS, LANES)
        highs = zhigh[:, group].reshape(nx * ROWS, LANES)
        for part in range(2):
            origin = 2 * (part * slots + to // 4) + to % 2
            is_low = (to % 4) < 2
            take_low = jnp.where((at == origin) & is_low, 1.0, 0.0)
            take_high = jnp.where((at == origin) & ~is_low, 1.0, 0.0)
            moved = jnp.dot(lows, take_low, precision=HIGH) + jnp.dot(highs, take_high, precision=HIGH)
            rims[:, 2 * group + part] = moved.reshape(nx, ROWS, LANES)

    for i in range(4):
        fetch(i).wait()

    def split(first, second):
        both = jnp.concatenate([first, second], axis=0)
        high = both.astype(jnp.bfloat16)
        return high, (both - high.astype(jnp.float32)).astype(jnp.bfloat16)

    def multiply(slot, t):
        both = right[slot, t].reshape(2 * half, nz)
        fresh = left[slot, t].reshape(2 * half, nz)
        acc[:half] += lax.dot_general(both[:half], both, LAST, preferred_element_type=jnp.float32)
        acc[half:] += lax.dot_general(fresh, both, LAST, preferred_element_type=jnp.float32)

    def advance(x, snap, rim_row, local):
        def tile(plane, t, c):
            return planes[x + plane, snap, t * ROWS : (t + 1) * ROWS, c * LANES : (c + 1) * LANES]

        centre = [[tile(2, t, c) for c in range(cols)] for t in range(tiles)]
        results = {}
        for t in range(tiles):
            place = local * tiles + t
            ring = centre[t] + [pltpu.roll(rim_row, (LANES - 4 * place - 2) % LANES, 1)]
            for c in range(cols):
                part = slice(c * LANES, (c + 1) * LANES)
                u = centre[t][c]
                above = 0.0 if t == tiles - 1 else centre[t + 1][c]
                below = 0.0 if t == 0 else centre[t - 1][c]
                after, before = ring[c + 1], ring[c - 1]
                yp1 = pltpu.roll(jnp.where(row == 0, above, u), ROWS - 1, 0)
                yp2 = pltpu.roll(jnp.where(row < 2, above, u), ROWS - 2, 0)
                ym1 = pltpu.roll(jnp.where(row == ROWS - 1, below, u), 1, 0)
                ym2 = pltpu.roll(jnp.where(row >= ROWS - 2, below, u), 2, 0)
                zp1 = pltpu.roll(jnp.where(lane == 0, after, u), LANES - 1, 1)
                zp2 = pltpu.roll(jnp.where(lane < 2, after, u), LANES - 2, 1)
                zm1 = pltpu.roll(jnp.where(lane == LANES - 1, before, u), 1, 1)
                zm2 = pltpu.roll(jnp.where(lane >= LANES - 2, before, u), 2, 1)
                xp1, xp2, xm1, xm2 = tile(3, t, c), tile(4, t, c), tile(1, t, c), tile(0, t, c)
                around = (xp1 + xm1) + (yp1 + ym1) + (zp1 + zm1)
                zd = 8.0 * (zp1 - zm1) - (zp2 - zm2)
                xyd = 8.0 * ((xp1 - xm1) + 0.75 * (yp1 - ym1)) - ((xp2 - xm2) + 0.75 * (yp2 - ym2))
                rows = slice(t * ROWS, (t + 1) * ROWS)
                new = (bare[x, rows, part] * u + diff[x, rows, part] * around) - (
                    (0.3 / 12 + 0.02 / 12 * u) * zd + (0.2 / 12) * xyd
                )
                if t == 0:
                    edge[x, 0, snap, :, part] = new
                elif t == tiles - 1:
                    edge[x, 1, snap, :, part] = new
                else:
                    out[x, snap, (t - 1) * ROWS : t * ROWS, part] = new
                results[t, c] = (u, new)
        return results

    def plane(x, _):
        slot = lax.rem(x, 2)
        pltpu.make_async_copy(x_hbm.at[:, 0], planes.at[x + 4], in_sems.at[x + 4]).wait()

        def some(j, _):
            multiply(1 - slot, j)
            first_place = j * per * tiles
            turn = LANES - 4 * lax.rem(first_place, slots)
            rim_row = pltpu.roll(rims[x, first_place // slots], turn, 1)
            for pair in range(per // 2):
                at = j * (per // 2) + pair
                first = advance(x, 2 * at, rim_row, 2 * pair)
                second = advance(x, 2 * at + 1, rim_row, 2 * pair + 1)
                for t, c in first:
                    part = slice(c * LANES, (c + 1) * LANES)
                    (u0, v0), (u1, v1) = first[t, c], second[t, c]
                    high, low = split(u0, u1)
                    right[slot, t, 0, at, :, part] = high
                    right[slot, t, 1, at, :, part] = low
                    high, low = split(v0, v1)
                    left[slot, t, 0, at, :, part] = high
                    left[slot, t, 1, at, :, part] = low
            return 0

        lax.fori_loop(0, tiles, some, 0)
        pltpu.make_async_copy(out.at[x], out_hbm.at[:, x, ROWS : ny - ROWS], out_sems.at[x]).start()
        return 0

    lax.fori_loop(0, nx, plane, 0)
    for t in range(tiles):
        multiply((nx - 1) % 2, t)

    same = (
        lax.broadcasted_iota(jnp.int32, acc.shape, 0) % ROWS
        == lax.broadcasted_iota(jnp.int32, acc.shape, 1) % ROWS
    )
    folded = jnp.where(same, acc[...], 0.0).reshape(3 * snaps, ROWS, 2 * half).sum(axis=1)
    at = lax.broadcasted_iota(jnp.int32, (LANES, 2 * half), 1)
    to = lax.broadcasted_iota(jnp.int32, (LANES, 2 * half), 0)
    member = (at % half) // ROWS == to % snaps
    every = jnp.where(member, 1.0, 0.0)
    upper = jnp.where(member & (at < half), 1.0, 0.0)
    lower = jnp.where(member & (at >= half), 1.0, 0.0)

    def dot(a, b):
        return lax.dot_general(a, b, LAST, precision=HIGH, preferred_element_type=jnp.float32)

    def spread(a):
        return jnp.concatenate([a] * (LANES // snaps), axis=0)

    own, fresh, rest = folded[:snaps], folded[snaps : 2 * snaps], folded[2 * snaps :]
    gram = dot(own, every) + dot(lower[:snaps], spread(own))
    cross = dot(every[:snaps], spread(fresh)) + dot(upper[:snaps], spread(rest))
    sums_ref[...] = beside([gram, cross])
    for i in range(nx):
        pltpu.make_async_copy(out.at[i], out_hbm.at[:, i, ROWS : ny - ROWS], out_sems.at[i]).wait()


def beside(squares):
    lane = iota(1)
    snaps = squares[0].shape[0]
    blocks = [square[i : i + ROWS] for square in squares for i in range(0, snaps, ROWS)]
    packed = jnp.zeros((ROWS, LANES), jnp.float32)
    for i, block in enumerate(blocks):
        packed = jnp.where(lane // snaps == i, block, packed)
    return packed


def step_and_sums(x, diff, x_halo, z_halo):
    snaps, nx, ny, nz = x.shape
    half = snaps * ROWS
    tiles = ny // ROWS
    anywhere = pl.BlockSpec(memory_space=pl.ANY)
    pieces = pltpu.VMEM((2, tiles, 2, snaps // 2, 2 * ROWS, nz), jnp.bfloat16)
    z_shape = z_halo[0].shape
    return pl.pallas_call(
        step_kernel,
        in_specs=[anywhere] * 6,
        out_specs=[anywhere, pl.BlockSpec(memory_space=pltpu.VMEM), pl.BlockSpec(memory_space=pltpu.VMEM)],
        out_shape=[
            jax.ShapeDtypeStruct(x.shape, jnp.float32),
            pltpu.VMEM((nx, 2, snaps, ROWS, nz), jnp.float32),
            jax.ShapeDtypeStruct((ROWS, LANES), jnp.float32),
        ],
        scratch_shapes=[
            pltpu.VMEM((nx + 4, snaps, ny, nz), jnp.float32),
            pltpu.VMEM(z_shape, jnp.float32),
            pltpu.VMEM(z_shape, jnp.float32),
            pltpu.VMEM((nx, 2 * z_shape[1], ROWS, LANES), jnp.float32),
            pltpu.VMEM(diff.shape, jnp.float32),
            pltpu.VMEM(diff.shape, jnp.float32),
            pltpu.VMEM((nx, snaps, ny - 2 * ROWS, nz), jnp.float32),
            pieces,
            pieces,
            pltpu.VMEM((3 * half, 2 * half), jnp.float32),
            pltpu.SemaphoreType.DMA((nx + 7,)),
            pltpu.SemaphoreType.DMA((nx,)),
        ],
        compiler_params=pltpu.CompilerParams(vmem_limit_bytes=40 << 20),
        name="step_and_sums",
    )(x, *x_halo, *z_halo, diff)


def finish_kernel(
    _, edge, sums, low_ref, high_ref, own_low, own_high, diff_first, diff_last,
    out_hbm, sums_ref, new, mine, delta, sems,
):
    nx, _, snaps, _, nz = edge.shape
    ny = out_hbm.shape[2]
    row = iota(0)
    groups = snaps // 4
    half = 2 * snaps

    def split(tiles):
        both = jnp.concatenate(tiles, axis=0)
        high = both.astype(jnp.bfloat16)
        return high, (both - high.astype(jnp.float32)).astype(jnp.bfloat16)

    def plane(x, _):
        for side in range(2):
            halo, own = ((low_ref, own_low), (high_ref, own_high))[side]
            for c in range(nz // LANES):
                part = slice(c * LANES, (c + 1) * LANES)
                column = pl.ds(pl.multiple_of((2 * x + side) * nz + c * LANES, LANES), LANES)
                if side == 0:
                    factor = jnp.broadcast_to(diff_first[x, :1, part], (ROWS, LANES)) + 0.1
                else:
                    factor = jnp.broadcast_to(diff_last[x, ROWS - 1 :, part], (ROWS, LANES)) - 0.1
                factor = jnp.where(row % 2 == side, factor, 0.0)
                fixes, owns = [], []
                for group in range(groups):
                    value = halo[x, group, :, part]
                    if side == 0:
                        fix = factor * pltpu.roll(value, ROWS - 1, 0) - 0.0125 * value
                    else:
                        fix = factor * pltpu.roll(value, 1, 0) + 0.0125 * value
                    fixes.append(fix)
                    owns.append(own[x, group, :, part])
                    for place in range(4):
                        snap = 4 * group + place
                        if side == 0:
                            term = jnp.where(row < 2, pltpu.roll(fix, (ROWS - 2 * place) % ROWS, 0), 0.0)
                        else:
                            term = jnp.where(row >= ROWS - 2, pltpu.roll(fix, (ROWS - 2 - 2 * place) % ROWS, 0), 0.0)
                        new[x, side, snap, :, part] = edge[x, side, snap, :, part] + term
                high, low = split(fixes)
                delta[:half, column] = high
                delta[half:, column] = low
                high, low = split(owns)
                mine[:half, column] = high
                mine[half:, column] = low
        pltpu.make_async_copy(new.at[x, 0], out_hbm.at[:, x, :ROWS], sems.at[2 * x]).start()
        pltpu.make_async_copy(new.at[x, 1], out_hbm.at[:, x, ny - ROWS :], sems.at[2 * x + 1]).start()
        return 0

    lax.fori_loop(0, nx, plane, 0)
    product = lax.dot_general(mine[...], delta[...], LAST, preferred_element_type=jnp.float32)
    same = (
        lax.broadcasted_iota(jnp.int32, product.shape, 0) % 2
        == lax.broadcasted_iota(jnp.int32, product.shape, 1) % 2
    )
    at = lax.broadcasted_iota(jnp.int32, (LANES, 2 * half), 1)
    to = lax.broadcasted_iota(jnp.int32, (LANES, 2 * half), 0)
    member = jnp.where((at % half) // 2 == to % snaps, 1.0, 0.0)
    masked = jnp.where(same, product, 0.0)
    extra = jnp.dot(member[:snaps], masked, precision=HIGH)
    extra = lax.dot_general(extra, member, LAST, precision=HIGH, preferred_element_type=jnp.float32)
    total = sums[...] + beside([jnp.zeros_like(extra), extra])
    sums_ref[...] = jnp.broadcast_to(total[None], sums_ref.shape)
    for i in range(nx):
        pltpu.make_async_copy(new.at[i, 0], out_hbm.at[:, i, :ROWS], sems.at[2 * i]).wait()
        pltpu.make_async_copy(new.at[i, 1], out_hbm.at[:, i, ny - ROWS :], sems.at[2 * i + 1]).wait()


def finish(partial, edge, sums, y_halo, own, diff, copies):
    nx, _, snaps, _, nz = edge.shape
    ny = diff.shape[1]
    anywhere, inside = pl.BlockSpec(memory_space=pl.ANY), pl.BlockSpec(memory_space=pltpu.VMEM)
    pieces = pltpu.VMEM((4 * snaps, nx * 2 * nz), jnp.bfloat16)
    return pl.pallas_call(
        finish_kernel,
        in_specs=[anywhere] + [inside] * 8,
        out_specs=[anywhere, inside],
        out_shape=[
            jax.ShapeDtypeStruct(partial.shape, jnp.float32),
            jax.ShapeDtypeStruct((copies, ROWS, LANES), jnp.float32),
        ],
        scratch_shapes=[
            pltpu.VMEM(edge.shape, jnp.float32),
            pieces,
            pieces,
            pltpu.SemaphoreType.DMA((2 * nx,)),
        ],
        input_output_aliases={0: 0},
        compiler_params=pltpu.CompilerParams(vmem_limit_bytes=24 << 20),
        name="finish",
    )(partial, edge, sums, *y_halo, *own, diff[:, :ROWS], diff[:, ny - ROWS :])


def spectral_kernel(ncell, sums_ref, reduced_ref, sigmas_ref):
    count = sigmas_ref.shape[1]
    slots = count // 2
    row, lane = iota(0), iota(1)
    total = sums_ref[0]
    for i in range(1, sums_ref.shape[0]):
        total = total + sums_ref[i]
    total = total * (1.0 / ncell)

    def whole(tile, at):
        return jnp.broadcast_to(tile[at : at + 1], (ROWS, LANES))

    def shift(x, turn):
        return pltpu.roll(x, turn % ROWS, 0)

    gram = [
        [jnp.broadcast_to(total[:, part * count + j : part * count + j + 1], (ROWS, LANES)) for part in range(2)]
        for j in range(count)
    ]
    rows = []
    inverse = [jnp.where(lane == row + count + part * ROWS, 1.0, 0.0) for part in range(2)]
    for j in range(count):
        part, at = divmod(j, ROWS)
        scale = 1.0 / jnp.sqrt(whole(gram[j][part], at))
        column = [jnp.where(row + i * ROWS >= j, gram[j][i] * scale, 0.0) for i in range(2)]
        for m in range(j + 1, count):
            factor = whole(column[m // ROWS], m % ROWS)
            gram[m] = [gram[m][i] - column[i] * factor for i in range(2)]
        line = whole(inverse[part], at) * scale
        for i in range(2):
            index = row + i * ROWS
            inverse[i] = jnp.where(
                index == j, line, inverse[i] - jnp.where(index > j, column[i], 0.0) * line
            )
        rows += column

    back = jnp.zeros((ROWS, LANES), jnp.float32)
    for i in range(slots):
        back = jnp.where(row == i, whole(inverse[1], ROWS - 1 - i), back)
    first = jnp.where(lane < count, jnp.where(lane == row, 1.0, 0.0), inverse[0])
    second = jnp.where(lane < count, jnp.where(lane == count - 1 - row, 1.0, 0.0), back)

    def join(a, b, turn):
        mask = (row & turn) == 0
        return jnp.where(mask, a, b) + jnp.where(mask, shift(a, -turn), shift(b, turn))

    def gather(parts):
        level = [join(parts[i], parts[i + 4], 4) for i in range(4)]
        level = [join(level[i], level[i + 2], 2) for i in range(2)]
        return join(level[0], level[1], 1)

    def norms(rows, players):
        return gather([rows[2 * p] * rows[2 * p] + rows[2 * p + 1] * rows[2 * p + 1] for p in players])

    heads, tails = list(range(slots)), list(range(count - 1, slots - 1, -1))

    def move(top, low):
        return (
            jnp.where(row == 0, top, shift(jnp.where(row == 0, low, top), 1)),
            jnp.where(row == ROWS - 1, top, shift(low, -1)),
        )

    def sweep(_, carry):
        rows, first, second = list(carry[:-2]), carry[-2], carry[-1]
        players = list(range(count))
        app, aqq = norms(rows, heads), norms(rows, tails)
        for turn in range(count - 1):
            pairs = [(players[i], players[count - 1 - i]) for i in range(slots)]
            apq = gather(
                [rows[2 * p] * rows[2 * q] + rows[2 * p + 1] * rows[2 * q + 1] for p, q in pairs]
            )
            tau = aqq - app
            twice = 2.0 * apq
            denom = jnp.abs(tau) + jnp.sqrt(tau * tau + twice * twice)
            signed = jnp.where(tau >= 0, twice, -twice)
            tangent = jnp.where(denom > 0, signed / jnp.where(denom > 0, denom, 1.0), 0.0)
            cosine = lax.rsqrt(1.0 + tangent * tangent)
            sine = tangent * cosine
            for i, (p, q) in enumerate(pairs):
                c, s = whole(cosine, i), whole(sine, i)
                for k in range(2):
                    a, b = rows[2 * p + k], rows[2 * q + k]
                    rows[2 * p + k], rows[2 * q + k] = c * a - s * b, s * a + c * b
            first, second = move(cosine * first - sine * second, sine * first + cosine * second)
            app, aqq = move(app - tangent * apq, aqq + tangent * apq)
            players = [players[0], players[-1]] + players[1:-1]
        return (*rows, first, second)

    carry = lax.fori_loop(0, SWEEPS, sweep, (*rows, first, second))
    rows, first, second = carry[:-2], carry[-2], carry[-1]
    lam = [norms(rows, heads), norms(rows, tails)]
    index = [row, count - 1 - row]
    above = [jnp.zeros((ROWS, LANES), jnp.int32)] * 2
    ahead = [jnp.zeros((ROWS, LANES), jnp.int32)] * 2
    for p in range(count):
        other = whole(lam[0], p) if p < slots else whole(lam[1], count - 1 - p)
        for i in range(2):
            larger = other > lam[i]
            above[i] = above[i] + jnp.where(larger, 1, 0)
            ahead[i] = ahead[i] + jnp.where(larger | ((other == lam[i]) & (p < index[i])), 1, 0)
    keep = [jnp.where(a < RANK, 1.0, 0.0) for a in above]
    ordered = jnp.where(ahead[0] == lane, lam[0], 0.0) + jnp.where(ahead[1] == lane, lam[1], 0.0)
    ordered = jnp.sum(ordered, axis=0, keepdims=True)
    sigmas_ref[...] = jnp.sqrt(ordered)[:, :count]

    weight = [keep[i] / lam[i] for i in range(2)]
    weighted = [first * weight[0], second * weight[1]]
    tail = [jnp.zeros((ROWS, LANES), jnp.float32)] * 2
    for p in range(count):
        line = whole(weighted[0], p) if p < slots else whole(weighted[1], count - 1 - p)
        tail = [tail[k] + rows[2 * p + k] * line for k in range(2)]

    def dot(a, b, dims):
        return lax.dot_general(a, b, dims, precision=HIGH, preferred_element_type=jnp.float32)

    def tall(tiles, offset):
        blank = jnp.zeros((ROWS, LANES), jnp.float32)
        stack = [blank] * (offset // ROWS) + tiles
        return jnp.concatenate(stack + [blank] * (LANES // ROWS - len(stack)), axis=0)

    head = dot(
        jnp.concatenate([first, second], axis=0),
        jnp.concatenate([first * keep[0], second * keep[1]], axis=0),
        FIRST,
    )[:count]
    cross = [
        jnp.where(lane < count, pltpu.roll(total, LANES - (2 + i) * count, 1), 0.0) for i in range(2)
    ]
    plain = (((1,), (0,)), ((), ()))
    middle = dot(head, tall(cross, count), plain)
    reduced_ref[...] = dot(middle, tall(tail, 0), plain)[:, :count]


def spectral(sums, count, ncell):
    return pl.pallas_call(
        functools.partial(spectral_kernel, ncell),
        out_shape=[
            jax.ShapeDtypeStruct((count, count), jnp.float32),
            jax.ShapeDtypeStruct((1, count), jnp.float32),
        ],
        compiler_params=pltpu.CompilerParams(vmem_limit_bytes=16 << 20),
        name="spectral",
    )(sums)


def shards(snapshots, diffusivity):
    snaps, nx, ny, nz = snapshots.shape
    copies = lax.axis_size(AXES)
    snapshots = pltpu.with_memory_space_constraint(snapshots, pltpu.HBM)
    x_low, x_high, y_low, y_high, z_low, z_high = pack_edges(snapshots)
    y_halo = neighbours(y_low, y_high, "gy")
    z_halo = neighbours(z_low, z_high, "gz")
    x_halo = neighbours(x_low, x_high, "gx")
    partial, edge, sums = step_and_sums(snapshots, diffusivity, x_halo, z_halo)
    edge = pltpu.with_memory_space_constraint(edge, pltpu.VMEM)
    shifted, sums = finish(partial, edge, sums, y_halo, (y_low, y_high), diffusivity, copies)
    sums = lax.all_to_all(sums, AXES, 0, 0, tiled=True)
    ncell = float(nx * ny * nz * copies)
    reduced, sigmas = spectral(sums, snaps, ncell)
    return shifted, reduced, sigmas.reshape(snaps)


def solution(mesh):
    placed = (P(None, "gx", "gy", "gz"), P("gx", "gy", "gz"))
    return jax.shard_map(
        shards,
        mesh=mesh,
        in_specs=placed,
        out_specs=(P(None, "gx", "gy", "gz"), P(), P()),
        check_vma=False,
    )
```

```python
import functools

import jax
import jax.numpy as jnp
from jax import lax
from jax.experimental import pallas as pl
from jax.experimental.pallas import tpu as pltpu
from jax.sharding import PartitionSpec as P

RANK = 12
SWEEPS = 6
ROWS = 8
LANES = 128
AXES = ("gx", "gy", "gz")
HIGH = lax.Precision.HIGHEST
LAST = (((1,), (1,)), ((), ()))
FIRST = (((0,), (0,)), ((), ()))


def neighbours(low_edge, high_edge, axis):
    count = lax.axis_size(axis)
    forward = [(i, (i + 1) % count) for i in range(count)]
    backward = [(target, source) for source, target in forward]
    return lax.ppermute(high_edge, axis, forward), lax.ppermute(low_edge, axis, backward)


def iota(dim):
    return lax.broadcasted_iota(jnp.int32, (ROWS, LANES), dim)


def edges_kernel(x_hbm, xedge_hbm, planes, ylow_ref, yhigh_ref, zlow_ref, zhigh_ref, sems):
    total, cols, snaps, height, _ = planes.shape
    nx, ny = total - 4, height - 2 * ROWS
    tiles = ny // ROWS
    row, lane = iota(0), iota(1)

    def fetch(i, c):
        return pltpu.make_async_copy(
            x_hbm.at[:, i, :, c * LANES : (c + 1) * LANES],
            planes.at[i + 2, c, :, ROWS : ROWS + ny],
            sems.at[i * cols + c],
        )

    for i in range(nx):
        for c in range(cols):
            fetch(i, c).start()
    edges = [
        pltpu.make_async_copy(x_hbm.at[:, i], xedge_hbm.at[k], sems.at[nx * cols + k])
        for k, i in enumerate((0, 1, nx - 2, nx - 1))
    ]
    for copy in edges:
        copy.start()
    blank = jnp.zeros((snaps, ROWS, LANES), jnp.float32)

    def clear(i, _):
        for c in range(cols):
            planes[i, c, :, :ROWS] = blank
            planes[i, c, :, ROWS + ny :] = blank
        return 0

    lax.fori_loop(0, total, clear, 0)

    def plane(x, _):
        for c in range(cols):
            pltpu.make_async_copy(
                x_hbm.at[:, 0, :, :LANES], planes.at[x + 2, c, :, ROWS : ROWS + ny], sems.at[x * cols + c]
            ).wait()
        for group in range(zlow_ref.shape[1]):
            low = jnp.zeros((ROWS, LANES), jnp.float32)
            high = jnp.zeros((ROWS, LANES), jnp.float32)
            for place in range(min(LANES // 2, snaps * tiles - group * (LANES // 2))):
                snap, tile = divmod(group * (LANES // 2) + place, tiles)
                rows = slice((tile + 1) * ROWS, (tile + 2) * ROWS)
                here = (lane >> 1) == place
                low = jnp.where(here, pltpu.roll(planes[x + 2, 0, snap, rows], 2 * place, 1), low)
                turn = (2 * place + 2) % LANES
                high = jnp.where(here, pltpu.roll(planes[x + 2, cols - 1, snap, rows], turn, 1), high)
            zlow_ref[x, group] = low
            zhigh_ref[x, group] = high
        for group in range(snaps // 4):
            for c in range(cols):
                part = slice(c * LANES, (c + 1) * LANES)
                low = jnp.zeros((ROWS, LANES), jnp.float32)
                high = jnp.zeros((ROWS, LANES), jnp.float32)
                for place in range(4):
                    here = (row >> 1) == place
                    first = planes[x + 2, c, 4 * group + place, ROWS : 2 * ROWS]
                    last = planes[x + 2, c, 4 * group + place, ny : ny + ROWS]
                    low = jnp.where(here, pltpu.roll(first, 2 * place, 0), low)
                    high = jnp.where(here, pltpu.roll(last, (2 * place + 2) % ROWS, 0), high)
                ylow_ref[x, group, :, part] = low
                yhigh_ref[x, group, :, part] = high
        return 0

    lax.fori_loop(0, nx, plane, 0)
    for copy in edges:
        copy.wait()


def pack_edges(x):
    snaps, nx, ny, nz = x.shape
    cols = nz // LANES
    groups = -(-snaps * (ny // ROWS) * 2 // LANES)
    x_edge = jax.ShapeDtypeStruct((4, snaps, ny, nz), jnp.float32)
    planes = pltpu.VMEM((nx + 4, cols, snaps, ny + 2 * ROWS, LANES), jnp.float32)
    y_edge = jax.ShapeDtypeStruct((nx, snaps // 4, ROWS, nz), jnp.float32)
    z_edge = jax.ShapeDtypeStruct((nx, groups, ROWS, LANES), jnp.float32)
    anywhere, inside = pl.BlockSpec(memory_space=pl.ANY), pl.BlockSpec(memory_space=pltpu.VMEM)
    return pl.pallas_call(
        edges_kernel,
        in_specs=[anywhere],
        out_specs=[anywhere] + [inside] * 5,
        out_shape=[x_edge, planes, y_edge, y_edge, z_edge, z_edge],
        scratch_shapes=[pltpu.SemaphoreType.DMA((nx * cols + 4,))],
        compiler_params=pltpu.CompilerParams(vmem_limit_bytes=8 << 20),
        name="pack_edges",
    )(x)


def step_kernel(
    x_places, _, xlow_hbm, xhigh_hbm, zlow_hbm, zhigh_hbm, diff_hbm,
    out_hbm, planes, edge, sums_ref, zlow, zhigh, rims, rim_tiles, diff, bare, out, left, right, acc, in_sems, out_sems,
):
    nx, _, snaps, _, nz = edge.shape
    ny = diff.shape[1]
    tiles, cols = ny // ROWS, nz // LANES
    half = snaps * ROWS
    per = snaps // 2
    row, lane = iota(0), iota(1)

    def fetch(i, c):
        source = xlow_hbm.at[x_places[0] + i] if i < 2 else xhigh_hbm.at[x_places[1] + i - 2]
        return pltpu.make_async_copy(
            source.at[:, :, c * LANES : (c + 1) * LANES],
            planes.at[i if i < 2 else nx + i, c, :, ROWS : ROWS + ny],
            in_sems.at[i * cols + c],
        )

    small = [(zlow_hbm, zlow), (zhigh_hbm, zhigh), (diff_hbm, diff)]
    small = [pltpu.make_async_copy(a, b, in_sems.at[4 * cols + i]) for i, (a, b) in enumerate(small)]
    for copy in small:
        copy.start()
    for i in range(4):
        for c in range(cols):
            fetch(i, c).start()
    acc[...] = jnp.zeros_like(acc)
    left[1] = jnp.zeros_like(left[1])
    right[1] = jnp.zeros_like(right[1])
    for copy in small:
        copy.wait()
    bare[...] = 1.0 - 6.0 * diff[...]

    slots = LANES // 4
    at = lax.broadcasted_iota(jnp.int32, (LANES, LANES), 0)
    to = lax.broadcasted_iota(jnp.int32, (LANES, LANES), 1)
    for group in range(zlow.shape[1]):
        lows = zlow[:, group].reshape(nx * ROWS, LANES)
        highs = zhigh[:, group].reshape(nx * ROWS, LANES)
        for part in range(2):
            origin = 2 * (part * slots + to // 4) + to % 2
            is_low = (to % 4) < 2
            take_low = jnp.where((at == origin) & is_low, 1.0, 0.0)
            take_high = jnp.where((at == origin) & ~is_low, 1.0, 0.0)
            moved = jnp.dot(lows, take_low, precision=HIGH) + jnp.dot(highs, take_high, precision=HIGH)
            rims[:, 2 * group + part] = moved.reshape(nx, ROWS, LANES)

    for i in range(4):
        for c in range(cols):
            fetch(i, c).wait()

    def split(first, second):
        both = jnp.concatenate([first, second], axis=0)
        high = both.astype(jnp.bfloat16)
        return high, (both - high.astype(jnp.float32)).astype(jnp.bfloat16)

    def multiply(slot, part):
        def wide(pieces):
            several = [pieces[slot, part * (tiles // 2) + t].reshape(2 * half, nz) for t in range(tiles // 2)]
            return jnp.concatenate(several, axis=1)

        both, fresh = wide(right), wide(left)
        acc[:half] += lax.dot_general(both[:half], both, LAST, preferred_element_type=jnp.float32)
        acc[half:] += lax.dot_general(fresh, both, LAST, preferred_element_type=jnp.float32)

    def advance(x, snap, t, c):
        rows, part = slice(t * ROWS, (t + 1) * ROWS), slice(c * LANES, (c + 1) * LANES)

        def at(plane, dy=0, c=c):
            return planes[x + plane, c, snap, (t + 1) * ROWS + dy : (t + 2) * ROWS + dy]

        u = at(2)
        rim = rim_tiles[snap * tiles + t]
        after = rim if c == cols - 1 else at(2, 0, c + 1)
        before = rim if c == 0 else at(2, 0, c - 1)
        zp1 = pltpu.roll(jnp.where(lane == 0, after, u), LANES - 1, 1)
        zp2 = pltpu.roll(jnp.where(lane < 2, after, u), LANES - 2, 1)
        zm1 = pltpu.roll(jnp.where(lane == LANES - 1, before, u), 1, 1)
        zm2 = pltpu.roll(jnp.where(lane >= LANES - 2, before, u), 2, 1)
        yp1, yp2, ym1, ym2 = at(2, 1), at(2, 2), at(2, -1), at(2, -2)
        xp1, xp2, xm1, xm2 = at(3), at(4), at(1), at(0)
        around = (xp1 + xm1) + (yp1 + ym1) + (zp1 + zm1)
        zd = 8.0 * (zp1 - zm1) - (zp2 - zm2)
        xyd = 8.0 * ((xp1 - xm1) + 0.75 * (yp1 - ym1)) - ((xp2 - xm2) + 0.75 * (yp2 - ym2))
        new = (bare[x, rows, part] * u + diff[x, rows, part] * around) - (
            (0.3 / 12 + 0.02 / 12 * u) * zd + (0.2 / 12) * xyd
        )
        if t == 0:
            edge[x, 0, snap, :, part] = new
        elif t == tiles - 1:
            edge[x, 1, snap, :, part] = new
        else:
            out[x, snap, (t - 1) * ROWS : t * ROWS, part] = new
        return u, new

    def plane(x, _):
        slot = lax.rem(x, 2)

        for place in range(snaps * tiles):
            turn = (LANES - 4 * (place % slots) - 2) % LANES
            rim_tiles[place] = pltpu.roll(rims[x, place // slots], turn, 1)

        def some(j, _):
            multiply(1 - slot, j)
            for pair in range(per // 2):
                at = j * (per // 2) + pair
                for t in range(tiles):
                    for c in range(cols):
                        part = slice(c * LANES, (c + 1) * LANES)
                        u0, v0 = advance(x, 2 * at, t, c)
                        u1, v1 = advance(x, 2 * at + 1, t, c)
                        high, low = split(u0, u1)
                        right[slot, t, 0, at, :, part] = high
                        right[slot, t, 1, at, :, part] = low
                        high, low = split(v0, v1)
                        left[slot, t, 0, at, :, part] = high
                        left[slot, t, 1, at, :, part] = low
            return 0

        lax.fori_loop(0, 2, some, 0)
        pltpu.make_async_copy(out.at[x], out_hbm.at[:, x, ROWS : ny - ROWS], out_sems.at[x]).start()
        return 0

    lax.fori_loop(0, nx, plane, 0)
    for part in range(2):
        multiply((nx - 1) % 2, part)

    same = (
        lax.broadcasted_iota(jnp.int32, acc.shape, 0) % ROWS
        == lax.broadcasted_iota(jnp.int32, acc.shape, 1) % ROWS
    )
    folded = jnp.where(same, acc[...], 0.0).reshape(3 * snaps, ROWS, 2 * half).sum(axis=1)
    at = lax.broadcasted_iota(jnp.int32, (LANES, 2 * half), 1)
    to = lax.broadcasted_iota(jnp.int32, (LANES, 2 * half), 0)
    member = (at % half) // ROWS == to % snaps
    every = jnp.where(member, 1.0, 0.0)
    upper = jnp.where(member & (at < half), 1.0, 0.0)
    lower = jnp.where(member & (at >= half), 1.0, 0.0)

    def dot(a, b):
        return lax.dot_general(a, b, LAST, precision=HIGH, preferred_element_type=jnp.float32)

    def spread(a):
        return jnp.concatenate([a] * (LANES // snaps), axis=0)

    own, fresh, rest = folded[:snaps], folded[snaps : 2 * snaps], folded[2 * snaps :]
    gram = dot(own, every) + dot(lower[:snaps], spread(own))
    cross = dot(every[:snaps], spread(fresh)) + dot(upper[:snaps], spread(rest))
    sums_ref[...] = beside([gram, cross])
    for i in range(nx):
        pltpu.make_async_copy(out.at[i], out_hbm.at[:, i, ROWS : ny - ROWS], out_sems.at[i]).wait()


def beside(squares):
    lane = iota(1)
    snaps = squares[0].shape[0]
    blocks = [square[i : i + ROWS] for square in squares for i in range(0, snaps, ROWS)]
    packed = jnp.zeros((ROWS, LANES), jnp.float32)
    for i, block in enumerate(blocks):
        packed = jnp.where(lane // snaps == i, block, packed)
    return packed


def step_and_sums(planes, diff, x_halo, x_places, z_halo):
    total, cols, snaps, height, _ = planes.shape
    nx, ny, nz = diff.shape
    half = snaps * ROWS
    tiles = ny // ROWS
    anywhere, inside = pl.BlockSpec(memory_space=pl.ANY), pl.BlockSpec(memory_space=pltpu.VMEM)
    pieces = pltpu.VMEM((2, tiles, 2, snaps // 2, 2 * ROWS, nz), jnp.bfloat16)
    z_shape = z_halo[0].shape
    return pl.pallas_call(
        functools.partial(step_kernel, x_places),
        in_specs=[inside] + [anywhere] * 5,
        out_specs=[anywhere] + [inside] * 3,
        out_shape=[
            jax.ShapeDtypeStruct((snaps, nx, ny, nz), jnp.float32),
            pltpu.VMEM(planes.shape, jnp.float32),
            pltpu.VMEM((nx, 2, snaps, ROWS, nz), jnp.float32),
            jax.ShapeDtypeStruct((ROWS, LANES), jnp.float32),
        ],
        scratch_shapes=[
            pltpu.VMEM(z_shape, jnp.float32),
            pltpu.VMEM(z_shape, jnp.float32),
            pltpu.VMEM((nx, 2 * z_shape[1], ROWS, LANES), jnp.float32),
            pltpu.VMEM((snaps * tiles, ROWS, LANES), jnp.float32),
            pltpu.VMEM(diff.shape, jnp.float32),
            pltpu.VMEM(diff.shape, jnp.float32),
            pltpu.VMEM((nx, snaps, ny - 2 * ROWS, nz), jnp.float32),
            pieces,
            pieces,
            pltpu.VMEM((3 * half, 2 * half), jnp.float32),
            pltpu.SemaphoreType.DMA((4 * cols + 3,)),
            pltpu.SemaphoreType.DMA((nx,)),
        ],
        input_output_aliases={0: 1},
        compiler_params=pltpu.CompilerParams(vmem_limit_bytes=20 << 20),
        name="step_and_sums",
    )(planes, *x_halo, *z_halo, diff)


def finish_kernel(
    _, edge, sums, low_ref, high_ref, own_low, own_high, diff_first, diff_last,
    out_hbm, sums_ref, new, mine, delta, sems,
):
    nx, _, snaps, _, nz = edge.shape
    ny = out_hbm.shape[2]
    row = iota(0)
    groups = snaps // 4
    half = 2 * snaps

    def split(tiles):
        both = jnp.concatenate(tiles, axis=0)
        high = both.astype(jnp.bfloat16)
        return high, (both - high.astype(jnp.float32)).astype(jnp.bfloat16)

    def plane(x, _):
        for side in range(2):
            halo, own = ((low_ref, own_low), (high_ref, own_high))[side]
            for c in range(nz // LANES):
                part = slice(c * LANES, (c + 1) * LANES)
                column = pl.ds(pl.multiple_of((2 * x + side) * nz + c * LANES, LANES), LANES)
                if side == 0:
                    factor = jnp.broadcast_to(diff_first[x, :1, part], (ROWS, LANES)) + 0.1
                else:
                    factor = jnp.broadcast_to(diff_last[x, ROWS - 1 :, part], (ROWS, LANES)) - 0.1
                factor = jnp.where(row % 2 == side, factor, 0.0)
                fixes, owns = [], []
                for group in range(groups):
                    value = halo[x, group, :, part]
                    if side == 0:
                        fix = factor * pltpu.roll(value, ROWS - 1, 0) - 0.0125 * value
                    else:
                        fix = factor * pltpu.roll(value, 1, 0) + 0.0125 * value
                    fixes.append(fix)
                    owns.append(own[x, group, :, part])
                    for place in range(4):
                        snap = 4 * group + place
                        if side == 0:
                            term = jnp.where(row < 2, pltpu.roll(fix, (ROWS - 2 * place) % ROWS, 0), 0.0)
                        else:
                            term = jnp.where(row >= ROWS - 2, pltpu.roll(fix, (ROWS - 2 - 2 * place) % ROWS, 0), 0.0)
                        new[x, side, snap, :, part] = edge[x, side, snap, :, part] + term
                high, low = split(fixes)
                delta[:half, column] = high
                delta[half:, column] = low
                high, low = split(owns)
                mine[:half, column] = high
                mine[half:, column] = low
        pltpu.make_async_copy(new.at[x, 0], out_hbm.at[:, x, :ROWS], sems.at[2 * x]).start()
        pltpu.make_async_copy(new.at[x, 1], out_hbm.at[:, x, ny - ROWS :], sems.at[2 * x + 1]).start()
        return 0

    lax.fori_loop(0, nx, plane, 0)
    product = lax.dot_general(mine[...], delta[...], LAST, preferred_element_type=jnp.float32)
    same = (
        lax.broadcasted_iota(jnp.int32, product.shape, 0) % 2
        == lax.broadcasted_iota(jnp.int32, product.shape, 1) % 2
    )
    at = lax.broadcasted_iota(jnp.int32, (LANES, 2 * half), 1)
    to = lax.broadcasted_iota(jnp.int32, (LANES, 2 * half), 0)
    member = jnp.where((at % half) // 2 == to % snaps, 1.0, 0.0)
    masked = jnp.where(same, product, 0.0)
    extra = jnp.dot(member[:snaps], masked, precision=HIGH)
    extra = lax.dot_general(extra, member, LAST, precision=HIGH, preferred_element_type=jnp.float32)
    total = sums[...] + beside([jnp.zeros_like(extra), extra])
    sums_ref[...] = jnp.broadcast_to(total[None], sums_ref.shape)
    for i in range(nx):
        pltpu.make_async_copy(new.at[i, 0], out_hbm.at[:, i, :ROWS], sems.at[2 * i]).wait()
        pltpu.make_async_copy(new.at[i, 1], out_hbm.at[:, i, ny - ROWS :], sems.at[2 * i + 1]).wait()


def finish(partial, edge, sums, y_halo, own, diff, copies):
    nx, _, snaps, _, nz = edge.shape
    ny = diff.shape[1]
    anywhere, inside = pl.BlockSpec(memory_space=pl.ANY), pl.BlockSpec(memory_space=pltpu.VMEM)
    pieces = pltpu.VMEM((4 * snaps, nx * 2 * nz), jnp.bfloat16)
    return pl.pallas_call(
        finish_kernel,
        in_specs=[anywhere] + [inside] * 8,
        out_specs=[anywhere, inside],
        out_shape=[
            jax.ShapeDtypeStruct(partial.shape, jnp.float32),
            jax.ShapeDtypeStruct((copies, ROWS, LANES), jnp.float32),
        ],
        scratch_shapes=[
            pltpu.VMEM(edge.shape, jnp.float32),
            pieces,
            pieces,
            pltpu.SemaphoreType.DMA((2 * nx,)),
        ],
        input_output_aliases={0: 0},
        compiler_params=pltpu.CompilerParams(vmem_limit_bytes=24 << 20),
        name="finish",
    )(partial, edge, sums, *y_halo, *own, diff[:, :ROWS], diff[:, ny - ROWS :])


def spectral_kernel(ncell, sums_ref, reduced_ref, sigmas_ref):
    count = sigmas_ref.shape[1]
    slots = count // 2
    row, lane = iota(0), iota(1)
    total = sums_ref[0]
    for i in range(1, sums_ref.shape[0]):
        total = total + sums_ref[i]
    total = total * (1.0 / ncell)

    def whole(tile, at):
        return jnp.broadcast_to(tile[at : at + 1], (ROWS, LANES))

    def shift(x, turn):
        return pltpu.roll(x, turn % ROWS, 0)

    gram = [
        [jnp.broadcast_to(total[:, part * count + j : part * count + j + 1], (ROWS, LANES)) for part in range(2)]
        for j in range(count)
    ]
    rows = []
    inverse = [jnp.where(lane == row + count + part * ROWS, 1.0, 0.0) for part in range(2)]
    for j in range(count):
        part, at = divmod(j, ROWS)
        scale = 1.0 / jnp.sqrt(whole(gram[j][part], at))
        column = [jnp.where(row + i * ROWS >= j, gram[j][i] * scale, 0.0) for i in range(2)]
        for m in range(j + 1, count):
            factor = whole(column[m // ROWS], m % ROWS)
            gram[m] = [gram[m][i] - column[i] * factor for i in range(2)]
        line = whole(inverse[part], at) * scale
        for i in range(2):
            index = row + i * ROWS
            inverse[i] = jnp.where(
                index == j, line, inverse[i] - jnp.where(index > j, column[i], 0.0) * line
            )
        rows += column

    back = jnp.zeros((ROWS, LANES), jnp.float32)
    for i in range(slots):
        back = jnp.where(row == i, whole(inverse[1], ROWS - 1 - i), back)
    first = jnp.where(lane < count, jnp.where(lane == row, 1.0, 0.0), inverse[0])
    second = jnp.where(lane < count, jnp.where(lane == count - 1 - row, 1.0, 0.0), back)

    def join(a, b, turn):
        mask = (row & turn) == 0
        return jnp.where(mask, a, b) + jnp.where(mask, shift(a, -turn), shift(b, turn))

    def gather(parts):
        level = [join(parts[i], parts[i + 4], 4) for i in range(4)]
        level = [join(level[i], level[i + 2], 2) for i in range(2)]
        return join(level[0], level[1], 1)

    def norms(rows, players):
        return gather([rows[2 * p] * rows[2 * p] + rows[2 * p + 1] * rows[2 * p + 1] for p in players])

    heads, tails = list(range(slots)), list(range(count - 1, slots - 1, -1))

    def move(top, low):
        return (
            jnp.where(row == 0, top, shift(jnp.where(row == 0, low, top), 1)),
            jnp.where(row == ROWS - 1, top, shift(low, -1)),
        )

    def sweep(_, carry):
        rows, first, second = list(carry[:-2]), carry[-2], carry[-1]
        players = list(range(count))
        app, aqq = norms(rows, heads), norms(rows, tails)
        for turn in range(count - 1):
            pairs = [(players[i], players[count - 1 - i]) for i in range(slots)]
            apq = gather(
                [rows[2 * p] * rows[2 * q] + rows[2 * p + 1] * rows[2 * q + 1] for p, q in pairs]
            )
            tau = aqq - app
            twice = 2.0 * apq
            denom = jnp.abs(tau) + jnp.sqrt(tau * tau + twice * twice)
            signed = jnp.where(tau >= 0, twice, -twice)
            tangent = jnp.where(denom > 0, signed / jnp.where(denom > 0, denom, 1.0), 0.0)
            cosine = lax.rsqrt(1.0 + tangent * tangent)
            sine = tangent * cosine
            for i, (p, q) in enumerate(pairs):
                c, s = whole(cosine, i), whole(sine, i)
                for k in range(2):
                    a, b = rows[2 * p + k], rows[2 * q + k]
                    rows[2 * p + k], rows[2 * q + k] = c * a - s * b, s * a + c * b
            first, second = move(cosine * first - sine * second, sine * first + cosine * second)
            app, aqq = move(app - tangent * apq, aqq + tangent * apq)
            players = [players[0], players[-1]] + players[1:-1]
        return (*rows, first, second)

    carry = lax.fori_loop(0, SWEEPS, sweep, (*rows, first, second))
    rows, first, second = carry[:-2], carry[-2], carry[-1]
    lam = [norms(rows, heads), norms(rows, tails)]
    index = [row, count - 1 - row]
    above = [jnp.zeros((ROWS, LANES), jnp.int32)] * 2
    ahead = [jnp.zeros((ROWS, LANES), jnp.int32)] * 2
    for p in range(count):
        other = whole(lam[0], p) if p < slots else whole(lam[1], count - 1 - p)
        for i in range(2):
            larger = other > lam[i]
            above[i] = above[i] + jnp.where(larger, 1, 0)
            ahead[i] = ahead[i] + jnp.where(larger | ((other == lam[i]) & (p < index[i])), 1, 0)
    keep = [jnp.where(a < RANK, 1.0, 0.0) for a in above]
    ordered = jnp.where(ahead[0] == lane, lam[0], 0.0) + jnp.where(ahead[1] == lane, lam[1], 0.0)
    ordered = jnp.sum(ordered, axis=0, keepdims=True)
    sigmas_ref[...] = jnp.sqrt(ordered)[:, :count]

    weight = [keep[i] / lam[i] for i in range(2)]
    weighted = [first * weight[0], second * weight[1]]
    tail = [jnp.zeros((ROWS, LANES), jnp.float32)] * 2
    for p in range(count):
        line = whole(weighted[0], p) if p < slots else whole(weighted[1], count - 1 - p)
        tail = [tail[k] + rows[2 * p + k] * line for k in range(2)]

    def dot(a, b, dims):
        return lax.dot_general(a, b, dims, precision=HIGH, preferred_element_type=jnp.float32)

    def tall(tiles, offset):
        blank = jnp.zeros((ROWS, LANES), jnp.float32)
        stack = [blank] * (offset // ROWS) + tiles
        return jnp.concatenate(stack + [blank] * (LANES // ROWS - len(stack)), axis=0)

    head = dot(
        jnp.concatenate([first, second], axis=0),
        jnp.concatenate([first * keep[0], second * keep[1]], axis=0),
        FIRST,
    )[:count]
    cross = [
        jnp.where(lane < count, pltpu.roll(total, LANES - (2 + i) * count, 1), 0.0) for i in range(2)
    ]
    plain = (((1,), (0,)), ((), ()))
    middle = dot(head, tall(cross, count), plain)
    reduced_ref[...] = dot(middle, tall(tail, 0), plain)[:, :count]


def spectral(sums, count, ncell):
    return pl.pallas_call(
        functools.partial(spectral_kernel, ncell),
        out_shape=[
            jax.ShapeDtypeStruct((count, count), jnp.float32),
            jax.ShapeDtypeStruct((1, count), jnp.float32),
        ],
        compiler_params=pltpu.CompilerParams(vmem_limit_bytes=16 << 20),
        name="spectral",
    )(sums)


def shards(snapshots, diffusivity):
    snaps, nx, ny, nz = snapshots.shape
    copies = lax.axis_size(AXES)
    snapshots = pltpu.with_memory_space_constraint(snapshots, pltpu.HBM)
    x_edge, planes, y_low, y_high, z_low, z_high = pack_edges(snapshots)
    y_halo = neighbours(y_low, y_high, "gy")
    z_halo = neighbours(z_low, z_high, "gz")
    if lax.axis_size("gx") == 2:
        x_halo = (lax.ppermute(x_edge, "gx", [(0, 1), (1, 0)]),) * 2
        x_places = (2, 0)
    else:
        x_halo = neighbours(x_edge[:2], x_edge[2:], "gx")
        x_places = (0, 0)
    planes = pltpu.with_memory_space_constraint(planes, pltpu.VMEM)
    partial, _, edge, sums = step_and_sums(planes, diffusivity, x_halo, x_places, z_halo)
    edge = pltpu.with_memory_space_constraint(edge, pltpu.VMEM)
    shifted, sums = finish(partial, edge, sums, y_halo, (y_low, y_high), diffusivity, copies)
    sums = lax.all_to_all(sums, AXES, 0, 0, tiled=True)
    ncell = float(nx * ny * nz * copies)
    reduced, sigmas = spectral(sums, snaps, ncell)
    return shifted, reduced, sigmas.reshape(snaps)


def solution(mesh):
    placed = (P(None, "gx", "gy", "gz"), P("gx", "gy", "gz"))
    return jax.shard_map(
        shards,
        mesh=mesh,
        in_specs=placed,
        out_specs=(P(None, "gx", "gy", "gz"), P(), P()),
        check_vma=False,
    )
```

```python
import functools

import jax
import jax.numpy as jnp
from jax import lax
from jax.experimental import pallas as pl
from jax.experimental.pallas import tpu as pltpu
from jax.sharding import PartitionSpec as P

RANK = 12
SWEEPS = 6
ROWS = 8
LANES = 128
AXES = ("gx", "gy", "gz")
HIGH = lax.Precision.HIGHEST
LAST = (((1,), (1,)), ((), ()))
FIRST = (((0,), (0,)), ((), ()))


OUT_SLOTS = 4
FIX_SLOTS = 8
SMALL = pl.CostEstimate(flops=1024, bytes_accessed=1024, transcendentals=0)


def neighbours(low_edge, high_edge, axis):
    count = lax.axis_size(axis)
    forward = [(i, (i + 1) % count) for i in range(count)]
    backward = [(target, source) for source, target in forward]
    return lax.ppermute(high_edge, axis, forward), lax.ppermute(low_edge, axis, backward)


def iota(dim):
    return lax.broadcasted_iota(jnp.int32, (ROWS, LANES), dim)


def split(first, second):
    both = jnp.concatenate([first, second], axis=0)
    high = both.astype(jnp.bfloat16)
    return high, (both - high.astype(jnp.float32)).astype(jnp.bfloat16)


def rows_copy(x_hbm, planes, sems, i, c, first, count):
    return pltpu.make_async_copy(
        x_hbm.at[:, i, first : first + count, c * LANES : (c + 1) * LANES],
        planes.at[i + 2, c, :, ROWS + first : ROWS + first + count],
        sems,
    )


def rim_rows_kernel(x_hbm, planes, xedge_ref, ylow_ref, yhigh_ref, sems):
    total, cols, snaps, height, _ = planes.shape
    nx, ny = total - 4, height - 2 * ROWS
    row = iota(0)

    def fetch(i, c, side):
        return rows_copy(x_hbm, planes, sems.at[(i * cols + c) * 2 + side], i, c, side * (ny - ROWS), ROWS)

    def fetch_inner(i, c):
        place = ((i if i < 2 else i - nx + 4) + 2 * nx) * cols + c
        return rows_copy(x_hbm, planes, sems.at[place], i, c, ROWS, ny - 2 * ROWS)

    outer = (0, 1, nx - 2, nx - 1)
    for i in outer:
        for c in range(cols):
            fetch_inner(i, c).start()
    for i in range(nx):
        for c in range(cols):
            for side in range(2):
                fetch(i, c, side).start()
    blank = jnp.zeros((snaps, ROWS, LANES), jnp.float32)

    def clear(i, _):
        for c in range(cols):
            planes[i, c, :, :ROWS] = blank
            planes[i, c, :, ROWS + ny :] = blank
        return 0

    lax.fori_loop(0, total, clear, 0)
    for x in range(nx):
        for c in range(cols):
            part = slice(c * LANES, (c + 1) * LANES)
            for side in range(2):
                fetch(x, c, side).wait()
            for group in range(snaps // 4):
                low = jnp.zeros((ROWS, LANES), jnp.float32)
                high = jnp.zeros((ROWS, LANES), jnp.float32)
                for place in range(4):
                    here = (row >> 1) == place
                    first = planes[x + 2, c, 4 * group + place, ROWS : 2 * ROWS]
                    last = planes[x + 2, c, 4 * group + place, ny : ny + ROWS]
                    low = jnp.where(here, pltpu.roll(first, 2 * place, 0), low)
                    high = jnp.where(here, pltpu.roll(last, (2 * place + 2) % ROWS, 0), high)
                ylow_ref[x, group, :, part] = low
                yhigh_ref[x, group, :, part] = high
            if x in outer:
                fetch_inner(x, c).wait()
                xedge_ref[outer.index(x), :, :, part] = planes[x + 2, c, :, ROWS : ROWS + ny]


def rim_rows(x):
    snaps, nx, ny, nz = x.shape
    cols = nz // LANES
    planes = pltpu.VMEM((nx + 4, cols, snaps, ny + 2 * ROWS, LANES), jnp.float32)
    x_edge = jax.ShapeDtypeStruct((4, snaps, ny, nz), jnp.float32)
    y_edge = jax.ShapeDtypeStruct((nx, snaps // 4, ROWS, nz), jnp.float32)
    anywhere, inside = pl.BlockSpec(memory_space=pl.ANY), pl.BlockSpec(memory_space=pltpu.VMEM)
    return pl.pallas_call(
        rim_rows_kernel,
        in_specs=[anywhere],
        out_specs=[inside] * 4,
        out_shape=[planes, x_edge, y_edge, y_edge],
        scratch_shapes=[pltpu.SemaphoreType.DMA(((nx * 2 + 4) * cols,))],
        compiler_params=pltpu.CompilerParams(vmem_limit_bytes=2 << 20),
        cost_estimate=SMALL,
        name="rim_rows",
    )(x)


def edges_kernel(x_hbm, diff_hbm, _, planes, diff, zlow_ref, zhigh_ref, sems):
    total, cols, snaps, height, _ = planes.shape
    nx, ny = total - 4, height - 2 * ROWS
    tiles = ny // ROWS
    lane = iota(1)

    def fetch(i, c):
        return rows_copy(x_hbm, planes, sems.at[i * cols + c], i, c, ROWS, ny - 2 * ROWS)

    for i in range(2, nx - 2):
        for c in range(cols):
            fetch(i, c).start()
    factors = pltpu.make_async_copy(diff_hbm, diff, sems.at[nx * cols])
    factors.start()

    def plane(x):
        for group in range(zlow_ref.shape[1]):
            low = jnp.zeros((ROWS, LANES), jnp.float32)
            high = jnp.zeros((ROWS, LANES), jnp.float32)
            for place in range(min(LANES // 2, snaps * tiles - group * (LANES // 2))):
                snap, tile = divmod(group * (LANES // 2) + place, tiles)
                rows = slice((tile + 1) * ROWS, (tile + 2) * ROWS)
                here = (lane >> 1) == place
                low = jnp.where(here, pltpu.roll(planes[x + 2, 0, snap, rows], 2 * place, 1), low)
                turn = (2 * place + 2) % LANES
                high = jnp.where(here, pltpu.roll(planes[x + 2, cols - 1, snap, rows], turn, 1), high)
            zlow_ref[x, group] = low
            zhigh_ref[x, group] = high

    def inner(i, _):
        for x in (2 + 2 * i, 3 + 2 * i):
            for c in range(cols):
                pltpu.make_async_copy(
                    x_hbm.at[:, 0, ROWS : ny - ROWS, :LANES],
                    planes.at[x + 2, c, :, 2 * ROWS : ny],
                    sems.at[x * cols + c],
                ).wait()
        plane(2 + 2 * i)
        plane(3 + 2 * i)
        return 0

    for x in (0, 1, nx - 2, nx - 1):
        plane(x)
    lax.fori_loop(0, (nx - 4) // 2, inner, 0)
    factors.wait()


def pack_edges(x, diff, planes):
    snaps, nx, ny, nz = x.shape
    cols = nz // LANES
    groups = -(-snaps * (ny // ROWS) * 2 // LANES)
    z_edge = jax.ShapeDtypeStruct((nx, groups, ROWS, LANES), jnp.float32)
    anywhere, inside = pl.BlockSpec(memory_space=pl.ANY), pl.BlockSpec(memory_space=pltpu.VMEM)
    return pl.pallas_call(
        edges_kernel,
        in_specs=[anywhere, anywhere, inside],
        out_specs=[inside] * 4,
        out_shape=[
            pltpu.VMEM(planes.shape, jnp.float32),
            pltpu.VMEM(diff.shape, jnp.float32),
            z_edge,
            z_edge,
        ],
        scratch_shapes=[pltpu.SemaphoreType.DMA((nx * cols + 1,))],
        input_output_aliases={2: 0},
        compiler_params=pltpu.CompilerParams(vmem_limit_bytes=2 << 20),
        cost_estimate=SMALL,
        name="pack_edges",
    )(x, diff, planes)


def base_kernel(planes, diff, base, right):
    nx, snaps, ny, nz = base.shape

    def plane(x, _):
        for t in range(ny // ROWS):
            rows = slice(t * ROWS, (t + 1) * ROWS)
            for c in range(nz // LANES):
                part = slice(c * LANES, (c + 1) * LANES)
                factor = diff[x, rows, part]
                keep, more, less = 1.0 - 6.0 * factor, factor + 1.2 / 12, factor - 1.2 / 12
                for pair in range(snaps // 2):
                    own = []
                    for snap in (2 * pair, 2 * pair + 1):

                        def at(dy):
                            return planes[x + 2, c, snap, (t + 1) * ROWS + dy : (t + 2) * ROWS + dy]

                        far = (0.15 / 12) * (at(2) - at(-2))
                        base[x, snap, rows, part] = (keep * at(0) + far) + (less * at(1) + more * at(-1))
                        own.append(at(0))
                    high, low = split(*own)
                    right[x, t, 0, pair, :, part] = high
                    right[x, t, 1, pair, :, part] = low
        return 0

    lax.fori_loop(0, nx, plane, 0)


def own_terms(planes, diff):
    snaps = planes.shape[2]
    nx, ny, nz = diff.shape
    inside = pl.BlockSpec(memory_space=pltpu.VMEM)
    return pl.pallas_call(
        base_kernel,
        in_specs=[inside] * 2,
        out_specs=[inside] * 2,
        out_shape=[
            pltpu.VMEM((nx, snaps, ny, nz), jnp.float32),
            pltpu.VMEM((nx, ny // ROWS, 2, snaps // 2, 2 * ROWS, nz), jnp.bfloat16),
        ],
        cost_estimate=SMALL,
        compiler_params=pltpu.CompilerParams(vmem_limit_bytes=2 << 20),
        name="own_terms",
    )(planes, diff)


def step_kernel(
    x_places, _, base, right, diff, xlow_hbm, xhigh_hbm, zlow_hbm, zhigh_hbm,
    out_hbm, planes, edge, sums_ref, zlow, zhigh, rims, rim_tiles, out, left, acc, in_sems, out_sems,
):
    nx, _, snaps, _, nz = edge.shape
    ny = diff.shape[1]
    tiles, cols = ny // ROWS, nz // LANES
    half = snaps * ROWS
    row, lane = iota(0), iota(1)

    def fetch(i, c):
        source = xlow_hbm.at[x_places[0] + i] if i < 2 else xhigh_hbm.at[x_places[1] + i - 2]
        return pltpu.make_async_copy(
            source.at[:, :, c * LANES : (c + 1) * LANES],
            planes.at[i if i < 2 else nx + i, c, :, ROWS : ROWS + ny],
            in_sems.at[i * cols + c],
        )

    small = [(zlow_hbm, zlow), (zhigh_hbm, zhigh)]
    small = [pltpu.make_async_copy(a, b, in_sems.at[4 * cols + i]) for i, (a, b) in enumerate(small)]
    for copy in small:
        copy.start()
    for i in range(4):
        for c in range(cols):
            fetch(i, c).start()
    acc[...] = jnp.zeros_like(acc)
    left[1] = jnp.zeros_like(left[1])
    for copy in small:
        copy.wait()

    slots = LANES // 4
    at = lax.broadcasted_iota(jnp.int32, (LANES, LANES), 0)
    to = lax.broadcasted_iota(jnp.int32, (LANES, LANES), 1)
    for group in range(zlow.shape[1]):
        lows = zlow[:, group].reshape(nx * ROWS, LANES)
        highs = zhigh[:, group].reshape(nx * ROWS, LANES)
        for part in range(2):
            origin = 2 * (part * slots + to // 4) + to % 2
            is_low = (to % 4) < 2
            take_low = jnp.where((at == origin) & is_low, 1.0, 0.0)
            take_high = jnp.where((at == origin) & ~is_low, 1.0, 0.0)
            moved = jnp.dot(lows, take_low, precision=HIGH) + jnp.dot(highs, take_high, precision=HIGH)
            rims[:, 2 * group + part] = moved.reshape(nx, ROWS, LANES)

    for i in range(4):
        for c in range(cols):
            fetch(i, c).wait()

    def multiply(x, slot):
        def wide(pieces):
            return jnp.concatenate([pieces[t].reshape(2 * half, nz) for t in range(tiles)], axis=1)

        both, fresh = wide(right.at[x]), wide(left.at[slot])
        acc[:half] += lax.dot_general(both[:half], both, LAST, preferred_element_type=jnp.float32)
        acc[half:] += lax.dot_general(fresh, both, LAST, preferred_element_type=jnp.float32)

    def advance(x, place, snap, t, c):
        rows, part = slice(t * ROWS, (t + 1) * ROWS), slice(c * LANES, (c + 1) * LANES)

        def at(plane, c=c):
            return planes[x + plane, c, snap, (t + 1) * ROWS : (t + 2) * ROWS]

        u = at(2)
        rim = rim_tiles[snap * tiles + t]
        after = rim if c == cols - 1 else at(2, c + 1)
        before = rim if c == 0 else at(2, c - 1)
        zp1 = pltpu.roll(jnp.where(lane == 0, after, u), LANES - 1, 1)
        zp2 = pltpu.roll(jnp.where(lane < 2, after, u), LANES - 2, 1)
        zm1 = pltpu.roll(jnp.where(lane == LANES - 1, before, u), 1, 1)
        zm2 = pltpu.roll(jnp.where(lane >= LANES - 2, before, u), 2, 1)
        xp1, xp2, xm1, xm2 = at(3), at(4), at(1), at(0)
        around = (xp1 + xm1) + (zp1 + zm1)
        zd = 8.0 * (zp1 - zm1) - (zp2 - zm2)
        xd = 8.0 * (xp1 - xm1) - (xp2 - xm2)
        new = (base[x, snap, rows, part] + diff[x, rows, part] * around) - (
            (0.3 / 12 + 0.02 / 12 * u) * zd + (0.2 / 12) * xd
        )
        if t == 0:
            edge[x, 0, snap, :, part] = new
        elif t == tiles - 1:
            edge[x, 1, snap, :, part] = new
        else:
            out[place, snap, (t - 1) * ROWS : t * ROWS, part] = new
        return new

    def sent(x, place):
        return pltpu.make_async_copy(out.at[place], out_hbm.at[:, x, ROWS : ny - ROWS], out_sems.at[place])

    def plane(x, _):
        slot = lax.rem(x, 2)
        place = lax.rem(x, OUT_SLOTS)

        @pl.when(x >= OUT_SLOTS)
        def _():
            sent(x - OUT_SLOTS, place).wait()


        for i in range(snaps * tiles):
            turn = (LANES - 4 * (i % slots) - 2) % LANES
            rim_tiles[i] = pltpu.roll(rims[x, i // slots], turn, 1)

        multiply(jnp.maximum(x - 1, 0), 1 - slot)
        for t in range(tiles):
            for c in range(cols):
                part = slice(c * LANES, (c + 1) * LANES)
                for pair in range(snaps // 2):
                    high, low = split(advance(x, place, 2 * pair, t, c), advance(x, place, 2 * pair + 1, t, c))
                    left[slot, t, 0, pair, :, part] = high
                    left[slot, t, 1, pair, :, part] = low
        sent(x, place).start()

        @pl.when(x == 0)
        def _():
            acc[...] = jnp.zeros_like(acc)

        return 0

    lax.fori_loop(0, nx, plane, 0)
    multiply(nx - 1, (nx - 1) % 2)

    same = (
        lax.broadcasted_iota(jnp.int32, acc.shape, 0) % ROWS
        == lax.broadcasted_iota(jnp.int32, acc.shape, 1) % ROWS
    )
    folded = jnp.where(same, acc[...], 0.0).reshape(3 * snaps, ROWS, 2 * half).sum(axis=1)
    at = lax.broadcasted_iota(jnp.int32, (LANES, 2 * half), 1)
    to = lax.broadcasted_iota(jnp.int32, (LANES, 2 * half), 0)
    member = (at % half) // ROWS == to % snaps
    every = jnp.where(member, 1.0, 0.0)
    upper = jnp.where(member & (at < half), 1.0, 0.0)
    lower = jnp.where(member & (at >= half), 1.0, 0.0)

    def dot(a, b):
        return lax.dot_general(a, b, LAST, precision=HIGH, preferred_element_type=jnp.float32)

    def spread(a):
        return jnp.concatenate([a] * (LANES // snaps), axis=0)

    own, fresh, rest = folded[:snaps], folded[snaps : 2 * snaps], folded[2 * snaps :]
    gram = dot(own, every) + dot(lower[:snaps], spread(own))
    cross = dot(every[:snaps], spread(fresh)) + dot(upper[:snaps], spread(rest))
    sums_ref[...] = beside([gram, cross])
    for x in range(nx - OUT_SLOTS, nx):
        sent(x, x % OUT_SLOTS).wait()


def beside(squares):
    lane = iota(1)
    snaps = squares[0].shape[0]
    blocks = [square[i : i + ROWS] for square in squares for i in range(0, snaps, ROWS)]
    packed = jnp.zeros((ROWS, LANES), jnp.float32)
    for i, block in enumerate(blocks):
        packed = jnp.where(lane // snaps == i, block, packed)
    return packed


def step_and_sums(planes, base, pieces, diff, x_halo, x_places, z_halo):
    total, cols, snaps, height, _ = planes.shape
    nx, ny, nz = diff.shape
    half = snaps * ROWS
    tiles = ny // ROWS
    anywhere, inside = pl.BlockSpec(memory_space=pl.ANY), pl.BlockSpec(memory_space=pltpu.VMEM)
    z_shape = z_halo[0].shape
    return pl.pallas_call(
        functools.partial(step_kernel, x_places),
        in_specs=[inside] * 4 + [anywhere] * 4,
        out_specs=[anywhere] + [inside] * 3,
        out_shape=[
            jax.ShapeDtypeStruct((snaps, nx, ny, nz), jnp.float32),
            pltpu.VMEM(planes.shape, jnp.float32),
            pltpu.VMEM((nx, 2, snaps, ROWS, nz), jnp.float32),
            jax.ShapeDtypeStruct((ROWS, LANES), jnp.float32),
        ],
        scratch_shapes=[
            pltpu.VMEM(z_shape, jnp.float32),
            pltpu.VMEM(z_shape, jnp.float32),
            pltpu.VMEM((nx, 2 * z_shape[1], ROWS, LANES), jnp.float32),
            pltpu.VMEM((snaps * tiles, ROWS, LANES), jnp.float32),
            pltpu.VMEM((OUT_SLOTS, snaps, ny - 2 * ROWS, nz), jnp.float32),
            pltpu.VMEM((2,) + pieces.shape[1:], jnp.bfloat16),
            pltpu.VMEM((3 * half, 2 * half), jnp.float32),
            pltpu.SemaphoreType.DMA((4 * cols + 2,)),
            pltpu.SemaphoreType.DMA((OUT_SLOTS,)),
        ],
        input_output_aliases={0: 1},
        compiler_params=pltpu.CompilerParams(vmem_limit_bytes=5 << 20),
        cost_estimate=SMALL,
        name="step_and_sums",
    )(planes, base, pieces, diff, *x_halo, *z_halo)


def finish_kernel(
    _, edge, sums, low_ref, high_ref, own_low, own_high, diff,
    out_hbm, sums_ref, new, mine, delta, sems,
):
    nx, _, snaps, _, nz = edge.shape
    ny = out_hbm.shape[2]
    row = iota(0)
    groups = snaps // 4
    half = 2 * snaps

    def split(tiles):
        both = jnp.concatenate(tiles, axis=0)
        high = both.astype(jnp.bfloat16)
        return high, (both - high.astype(jnp.float32)).astype(jnp.bfloat16)

    def sent(x, place):
        return [
            pltpu.make_async_copy(new.at[place, 0], out_hbm.at[:, x, :ROWS], sems.at[2 * place]),
            pltpu.make_async_copy(new.at[place, 1], out_hbm.at[:, x, ny - ROWS :], sems.at[2 * place + 1]),
        ]

    def plane(x, _):
        slot = lax.rem(x, FIX_SLOTS)

        @pl.when(x >= FIX_SLOTS)
        def _():
            for copy in sent(x - FIX_SLOTS, slot):
                copy.wait()

        for side in range(2):
            halo, own = ((low_ref, own_low), (high_ref, own_high))[side]
            for c in range(nz // LANES):
                part = slice(c * LANES, (c + 1) * LANES)
                column = pl.ds(pl.multiple_of((2 * x + side) * nz + c * LANES, LANES), LANES)
                if side == 0:
                    factor = jnp.broadcast_to(diff[x, :1, part], (ROWS, LANES)) + 0.1
                else:
                    factor = jnp.broadcast_to(diff[x, ny - 1 :, part], (ROWS, LANES)) - 0.1
                factor = jnp.where(row % 2 == side, factor, 0.0)
                fixes, owns = [], []
                for group in range(groups):
                    value = halo[x, group, :, part]
                    if side == 0:
                        fix = factor * pltpu.roll(value, ROWS - 1, 0) - 0.0125 * value
                    else:
                        fix = factor * pltpu.roll(value, 1, 0) + 0.0125 * value
                    fixes.append(fix)
                    owns.append(own[x, group, :, part])
                    for place in range(4):
                        snap = 4 * group + place
                        if side == 0:
                            term = jnp.where(row < 2, pltpu.roll(fix, (ROWS - 2 * place) % ROWS, 0), 0.0)
                        else:
                            term = jnp.where(row >= ROWS - 2, pltpu.roll(fix, (ROWS - 2 - 2 * place) % ROWS, 0), 0.0)
                        new[slot, side, snap, :, part] = edge[x, side, snap, :, part] + term
                high, low = split(fixes)
                delta[:half, column] = high
                delta[half:, column] = low
                high, low = split(owns)
                mine[:half, column] = high
                mine[half:, column] = low
        for copy in sent(x, slot):
            copy.start()
        return 0

    lax.fori_loop(0, nx, plane, 0)
    product = lax.dot_general(mine[...], delta[...], LAST, preferred_element_type=jnp.float32)
    same = (
        lax.broadcasted_iota(jnp.int32, product.shape, 0) % 2
        == lax.broadcasted_iota(jnp.int32, product.shape, 1) % 2
    )
    at = lax.broadcasted_iota(jnp.int32, (LANES, 2 * half), 1)
    to = lax.broadcasted_iota(jnp.int32, (LANES, 2 * half), 0)
    member = jnp.where((at % half) // 2 == to % snaps, 1.0, 0.0)
    masked = jnp.where(same, product, 0.0)
    extra = jnp.dot(member[:snaps], masked, precision=HIGH)
    extra = lax.dot_general(extra, member, LAST, precision=HIGH, preferred_element_type=jnp.float32)
    total = sums[...] + beside([jnp.zeros_like(extra), extra])
    sums_ref[...] = jnp.broadcast_to(total[None], sums_ref.shape)
    for x in range(nx - FIX_SLOTS, nx):
        for copy in sent(x, x % FIX_SLOTS):
            copy.wait()


def finish(partial, edge, sums, y_halo, own, diff, copies):
    nx, _, snaps, _, nz = edge.shape
    anywhere, inside = pl.BlockSpec(memory_space=pl.ANY), pl.BlockSpec(memory_space=pltpu.VMEM)
    pieces = pltpu.VMEM((4 * snaps, nx * 2 * nz), jnp.bfloat16)
    return pl.pallas_call(
        finish_kernel,
        in_specs=[anywhere] + [inside] * 7,
        out_specs=[anywhere, inside],
        out_shape=[
            jax.ShapeDtypeStruct(partial.shape, jnp.float32),
            jax.ShapeDtypeStruct((copies, ROWS, LANES), jnp.float32),
        ],
        scratch_shapes=[
            pltpu.VMEM((FIX_SLOTS,) + edge.shape[1:], jnp.float32),
            pieces,
            pieces,
            pltpu.SemaphoreType.DMA((2 * FIX_SLOTS,)),
        ],
        input_output_aliases={0: 0},
        compiler_params=pltpu.CompilerParams(vmem_limit_bytes=5 << 20),
        cost_estimate=SMALL,
        name="finish",
    )(partial, edge, sums, *y_halo, *own, diff)


def spectral_kernel(ncell, sums_ref, reduced_ref, sigmas_ref):
    count = sigmas_ref.shape[1]
    slots = count // 2
    row, lane = iota(0), iota(1)
    total = sums_ref[0]
    for i in range(1, sums_ref.shape[0]):
        total = total + sums_ref[i]
    total = total * (1.0 / ncell)

    def whole(tile, at):
        return jnp.broadcast_to(tile[at : at + 1], (ROWS, LANES))

    def shift(x, turn):
        return pltpu.roll(x, turn % ROWS, 0)

    gram = [
        [jnp.broadcast_to(total[:, part * count + j : part * count + j + 1], (ROWS, LANES)) for part in range(2)]
        for j in range(count)
    ]
    rows = []
    inverse = [jnp.where(lane == row + count + part * ROWS, 1.0, 0.0) for part in range(2)]
    for j in range(count):
        part, at = divmod(j, ROWS)
        scale = 1.0 / jnp.sqrt(whole(gram[j][part], at))
        column = [jnp.where(row + i * ROWS >= j, gram[j][i] * scale, 0.0) for i in range(2)]
        for m in range(j + 1, count):
            factor = whole(column[m // ROWS], m % ROWS)
            gram[m] = [gram[m][i] - column[i] * factor for i in range(2)]
        line = whole(inverse[part], at) * scale
        for i in range(2):
            index = row + i * ROWS
            inverse[i] = jnp.where(
                index == j, line, inverse[i] - jnp.where(index > j, column[i], 0.0) * line
            )
        rows += column

    back = jnp.zeros((ROWS, LANES), jnp.float32)
    for i in range(slots):
        back = jnp.where(row == i, whole(inverse[1], ROWS - 1 - i), back)
    first = jnp.where(lane < count, jnp.where(lane == row, 1.0, 0.0), inverse[0])
    second = jnp.where(lane < count, jnp.where(lane == count - 1 - row, 1.0, 0.0), back)

    def join(a, b, turn):
        mask = (row & turn) == 0
        return jnp.where(mask, a, b) + jnp.where(mask, shift(a, -turn), shift(b, turn))

    def gather(parts):
        level = [join(parts[i], parts[i + 4], 4) for i in range(4)]
        level = [join(level[i], level[i + 2], 2) for i in range(2)]
        return join(level[0], level[1], 1)

    def norms(rows, players):
        return gather([rows[2 * p] * rows[2 * p] + rows[2 * p + 1] * rows[2 * p + 1] for p in players])

    heads, tails = list(range(slots)), list(range(count - 1, slots - 1, -1))

    def move(top, low):
        return (
            jnp.where(row == 0, top, shift(jnp.where(row == 0, low, top), 1)),
            jnp.where(row == ROWS - 1, top, shift(low, -1)),
        )

    def sweep(_, carry):
        rows, first, second = list(carry[:-2]), carry[-2], carry[-1]
        players = list(range(count))
        app, aqq = norms(rows, heads), norms(rows, tails)
        for turn in range(count - 1):
            pairs = [(players[i], players[count - 1 - i]) for i in range(slots)]
            apq = gather(
                [rows[2 * p] * rows[2 * q] + rows[2 * p + 1] * rows[2 * q + 1] for p, q in pairs]
            )
            tau = aqq - app
            twice = 2.0 * apq
            denom = jnp.abs(tau) + jnp.sqrt(tau * tau + twice * twice)
            signed = jnp.where(tau >= 0, twice, -twice)
            tangent = jnp.where(denom > 0, signed / jnp.where(denom > 0, denom, 1.0), 0.0)
            cosine = lax.rsqrt(1.0 + tangent * tangent)
            sine = tangent * cosine
            for i, (p, q) in enumerate(pairs):
                c, s = whole(cosine, i), whole(sine, i)
                for k in range(2):
                    a, b = rows[2 * p + k], rows[2 * q + k]
                    rows[2 * p + k], rows[2 * q + k] = c * a - s * b, s * a + c * b
            first, second = move(cosine * first - sine * second, sine * first + cosine * second)
            app, aqq = move(app - tangent * apq, aqq + tangent * apq)
            players = [players[0], players[-1]] + players[1:-1]
        return (*rows, first, second)

    carry = lax.fori_loop(0, SWEEPS, sweep, (*rows, first, second))
    rows, first, second = carry[:-2], carry[-2], carry[-1]
    lam = [norms(rows, heads), norms(rows, tails)]
    index = [row, count - 1 - row]
    above = [jnp.zeros((ROWS, LANES), jnp.int32)] * 2
    ahead = [jnp.zeros((ROWS, LANES), jnp.int32)] * 2
    for p in range(count):
        other = whole(lam[0], p) if p < slots else whole(lam[1], count - 1 - p)
        for i in range(2):
            larger = other > lam[i]
            above[i] = above[i] + jnp.where(larger, 1, 0)
            ahead[i] = ahead[i] + jnp.where(larger | ((other == lam[i]) & (p < index[i])), 1, 0)
    keep = [jnp.where(a < RANK, 1.0, 0.0) for a in above]
    ordered = jnp.where(ahead[0] == lane, lam[0], 0.0) + jnp.where(ahead[1] == lane, lam[1], 0.0)
    ordered = jnp.sum(ordered, axis=0, keepdims=True)
    sigmas_ref[...] = jnp.sqrt(ordered)[:, :count]

    weight = [keep[i] / lam[i] for i in range(2)]
    weighted = [first * weight[0], second * weight[1]]
    tail = [jnp.zeros((ROWS, LANES), jnp.float32)] * 2
    for p in range(count):
        line = whole(weighted[0], p) if p < slots else whole(weighted[1], count - 1 - p)
        tail = [tail[k] + rows[2 * p + k] * line for k in range(2)]

    def dot(a, b, dims):
        return lax.dot_general(a, b, dims, precision=HIGH, preferred_element_type=jnp.float32)

    def tall(tiles, offset):
        blank = jnp.zeros((ROWS, LANES), jnp.float32)
        stack = [blank] * (offset // ROWS) + tiles
        return jnp.concatenate(stack + [blank] * (LANES // ROWS - len(stack)), axis=0)

    head = dot(
        jnp.concatenate([first, second], axis=0),
        jnp.concatenate([first * keep[0], second * keep[1]], axis=0),
        FIRST,
    )[:count]
    cross = [
        jnp.where(lane < count, pltpu.roll(total, LANES - (2 + i) * count, 1), 0.0) for i in range(2)
    ]
    plain = (((1,), (0,)), ((), ()))
    middle = dot(head, tall(cross, count), plain)
    reduced_ref[...] = dot(middle, tall(tail, 0), plain)[:, :count]


def spectral(sums, count, ncell):
    return pl.pallas_call(
        functools.partial(spectral_kernel, ncell),
        out_shape=[
            jax.ShapeDtypeStruct((count, count), jnp.float32),
            jax.ShapeDtypeStruct((1, count), jnp.float32),
        ],
        compiler_params=pltpu.CompilerParams(vmem_limit_bytes=4 << 20),
        cost_estimate=SMALL,
        name="spectral",
    )(sums)


def inside_vmem(array):
    return pltpu.with_memory_space_constraint(array, pltpu.VMEM)


def shards(snapshots, diffusivity):
    snaps, nx, ny, nz = snapshots.shape
    copies = lax.axis_size(AXES)
    snapshots = pltpu.with_memory_space_constraint(snapshots, pltpu.HBM)
    diffusivity = pltpu.with_memory_space_constraint(diffusivity, pltpu.HBM)
    planes, x_edge, y_low, y_high = rim_rows(snapshots)
    y_halo = neighbours(y_low, y_high, "gy")
    planes, factors, z_low, z_high = pack_edges(snapshots, diffusivity, inside_vmem(planes))
    factors = inside_vmem(factors)
    z_halo = neighbours(z_low, z_high, "gz")
    if lax.axis_size("gx") == 2:
        x_halo = (lax.ppermute(x_edge, "gx", [(0, 1), (1, 0)]),) * 2
        x_places = (2, 0)
    else:
        x_halo = neighbours(x_edge[:2], x_edge[2:], "gx")
        x_places = (0, 0)
    planes = inside_vmem(planes)
    base, pieces = own_terms(planes, factors)
    kept = [planes, inside_vmem(base), inside_vmem(pieces), factors]
    partial, _, edge, sums = step_and_sums(*kept, x_halo, x_places, z_halo)
    edge = inside_vmem(edge)
    shifted, sums = finish(partial, edge, sums, y_halo, (y_low, y_high), factors, copies)
    sums = lax.all_to_all(sums, AXES, 0, 0, tiled=True)
    ncell = float(nx * ny * nz * copies)
    reduced, sigmas = spectral(sums, snaps, ncell)
    return shifted, reduced, sigmas.reshape(snaps)


def solution(mesh):
    placed = (P(None, "gx", "gy", "gz"), P("gx", "gy", "gz"))
    return jax.shard_map(
        shards,
        mesh=mesh,
        in_specs=placed,
        out_specs=(P(None, "gx", "gy", "gz"), P(), P()),
        check_vma=False,
    )
```

```python
import functools

import jax
import jax.numpy as jnp
from jax import lax
from jax.experimental import pallas as pl
from jax.experimental.pallas import tpu as pltpu
from jax.sharding import PartitionSpec as P

RANK = 12
SWEEPS = 6
ROWS = 8
LANES = 128
AXES = ("gx", "gy", "gz")
HIGH = lax.Precision.HIGHEST
LAST = (((1,), (1,)), ((), ()))
FIRST = (((0,), (0,)), ((), ()))


OUT_SLOTS = 4
SMALL = pl.CostEstimate(flops=1024, bytes_accessed=1024, transcendentals=0)


def neighbours(low_edge, high_edge, axis):
    count = lax.axis_size(axis)
    forward = [(i, (i + 1) % count) for i in range(count)]
    backward = [(target, source) for source, target in forward]
    return lax.ppermute(high_edge, axis, forward), lax.ppermute(low_edge, axis, backward)


def iota(dim):
    return lax.broadcasted_iota(jnp.int32, (ROWS, LANES), dim)


def split(first, second):
    both = jnp.concatenate([first, second], axis=0)
    high = both.astype(jnp.bfloat16)
    return high, (both - high.astype(jnp.float32)).astype(jnp.bfloat16)


def rows_copy(x_hbm, planes, sems, i, c, first, count):
    return pltpu.make_async_copy(
        x_hbm.at[:, i, first : first + count, c * LANES : (c + 1) * LANES],
        planes.at[i + 2, c, :, ROWS + first : ROWS + first + count],
        sems,
    )


def rim_rows_kernel(x_hbm, planes, xedge_ref, ylow_ref, yhigh_ref, sems):
    total, cols, snaps, height, _ = planes.shape
    nx, ny = total - 4, height - 2 * ROWS
    row = iota(0)

    def fetch(i, c, side):
        return rows_copy(x_hbm, planes, sems.at[(i * cols + c) * 2 + side], i, c, side * (ny - ROWS), ROWS)

    def fetch_inner(i, c):
        place = ((i if i < 2 else i - nx + 4) + 2 * nx) * cols + c
        return rows_copy(x_hbm, planes, sems.at[place], i, c, ROWS, ny - 2 * ROWS)

    outer = (0, 1, nx - 2, nx - 1)
    for i in outer:
        for c in range(cols):
            fetch_inner(i, c).start()
    for i in range(nx):
        for c in range(cols):
            for side in range(2):
                fetch(i, c, side).start()
    blank = jnp.zeros((snaps, ROWS, LANES), jnp.float32)

    def clear(i, _):
        for c in range(cols):
            planes[i, c, :, :ROWS] = blank
            planes[i, c, :, ROWS + ny :] = blank
        return 0

    lax.fori_loop(0, total, clear, 0)
    for x in range(nx):
        for c in range(cols):
            part = slice(c * LANES, (c + 1) * LANES)
            for side in range(2):
                fetch(x, c, side).wait()
            for group in range(snaps // 4):
                low = jnp.zeros((ROWS, LANES), jnp.float32)
                high = jnp.zeros((ROWS, LANES), jnp.float32)
                for place in range(4):
                    here = (row >> 1) == place
                    first = planes[x + 2, c, 4 * group + place, ROWS : 2 * ROWS]
                    last = planes[x + 2, c, 4 * group + place, ny : ny + ROWS]
                    low = jnp.where(here, pltpu.roll(first, 2 * place, 0), low)
                    high = jnp.where(here, pltpu.roll(last, (2 * place + 2) % ROWS, 0), high)
                ylow_ref[x, group, :, part] = low
                yhigh_ref[x, group, :, part] = high
            if x in outer:
                fetch_inner(x, c).wait()
                xedge_ref[outer.index(x), :, :, part] = planes[x + 2, c, :, ROWS : ROWS + ny]


def rim_rows(x):
    snaps, nx, ny, nz = x.shape
    cols = nz // LANES
    planes = pltpu.VMEM((nx + 4, cols, snaps, ny + 2 * ROWS, LANES), jnp.float32)
    x_edge = jax.ShapeDtypeStruct((4, snaps, ny, nz), jnp.float32)
    y_edge = jax.ShapeDtypeStruct((nx, snaps // 4, ROWS, nz), jnp.float32)
    anywhere, inside = pl.BlockSpec(memory_space=pl.ANY), pl.BlockSpec(memory_space=pltpu.VMEM)
    return pl.pallas_call(
        rim_rows_kernel,
        in_specs=[anywhere],
        out_specs=[inside] * 4,
        out_shape=[planes, x_edge, y_edge, y_edge],
        scratch_shapes=[pltpu.SemaphoreType.DMA(((nx * 2 + 4) * cols,))],
        compiler_params=pltpu.CompilerParams(vmem_limit_bytes=5 << 20),
        cost_estimate=SMALL,
        name="rim_rows",
    )(x)


def edges_kernel(x_hbm, diff_hbm, _, planes, diff, zlow_ref, zhigh_ref, sems):
    total, cols, snaps, height, _ = planes.shape
    nx, ny = total - 4, height - 2 * ROWS
    tiles = ny // ROWS
    lane = iota(1)

    def fetch(i, c):
        return rows_copy(x_hbm, planes, sems.at[i * cols + c], i, c, ROWS, ny - 2 * ROWS)

    for i in range(2, nx - 2):
        for c in range(cols):
            fetch(i, c).start()
    factors = pltpu.make_async_copy(diff_hbm, diff, sems.at[nx * cols])
    factors.start()

    def plane(x):
        for group in range(zlow_ref.shape[1]):
            low = jnp.zeros((ROWS, LANES), jnp.float32)
            high = jnp.zeros((ROWS, LANES), jnp.float32)
            for place in range(min(LANES // 2, snaps * tiles - group * (LANES // 2))):
                snap, tile = divmod(group * (LANES // 2) + place, tiles)
                rows = slice((tile + 1) * ROWS, (tile + 2) * ROWS)
                here = (lane >> 1) == place
                low = jnp.where(here, pltpu.roll(planes[x + 2, 0, snap, rows], 2 * place, 1), low)
                turn = (2 * place + 2) % LANES
                high = jnp.where(here, pltpu.roll(planes[x + 2, cols - 1, snap, rows], turn, 1), high)
            zlow_ref[x, group] = low
            zhigh_ref[x, group] = high

    def inner(i, _):
        for x in (2 + 2 * i, 3 + 2 * i):
            for c in range(cols):
                pltpu.make_async_copy(
                    x_hbm.at[:, 0, ROWS : ny - ROWS, :LANES],
                    planes.at[x + 2, c, :, 2 * ROWS : ny],
                    sems.at[x * cols + c],
                ).wait()
        plane(2 + 2 * i)
        plane(3 + 2 * i)
        return 0

    for x in (0, 1, nx - 2, nx - 1):
        plane(x)
    lax.fori_loop(0, (nx - 4) // 2, inner, 0)
    factors.wait()


def pack_edges(x, diff, planes):
    snaps, nx, ny, nz = x.shape
    cols = nz // LANES
    groups = -(-snaps * (ny // ROWS) * 2 // LANES)
    z_edge = jax.ShapeDtypeStruct((nx, groups, ROWS, LANES), jnp.float32)
    anywhere, inside = pl.BlockSpec(memory_space=pl.ANY), pl.BlockSpec(memory_space=pltpu.VMEM)
    return pl.pallas_call(
        edges_kernel,
        in_specs=[anywhere, anywhere, inside],
        out_specs=[inside] * 4,
        out_shape=[
            pltpu.VMEM(planes.shape, jnp.float32),
            pltpu.VMEM(diff.shape, jnp.float32),
            z_edge,
            z_edge,
        ],
        scratch_shapes=[pltpu.SemaphoreType.DMA((nx * cols + 1,))],
        input_output_aliases={2: 0},
        compiler_params=pltpu.CompilerParams(vmem_limit_bytes=5 << 20),
        cost_estimate=SMALL,
        name="pack_edges",
    )(x, diff, planes)


def base_kernel(x_places, _, xlow_hbm, xhigh_hbm, diff, planes, base, right, sems):
    nx, snaps, ny, nz = base.shape
    cols = nz // LANES

    def fetch(i, c):
        source = xlow_hbm.at[x_places[0] + i] if i < 2 else xhigh_hbm.at[x_places[1] + i - 2]
        return pltpu.make_async_copy(
            source.at[:, :, c * LANES : (c + 1) * LANES],
            planes.at[i if i < 2 else nx + i, c, :, ROWS : ROWS + ny],
            sems.at[i * cols + c],
        )

    copies = [fetch(i, c) for i in range(4) for c in range(cols)]
    for copy in copies:
        copy.start()

    def plane(x, _):
        for t in range(ny // ROWS):
            rows = slice(t * ROWS, (t + 1) * ROWS)
            for c in range(nz // LANES):
                part = slice(c * LANES, (c + 1) * LANES)
                factor = diff[x, rows, part]
                keep, more, less = 1.0 - 6.0 * factor, factor + 1.2 / 12, factor - 1.2 / 12
                for pair in range(snaps // 2):
                    own = []
                    for snap in (2 * pair, 2 * pair + 1):

                        def at(dy):
                            return planes[x + 2, c, snap, (t + 1) * ROWS + dy : (t + 2) * ROWS + dy]

                        far = (0.15 / 12) * (at(2) - at(-2))
                        base[x, snap, rows, part] = (keep * at(0) + far) + (less * at(1) + more * at(-1))
                        own.append(at(0))
                    high, low = split(*own)
                    right[x, t, 0, pair, :, part] = high
                    right[x, t, 1, pair, :, part] = low
        return 0

    lax.fori_loop(0, nx, plane, 0)
    for copy in copies:
        copy.wait()


def own_terms(planes, x_halo, x_places, diff):
    snaps = planes.shape[2]
    nx, ny, nz = diff.shape
    anywhere, inside = pl.BlockSpec(memory_space=pl.ANY), pl.BlockSpec(memory_space=pltpu.VMEM)
    return pl.pallas_call(
        functools.partial(base_kernel, x_places),
        in_specs=[inside, anywhere, anywhere, inside],
        out_specs=[inside] * 3,
        out_shape=[
            pltpu.VMEM(planes.shape, jnp.float32),
            pltpu.VMEM((nx, snaps, ny, nz), jnp.float32),
            pltpu.VMEM((nx, ny // ROWS, 2, snaps // 2, 2 * ROWS, nz), jnp.bfloat16),
        ],
        scratch_shapes=[pltpu.SemaphoreType.DMA((4 * (nz // LANES),))],
        input_output_aliases={0: 0},
        cost_estimate=SMALL,
        compiler_params=pltpu.CompilerParams(vmem_limit_bytes=5 << 20),
        name="own_terms",
    )(planes, *x_halo, diff)


def step_kernel(
    planes, base, right, diff, zlow_hbm, zhigh_hbm,
    out_hbm, edge, sums_ref, zlow, zhigh, rims, rim_tiles, out, left, acc, in_sems, out_sems,
):
    nx, _, snaps, _, nz = edge.shape
    ny = diff.shape[1]
    tiles, cols = ny // ROWS, nz // LANES
    half = snaps * ROWS
    row, lane = iota(0), iota(1)

    small = [(zlow_hbm, zlow), (zhigh_hbm, zhigh)]
    small = [pltpu.make_async_copy(a, b, in_sems.at[i]) for i, (a, b) in enumerate(small)]
    for copy in small:
        copy.start()
    acc[...] = jnp.zeros_like(acc)
    left[1] = jnp.zeros_like(left[1])
    for copy in small:
        copy.wait()

    slots = LANES // 4
    at = lax.broadcasted_iota(jnp.int32, (LANES, LANES), 0)
    to = lax.broadcasted_iota(jnp.int32, (LANES, LANES), 1)
    for group in range(zlow.shape[1]):
        lows = zlow[:, group].reshape(nx * ROWS, LANES)
        highs = zhigh[:, group].reshape(nx * ROWS, LANES)
        for part in range(2):
            origin = 2 * (part * slots + to // 4) + to % 2
            is_low = (to % 4) < 2
            take_low = jnp.where((at == origin) & is_low, 1.0, 0.0)
            take_high = jnp.where((at == origin) & ~is_low, 1.0, 0.0)
            moved = jnp.dot(lows, take_low, precision=HIGH) + jnp.dot(highs, take_high, precision=HIGH)
            rims[:, 2 * group + part] = moved.reshape(nx, ROWS, LANES)


    def multiply(x, slot):
        def wide(pieces):
            return jnp.concatenate([pieces[t].reshape(2 * half, nz) for t in range(tiles)], axis=1)

        both, fresh = wide(right.at[x]), wide(left.at[slot])
        acc[:half] += lax.dot_general(both[:half], both, LAST, preferred_element_type=jnp.float32)
        acc[half:] += lax.dot_general(fresh, both, LAST, preferred_element_type=jnp.float32)

    def advance(x, place, snap, t, c):
        rows, part = slice(t * ROWS, (t + 1) * ROWS), slice(c * LANES, (c + 1) * LANES)

        def at(plane, c=c):
            return planes[x + plane, c, snap, (t + 1) * ROWS : (t + 2) * ROWS]

        u = at(2)
        rim = rim_tiles[snap * tiles + t]
        after = rim if c == cols - 1 else at(2, c + 1)
        before = rim if c == 0 else at(2, c - 1)
        zp1 = pltpu.roll(jnp.where(lane == 0, after, u), LANES - 1, 1)
        zp2 = pltpu.roll(jnp.where(lane < 2, after, u), LANES - 2, 1)
        zm1 = pltpu.roll(jnp.where(lane == LANES - 1, before, u), 1, 1)
        zm2 = pltpu.roll(jnp.where(lane >= LANES - 2, before, u), 2, 1)
        xp1, xp2, xm1, xm2 = at(3), at(4), at(1), at(0)
        around = (xp1 + xm1) + (zp1 + zm1)
        zd = 8.0 * (zp1 - zm1) - (zp2 - zm2)
        xd = 8.0 * (xp1 - xm1) - (xp2 - xm2)
        new = (base[x, snap, rows, part] + diff[x, rows, part] * around) - (
            (0.3 / 12 + 0.02 / 12 * u) * zd + (0.2 / 12) * xd
        )
        if t == 0:
            edge[x, 0, snap, :, part] = new
        elif t == tiles - 1:
            edge[x, 1, snap, :, part] = new
        else:
            out[place, snap, (t - 1) * ROWS : t * ROWS, part] = new
        return new

    def sent(x, place):
        return pltpu.make_async_copy(out.at[place], out_hbm.at[:, x, ROWS : ny - ROWS], out_sems.at[place])

    def plane(x, _):
        slot = lax.rem(x, 2)
        place = lax.rem(x, OUT_SLOTS)

        @pl.when(x >= OUT_SLOTS)
        def _():
            sent(x - OUT_SLOTS, place).wait()


        for i in range(snaps * tiles):
            turn = (LANES - 4 * (i % slots) - 2) % LANES
            rim_tiles[i] = pltpu.roll(rims[x, i // slots], turn, 1)

        multiply(jnp.maximum(x - 1, 0), 1 - slot)
        for t in range(tiles):
            for c in range(cols):
                part = slice(c * LANES, (c + 1) * LANES)
                for pair in range(snaps // 2):
                    high, low = split(advance(x, place, 2 * pair, t, c), advance(x, place, 2 * pair + 1, t, c))
                    left[slot, t, 0, pair, :, part] = high
                    left[slot, t, 1, pair, :, part] = low
        sent(x, place).start()

        @pl.when(x == 0)
        def _():
            acc[...] = jnp.zeros_like(acc)

        return 0

    lax.fori_loop(0, nx, plane, 0)
    multiply(nx - 1, (nx - 1) % 2)

    same = (
        lax.broadcasted_iota(jnp.int32, acc.shape, 0) % ROWS
        == lax.broadcasted_iota(jnp.int32, acc.shape, 1) % ROWS
    )
    folded = jnp.where(same, acc[...], 0.0).reshape(3 * snaps, ROWS, 2 * half).sum(axis=1)
    at = lax.broadcasted_iota(jnp.int32, (LANES, 2 * half), 1)
    to = lax.broadcasted_iota(jnp.int32, (LANES, 2 * half), 0)
    member = (at % half) // ROWS == to % snaps
    every = jnp.where(member, 1.0, 0.0)
    upper = jnp.where(member & (at < half), 1.0, 0.0)
    lower = jnp.where(member & (at >= half), 1.0, 0.0)

    def dot(a, b):
        return lax.dot_general(a, b, LAST, precision=HIGH, preferred_element_type=jnp.float32)

    def spread(a):
        return jnp.concatenate([a] * (LANES // snaps), axis=0)

    own, fresh, rest = folded[:snaps], folded[snaps : 2 * snaps], folded[2 * snaps :]
    gram = dot(own, every) + dot(lower[:snaps], spread(own))
    cross = dot(every[:snaps], spread(fresh)) + dot(upper[:snaps], spread(rest))
    sums_ref[...] = beside([gram, cross])
    for x in range(nx - OUT_SLOTS, nx):
        sent(x, x % OUT_SLOTS).wait()


def beside(squares):
    lane = iota(1)
    snaps = squares[0].shape[0]
    blocks = [square[i : i + ROWS] for square in squares for i in range(0, snaps, ROWS)]
    packed = jnp.zeros((ROWS, LANES), jnp.float32)
    for i, block in enumerate(blocks):
        packed = jnp.where(lane // snaps == i, block, packed)
    return packed


def step_and_sums(planes, base, pieces, diff, z_halo):
    total, cols, snaps, height, _ = planes.shape
    nx, ny, nz = diff.shape
    half = snaps * ROWS
    tiles = ny // ROWS
    anywhere, inside = pl.BlockSpec(memory_space=pl.ANY), pl.BlockSpec(memory_space=pltpu.VMEM)
    z_shape = z_halo[0].shape
    return pl.pallas_call(
        step_kernel,
        in_specs=[inside] * 4 + [anywhere] * 2,
        out_specs=[anywhere] + [inside] * 2,
        out_shape=[
            jax.ShapeDtypeStruct((snaps, nx, ny, nz), jnp.float32),
            pltpu.VMEM((nx, 2, snaps, ROWS, nz), jnp.float32),
            jax.ShapeDtypeStruct((ROWS, LANES), jnp.float32),
        ],
        scratch_shapes=[
            pltpu.VMEM(z_shape, jnp.float32),
            pltpu.VMEM(z_shape, jnp.float32),
            pltpu.VMEM((nx, 2 * z_shape[1], ROWS, LANES), jnp.float32),
            pltpu.VMEM((snaps * tiles, ROWS, LANES), jnp.float32),
            pltpu.VMEM((OUT_SLOTS, snaps, ny - 2 * ROWS, nz), jnp.float32),
            pltpu.VMEM((2,) + pieces.shape[1:], jnp.bfloat16),
            pltpu.VMEM((3 * half, 2 * half), jnp.float32),
            pltpu.SemaphoreType.DMA((2,)),
            pltpu.SemaphoreType.DMA((OUT_SLOTS,)),
        ],
        compiler_params=pltpu.CompilerParams(vmem_limit_bytes=5 << 20),
        cost_estimate=SMALL,
        name="step_and_sums",
    )(planes, base, pieces, diff, *z_halo)


def halo_terms(side, halo, x, group, part, diff):
    row = iota(0)
    ny = diff.shape[1]
    value = halo[x, group, :, part]
    edge = slice(0, 1) if side == 0 else slice(ny - 1, ny)
    sign = 1.0 - 2.0 * side
    factor = jnp.broadcast_to(diff[x, edge, part], (ROWS, LANES)) + sign * 1.2 / 12
    near = jnp.where(row % 2 == side, factor, 0.0) * pltpu.roll(value, 1 if side else ROWS - 1, 0)
    return near - sign * (0.15 / 12) * value


def extra_kernel(sums, low_ref, high_ref, own_low, own_high, diff, sums_ref, mine, delta):
    nx, groups, _, nz = low_ref.shape
    snaps = 4 * groups
    half = 2 * snaps

    def pieces(tiles):
        both = jnp.concatenate(tiles, axis=0)
        high = both.astype(jnp.bfloat16)
        return high, (both - high.astype(jnp.float32)).astype(jnp.bfloat16)

    def plane(x, _):
        for side in range(2):
            halo, own = ((low_ref, own_low), (high_ref, own_high))[side]
            for c in range(nz // LANES):
                part = slice(c * LANES, (c + 1) * LANES)
                column = pl.ds(pl.multiple_of((2 * x + side) * nz + c * LANES, LANES), LANES)
                high, low = pieces([halo_terms(side, halo, x, group, part, diff) for group in range(groups)])
                delta[:half, column] = high
                delta[half:, column] = low
                high, low = pieces([own[x, group, :, part] for group in range(groups)])
                mine[:half, column] = high
                mine[half:, column] = low
        return 0

    lax.fori_loop(0, nx, plane, 0, unroll=2)
    product = lax.dot_general(mine[...], delta[...], LAST, preferred_element_type=jnp.float32)
    same = (
        lax.broadcasted_iota(jnp.int32, product.shape, 0) % 2
        == lax.broadcasted_iota(jnp.int32, product.shape, 1) % 2
    )
    at = lax.broadcasted_iota(jnp.int32, (LANES, 2 * half), 1)
    to = lax.broadcasted_iota(jnp.int32, (LANES, 2 * half), 0)
    member = jnp.where((at % half) // 2 == to % snaps, 1.0, 0.0)
    masked = jnp.where(same, product, 0.0)
    extra = jnp.dot(member[:snaps], masked, precision=HIGH)
    extra = lax.dot_general(extra, member, LAST, precision=HIGH, preferred_element_type=jnp.float32)
    total = sums[...] + beside([jnp.zeros_like(extra), extra])
    folded = pltpu.roll(pltpu.roll(total, LANES // 2, 1), ROWS // 2, 0)
    total = jnp.where(iota(1) < LANES // 2, total, folded)
    sums_ref[...] = jnp.broadcast_to(total[None, : ROWS // 2], sums_ref.shape)


def extra_sums(sums, y_halo, own, diff, copies):
    nx, groups, _, nz = y_halo[0].shape
    inside = pl.BlockSpec(memory_space=pltpu.VMEM)
    pieces = pltpu.VMEM((16 * groups, nx * 2 * nz), jnp.bfloat16)
    return pl.pallas_call(
        extra_kernel,
        in_specs=[inside] * 6,
        out_specs=inside,
        out_shape=jax.ShapeDtypeStruct((copies, ROWS // 2, LANES), jnp.float32),
        scratch_shapes=[pieces, pieces],
        compiler_params=pltpu.CompilerParams(vmem_limit_bytes=5 << 20),
        cost_estimate=SMALL,
        name="extra_sums",
    )(sums, *y_halo, *own, diff)


def spectral_kernel(
    ncell, sums_ref, _, edge, low_ref, high_ref, diff, reduced_ref, sigmas_ref, out_hbm, new, sems
):
    count = sigmas_ref.shape[1]
    slots = count // 2
    row, lane = iota(0), iota(1)
    nx, ny, nz = diff.shape
    share = -(-nx // SWEEPS)

    def fixed(x):
        return [
            pltpu.make_async_copy(new.at[x, 0], out_hbm.at[:, x, :ROWS], sems.at[2 * x]),
            pltpu.make_async_copy(new.at[x, 1], out_hbm.at[:, x, ny - ROWS :], sems.at[2 * x + 1]),
        ]

    def fix(x):
        for side in range(2):
            halo = (low_ref, high_ref)[side]
            for c in range(nz // LANES):
                part = slice(c * LANES, (c + 1) * LANES)
                for group in range(count // 4):
                    terms = halo_terms(side, halo, x, group, part, diff)
                    for place in range(4):
                        snap = 4 * group + place
                        turn = (6 * side + ROWS - 2 * place) % ROWS
                        mask = row >= ROWS - 2 if side else row < 2
                        term = jnp.where(mask, pltpu.roll(terms, turn, 0), 0.0)
                        new[x, side, snap, :, part] = edge[x, side, snap, :, part] + term

    total = sums_ref[0]
    for i in range(1, sums_ref.shape[0]):
        total = total + sums_ref[i]
    total = total * (1.0 / ncell)
    total = jnp.concatenate([total, total], axis=0)
    total = jnp.where(row < ROWS // 2, total, pltpu.roll(total, LANES // 2, 1))

    def whole(tile, at):
        return jnp.broadcast_to(tile[at : at + 1], (ROWS, LANES))

    def shift(x, turn):
        return pltpu.roll(x, turn % ROWS, 0)

    gram = [
        [jnp.broadcast_to(total[:, part * count + j : part * count + j + 1], (ROWS, LANES)) for part in range(2)]
        for j in range(count)
    ]
    diagonal = [whole(gram[j][j // ROWS], j % ROWS) for j in range(count)]
    while len(diagonal) > 1:
        diagonal = [a + b for a, b in zip(diagonal[::2], diagonal[1::2])]
    unit = count / diagonal[0]
    gram = [[unit * part for part in column] for column in gram]
    rows = []
    inverse = [jnp.where(lane == row + count + part * ROWS, 1.0, 0.0) for part in range(2)]
    for j in range(count):
        part, at = divmod(j, ROWS)
        scale = 1.0 / jnp.sqrt(whole(gram[j][part], at))
        column = [jnp.where(row + i * ROWS >= j, gram[j][i] * scale, 0.0) for i in range(2)]
        for m in range(j + 1, count):
            factor = whole(column[m // ROWS], m % ROWS)
            gram[m] = [gram[m][i] - column[i] * factor for i in range(2)]
        line = whole(inverse[part], at) * scale
        for i in range(2):
            index = row + i * ROWS
            inverse[i] = jnp.where(
                index == j, line, inverse[i] - jnp.where(index > j, column[i], 0.0) * line
            )
        rows += column

    back = jnp.zeros((ROWS, LANES), jnp.float32)
    for i in range(slots):
        back = jnp.where(row == i, whole(inverse[1], ROWS - 1 - i), back)
    first = jnp.where(lane < count, jnp.where(lane == row, 1.0, 0.0), inverse[0])
    second = jnp.where(lane < count, jnp.where(lane == count - 1 - row, 1.0, 0.0), back)

    def join(a, b, turn):
        mask = (row & turn) == 0
        return jnp.where(mask, a, b) + jnp.where(mask, shift(a, -turn), shift(b, turn))

    def gather(parts):
        level = [join(parts[i], parts[i + 4], 4) for i in range(4)]
        level = [join(level[i], level[i + 2], 2) for i in range(2)]
        return join(level[0], level[1], 1)

    def norms(rows, players):
        return gather([rows[2 * p] * rows[2 * p] + rows[2 * p + 1] * rows[2 * p + 1] for p in players])

    heads, tails = list(range(slots)), list(range(count - 1, slots - 1, -1))

    def move(top, low):
        return (
            jnp.where(row == 0, top, shift(jnp.where(row == 0, low, top), 1)),
            jnp.where(row == ROWS - 1, top, shift(low, -1)),
        )

    def sweep(number, carry):
        for i in range(share):
            fix(jnp.minimum(number * share + i, nx - 1))
        rows, first, second = list(carry[:-2]), carry[-2], carry[-1]
        players = list(range(count))
        app, aqq = norms(rows, heads), norms(rows, tails)
        for turn in range(count - 1):
            pairs = [(players[i], players[count - 1 - i]) for i in range(slots)]
            apq = gather(
                [rows[2 * p] * rows[2 * q] + rows[2 * p + 1] * rows[2 * q + 1] for p, q in pairs]
            )
            tau = aqq - app
            twice = 2.0 * apq
            square = tau * tau + twice * twice
            turned = square > 0
            inverted = lax.rsqrt(square)
            doubled = jnp.where(turned, 0.5 + 0.5 * jnp.abs(tau) * inverted, 1.0)
            scaled = lax.rsqrt(doubled)
            cosine = doubled * scaled
            half_sine = jnp.where(turned, 0.5 * jnp.where(tau >= 0, twice, -twice) * inverted, 0.0)
            sine = half_sine * scaled
            tangent = sine * scaled
            for i, (p, q) in enumerate(pairs):
                c, s = whole(cosine, i), whole(sine, i)
                for k in range(2):
                    a, b = rows[2 * p + k], rows[2 * q + k]
                    rows[2 * p + k], rows[2 * q + k] = c * a - s * b, s * a + c * b
            first, second = move(cosine * first - sine * second, sine * first + cosine * second)
            app, aqq = move(app - tangent * apq, aqq + tangent * apq)
            players = [players[0], players[-1]] + players[1:-1]
        for i in range(share):

            @pl.when(number * share + i < nx)
            def _():
                for copy in fixed(number * share + i):
                    copy.start()

        return (*rows, first, second)

    carry = lax.fori_loop(0, SWEEPS, sweep, (*rows, first, second))
    rows, first, second = carry[:-2], carry[-2], carry[-1]
    lam = [norms(rows, heads), norms(rows, tails)]
    index = [row, count - 1 - row]
    above = [jnp.zeros((ROWS, LANES), jnp.int32)] * 2
    ahead = [jnp.zeros((ROWS, LANES), jnp.int32)] * 2
    for p in range(count):
        other = whole(lam[0], p) if p < slots else whole(lam[1], count - 1 - p)
        for i in range(2):
            larger = other > lam[i]
            above[i] = above[i] + jnp.where(larger, 1, 0)
            ahead[i] = ahead[i] + jnp.where(larger | ((other == lam[i]) & (p < index[i])), 1, 0)
    keep = [jnp.where(a < RANK, 1.0, 0.0) for a in above]
    ordered = jnp.where(ahead[0] == lane, lam[0], 0.0) + jnp.where(ahead[1] == lane, lam[1], 0.0)
    ordered = jnp.sum(ordered, axis=0, keepdims=True)
    sigmas_ref[...] = jnp.sqrt(ordered / unit[:1])[:, :count]

    weight = [keep[i] / lam[i] for i in range(2)]
    weighted = [first * weight[0], second * weight[1]]
    tail = [jnp.zeros((ROWS, LANES), jnp.float32)] * 2
    for p in range(count):
        line = whole(weighted[0], p) if p < slots else whole(weighted[1], count - 1 - p)
        tail = [tail[k] + rows[2 * p + k] * line for k in range(2)]

    def dot(a, b, dims):
        return lax.dot_general(a, b, dims, precision=HIGH, preferred_element_type=jnp.float32)

    def tall(tiles, offset):
        blank = jnp.zeros((ROWS, LANES), jnp.float32)
        stack = [blank] * (offset // ROWS) + tiles
        return jnp.concatenate(stack + [blank] * (LANES // ROWS - len(stack)), axis=0)

    head = dot(
        jnp.concatenate([first, second], axis=0),
        jnp.concatenate([first * keep[0], second * keep[1]], axis=0),
        FIRST,
    )[:count]
    cross = [
        jnp.where(lane < count, pltpu.roll(total, LANES - (2 + i) * count, 1), 0.0) for i in range(2)
    ]
    plain = (((1,), (0,)), ((), ()))
    middle = dot(head * unit[:1, :1], tall(cross, count), plain)
    reduced_ref[...] = dot(middle, tall(tail, 0), plain)[:, :count]
    for x in range(nx):
        for copy in fixed(x):
            copy.wait()


def spectral(sums, partial, edge, y_halo, diff, ncell):
    nx, _, count, _, _ = edge.shape
    anywhere, inside = pl.BlockSpec(memory_space=pl.ANY), pl.BlockSpec(memory_space=pltpu.VMEM)
    return pl.pallas_call(
        functools.partial(spectral_kernel, ncell),
        in_specs=[inside, anywhere] + [inside] * 4,
        out_specs=[inside, inside, anywhere],
        out_shape=[
            jax.ShapeDtypeStruct((count, count), jnp.float32),
            jax.ShapeDtypeStruct((1, count), jnp.float32),
            jax.ShapeDtypeStruct(partial.shape, jnp.float32),
        ],
        scratch_shapes=[pltpu.VMEM(edge.shape, jnp.float32), pltpu.SemaphoreType.DMA((2 * nx,))],
        input_output_aliases={1: 2},
        compiler_params=pltpu.CompilerParams(vmem_limit_bytes=12 << 20),
        cost_estimate=SMALL,
        name="spectral",
    )(sums, partial, edge, *y_halo, diff)


def inside_vmem(array):
    return pltpu.with_memory_space_constraint(array, pltpu.VMEM)


def shards(snapshots, diffusivity):
    snaps, nx, ny, nz = snapshots.shape
    copies = lax.axis_size(AXES)
    snapshots = pltpu.with_memory_space_constraint(snapshots, pltpu.HBM)
    diffusivity = pltpu.with_memory_space_constraint(diffusivity, pltpu.HBM)
    planes, x_edge, y_low, y_high = rim_rows(snapshots)
    y_halo = neighbours(y_low, y_high, "gy")
    planes, factors, z_low, z_high = pack_edges(snapshots, diffusivity, inside_vmem(planes))
    factors = inside_vmem(factors)
    z_halo = neighbours(z_low, z_high, "gz")
    if lax.axis_size("gx") == 2:
        x_halo = (lax.ppermute(x_edge, "gx", [(0, 1), (1, 0)]),) * 2
        x_places = (2, 0)
    else:
        x_halo = neighbours(x_edge[:2], x_edge[2:], "gx")
        x_places = (0, 0)
    planes, base, pieces = own_terms(inside_vmem(planes), x_halo, x_places, factors)
    kept = [inside_vmem(planes), inside_vmem(base), inside_vmem(pieces), factors]
    partial, edge, sums = step_and_sums(*kept, z_halo)
    sums = extra_sums(sums, y_halo, (y_low, y_high), factors, copies)
    sums = lax.all_to_all(sums, AXES, 0, 0, tiled=True)
    ncell = float(nx * ny * nz * copies)
    reduced, sigmas, shifted = spectral(sums, partial, inside_vmem(edge), y_halo, factors, ncell)
    return shifted, reduced, sigmas.reshape(snaps)


def solution(mesh):
    placed = (P(None, "gx", "gy", "gz"), P("gx", "gy", "gz"))
    return jax.shard_map(
        shards,
        mesh=mesh,
        in_specs=placed,
        out_specs=(P(None, "gx", "gy", "gz"), P(), P()),
        check_vma=False,
    )
```

```python
import functools

import jax
import jax.numpy as jnp
from jax import lax
from jax.experimental import pallas as pl
from jax.experimental.pallas import tpu as pltpu
from jax.sharding import PartitionSpec as P

RANK = 12
SWEEPS = 6
ROWS = 8
LANES = 128
AXES = ("gx", "gy", "gz")
HIGH = lax.Precision.HIGHEST
LAST = (((1,), (1,)), ((), ()))
FIRST = (((0,), (0,)), ((), ()))


OUT_SLOTS = 4
SMALL = pl.CostEstimate(flops=1024, bytes_accessed=1024, transcendentals=0)


def ring(axis, by=1):
    count = lax.axis_size(axis)
    return [(i, (i + by) % count) for i in range(count)]


def neighbours(low_edge, high_edge, axis):
    return lax.ppermute(high_edge, axis, ring(axis)), lax.ppermute(low_edge, axis, ring(axis, -1))


def iota(dim):
    return lax.broadcasted_iota(jnp.int32, (ROWS, LANES), dim)


def split(first, second):
    both = jnp.concatenate([first, second], axis=0)
    high = both.astype(jnp.bfloat16)
    return high, (both - high.astype(jnp.float32)).astype(jnp.bfloat16)


def edges_kernel(x_hbm, diff_hbm, planes, diff, xedge_ref, ylow_ref, yhigh_ref, zlow_ref, zhigh_ref, sems):
    total, cols, snaps, height, _ = planes.shape
    nx, ny = total - 4, height - 2 * ROWS
    tiles, groups = ny // ROWS, snaps // 4
    row, lane = iota(0), iota(1)

    def fetch(i, c):
        return pltpu.make_async_copy(
            x_hbm.at[:, i, :, c * LANES : (c + 1) * LANES],
            planes.at[i + 2, c, :, ROWS : ROWS + ny],
            sems.at[i * cols + c],
        )

    for i in range(nx):
        for c in range(cols):
            fetch(i, c).start()
    factors = pltpu.make_async_copy(diff_hbm, diff, sems.at[nx * cols])
    factors.start()
    blank = jnp.zeros((snaps, ROWS, LANES), jnp.float32)

    def clear(i, _):
        for c in range(cols):
            planes[i, c, :, :ROWS] = blank
            planes[i, c, :, ROWS + ny :] = blank
        return 0

    lax.fori_loop(0, total, clear, 0)

    def plane(x):
        for group in range(zlow_ref.shape[1]):
            low = jnp.zeros((ROWS, LANES), jnp.float32)
            high = jnp.zeros((ROWS, LANES), jnp.float32)
            for place in range(min(LANES // 2, snaps * tiles - group * (LANES // 2))):
                snap, tile = divmod(group * (LANES // 2) + place, tiles)
                rows = slice((tile + 1) * ROWS, (tile + 2) * ROWS)
                here = (lane >> 1) == place
                low = jnp.where(here, pltpu.roll(planes[x + 2, 0, snap, rows], 2 * place, 1), low)
                turn = (2 * place + 2) % LANES
                high = jnp.where(here, pltpu.roll(planes[x + 2, cols - 1, snap, rows], turn, 1), high)
            zlow_ref[x, group] = low
            zhigh_ref[x, group] = high
        for c in range(cols):
            part = slice(c * LANES, (c + 1) * LANES)
            for group in range(groups):
                low = jnp.zeros((ROWS, LANES), jnp.float32)
                high = jnp.zeros((ROWS, LANES), jnp.float32)
                for place in range(4):
                    here = (row >> 1) == place
                    first = planes[x + 2, c, 4 * group + place, ROWS : 2 * ROWS]
                    last = planes[x + 2, c, 4 * group + place, ny : ny + ROWS]
                    low = jnp.where(here, pltpu.roll(first, 2 * place, 0), low)
                    high = jnp.where(here, pltpu.roll(last, (2 * place + 2) % ROWS, 0), high)
                ylow_ref[x, group, :, part] = low
                yhigh_ref[x, group, :, part] = high

    def two(i, _):
        for x in (2 * i, 2 * i + 1):
            for c in range(cols):
                pltpu.make_async_copy(
                    x_hbm.at[:, 0, :, :LANES], planes.at[x + 2, c, :, ROWS : ROWS + ny], sems.at[x * cols + c]
                ).wait()
        plane(2 * i)
        plane(2 * i + 1)

        @pl.when((i == 0) | (i == nx // 2 - 1))
        def _():
            place = jnp.where(i == 0, 0, 2)
            for k in range(2):
                for c in range(cols):
                    xedge_ref[place + k, :, :, c * LANES : (c + 1) * LANES] = planes[
                        2 * i + 2 + k, c, :, ROWS : ROWS + ny
                    ]

        return 0

    lax.fori_loop(0, nx // 2, two, 0)
    factors.wait()
    for group in range(groups):
        for c in range(cols):
            part = slice(c * LANES, (c + 1) * LANES)
            last = jnp.zeros((ROWS, LANES), jnp.float32)
            for i in range(min(ROWS, nx - group * ROWS)):
                line = jnp.broadcast_to(diff[group * ROWS + i, ny - 1 :, part], (ROWS, LANES))
                last = jnp.where(row == i, line, last)
            yhigh_ref[nx, group, :, part] = last


def pack_edges(x, diff):
    snaps, nx, ny, nz = x.shape
    cols = nz // LANES
    groups = -(-snaps * (ny // ROWS) * 2 // LANES)
    z_edge = jax.ShapeDtypeStruct((nx, groups, ROWS, LANES), jnp.float32)
    anywhere, inside = pl.BlockSpec(memory_space=pl.ANY), pl.BlockSpec(memory_space=pltpu.VMEM)
    return pl.pallas_call(
        edges_kernel,
        in_specs=[anywhere] * 2,
        out_specs=[inside] * 7,
        out_shape=[
            pltpu.VMEM((nx + 4, cols, snaps, ny + 2 * ROWS, LANES), jnp.float32),
            pltpu.VMEM(diff.shape, jnp.float32),
            jax.ShapeDtypeStruct((4, snaps, ny, nz), jnp.float32),
            jax.ShapeDtypeStruct((nx, snaps // 4, ROWS, nz), jnp.float32),
            jax.ShapeDtypeStruct((nx + 1, snaps // 4, ROWS, nz), jnp.float32),
            z_edge,
            z_edge,
        ],
        scratch_shapes=[pltpu.SemaphoreType.DMA((nx * cols + 1,))],
        compiler_params=pltpu.CompilerParams(vmem_limit_bytes=5 << 20),
        cost_estimate=SMALL,
        name="pack_edges",
    )(x, diff)


def base_kernel(x_places, _, xlow_hbm, xhigh_hbm, diff, planes, base, right, sems):
    nx, snaps, ny, nz = base.shape
    cols = nz // LANES

    def fetch(i, c):
        source = xlow_hbm.at[x_places[0] + i] if i < 2 else xhigh_hbm.at[x_places[1] + i - 2]
        return pltpu.make_async_copy(
            source.at[:, :, c * LANES : (c + 1) * LANES],
            planes.at[i if i < 2 else nx + i, c, :, ROWS : ROWS + ny],
            sems.at[i * cols + c],
        )

    copies = [fetch(i, c) for i in range(4) for c in range(cols)]
    for copy in copies:
        copy.start()

    def plane(x, _):
        for t in range(ny // ROWS):
            rows = slice(t * ROWS, (t + 1) * ROWS)
            for c in range(nz // LANES):
                part = slice(c * LANES, (c + 1) * LANES)
                factor = diff[x, rows, part]
                keep, more, less = 1.0 - 6.0 * factor, factor + 1.2 / 12, factor - 1.2 / 12
                for pair in range(snaps // 2):
                    own = []
                    for snap in (2 * pair, 2 * pair + 1):

                        def at(dy):
                            return planes[x + 2, c, snap, (t + 1) * ROWS + dy : (t + 2) * ROWS + dy]

                        far = (0.15 / 12) * (at(2) - at(-2))
                        base[x, snap, rows, part] = (keep * at(0) + far) + (less * at(1) + more * at(-1))
                        own.append(at(0))
                    high, low = split(*own)
                    right[x, t, 0, pair, :, part] = high
                    right[x, t, 1, pair, :, part] = low
        return 0

    lax.fori_loop(0, nx, plane, 0)
    for copy in copies:
        copy.wait()


def own_terms(planes, x_halo, x_places, diff):
    snaps = planes.shape[2]
    nx, ny, nz = diff.shape
    anywhere, inside = pl.BlockSpec(memory_space=pl.ANY), pl.BlockSpec(memory_space=pltpu.VMEM)
    return pl.pallas_call(
        functools.partial(base_kernel, x_places),
        in_specs=[inside, anywhere, anywhere, inside],
        out_specs=[inside] * 3,
        out_shape=[
            pltpu.VMEM(planes.shape, jnp.float32),
            pltpu.VMEM((nx, snaps, ny, nz), jnp.float32),
            pltpu.VMEM((nx, ny // ROWS, 2, snaps // 2, 2 * ROWS, nz), jnp.bfloat16),
        ],
        scratch_shapes=[pltpu.SemaphoreType.DMA((4 * (nz // LANES),))],
        input_output_aliases={0: 0},
        cost_estimate=SMALL,
        compiler_params=pltpu.CompilerParams(vmem_limit_bytes=5 << 20),
        name="own_terms",
    )(planes, *x_halo, diff)


def step_kernel(
    planes, base, right, diff, zlow, zhigh,
    out_hbm, sums_ref, rims, rim_tiles, out, left, acc, out_sems,
):
    nx, ny, nz = diff.shape
    snaps = planes.shape[2]
    tiles, cols = ny // ROWS, nz // LANES
    half = snaps * ROWS
    row, lane = iota(0), iota(1)

    acc[...] = jnp.zeros_like(acc)
    left[1] = jnp.zeros_like(left[1])

    slots = LANES // 4
    at = lax.broadcasted_iota(jnp.int32, (LANES, LANES), 0)
    to = lax.broadcasted_iota(jnp.int32, (LANES, LANES), 1)
    for group in range(zlow.shape[1]):
        lows = zlow[:, group].reshape(nx * ROWS, LANES)
        highs = zhigh[:, group].reshape(nx * ROWS, LANES)
        for part in range(2):
            origin = 2 * (part * slots + to // 4) + to % 2
            is_low = (to % 4) < 2
            take_low = jnp.where((at == origin) & is_low, 1.0, 0.0)
            take_high = jnp.where((at == origin) & ~is_low, 1.0, 0.0)
            moved = jnp.dot(lows, take_low, precision=HIGH) + jnp.dot(highs, take_high, precision=HIGH)
            rims[:, 2 * group + part] = moved.reshape(nx, ROWS, LANES)


    def multiply(x, slot):
        def wide(pieces):
            return jnp.concatenate([pieces[t].reshape(2 * half, nz) for t in range(tiles)], axis=1)

        both, fresh = wide(right.at[x]), wide(left.at[slot])
        acc[:half] += lax.dot_general(both[:half], both, LAST, preferred_element_type=jnp.float32)
        acc[half:] += lax.dot_general(fresh, both, LAST, preferred_element_type=jnp.float32)

    def advance(x, place, snap, t, c):
        rows, part = slice(t * ROWS, (t + 1) * ROWS), slice(c * LANES, (c + 1) * LANES)

        def at(plane, c=c):
            return planes[x + plane, c, snap, (t + 1) * ROWS : (t + 2) * ROWS]

        u = at(2)
        rim = rim_tiles[snap * tiles + t]
        after = rim if c == cols - 1 else at(2, c + 1)
        before = rim if c == 0 else at(2, c - 1)
        zp1 = pltpu.roll(jnp.where(lane == 0, after, u), LANES - 1, 1)
        zp2 = pltpu.roll(jnp.where(lane < 2, after, u), LANES - 2, 1)
        zm1 = pltpu.roll(jnp.where(lane == LANES - 1, before, u), 1, 1)
        zm2 = pltpu.roll(jnp.where(lane >= LANES - 2, before, u), 2, 1)
        xp1, xp2, xm1, xm2 = at(3), at(4), at(1), at(0)
        around = (xp1 + xm1) + (zp1 + zm1)
        zd = 8.0 * (zp1 - zm1) - (zp2 - zm2)
        xd = 8.0 * (xp1 - xm1) - (xp2 - xm2)
        new = (base[x, snap, rows, part] + diff[x, rows, part] * around) - (
            (0.3 / 12 + 0.02 / 12 * u) * zd + (0.2 / 12) * xd
        )
        out[place, snap, rows, part] = new
        return new

    def sent(x, place):
        return pltpu.make_async_copy(out.at[place], out_hbm.at[:, x], out_sems.at[place])

    def plane(x, _):
        slot = lax.rem(x, 2)
        place = lax.rem(x, OUT_SLOTS)

        @pl.when(x >= OUT_SLOTS)
        def _():
            sent(x - OUT_SLOTS, place).wait()


        for i in range(snaps * tiles):
            turn = (LANES - 4 * (i % slots) - 2) % LANES
            rim_tiles[i] = pltpu.roll(rims[x, i // slots], turn, 1)

        multiply(jnp.maximum(x - 1, 0), 1 - slot)
        for t in range(tiles):
            for c in range(cols):
                part = slice(c * LANES, (c + 1) * LANES)
                for pair in range(snaps // 2):
                    high, low = split(advance(x, place, 2 * pair, t, c), advance(x, place, 2 * pair + 1, t, c))
                    left[slot, t, 0, pair, :, part] = high
                    left[slot, t, 1, pair, :, part] = low
        sent(x, place).start()

        @pl.when(x == 0)
        def _():
            acc[...] = jnp.zeros_like(acc)

        return 0

    lax.fori_loop(0, nx, plane, 0)
    multiply(nx - 1, (nx - 1) % 2)

    same = (
        lax.broadcasted_iota(jnp.int32, acc.shape, 0) % ROWS
        == lax.broadcasted_iota(jnp.int32, acc.shape, 1) % ROWS
    )
    folded = jnp.where(same, acc[...], 0.0).reshape(3 * snaps, ROWS, 2 * half).sum(axis=1)
    at = lax.broadcasted_iota(jnp.int32, (LANES, 2 * half), 1)
    to = lax.broadcasted_iota(jnp.int32, (LANES, 2 * half), 0)
    member = (at % half) // ROWS == to % snaps
    every = jnp.where(member, 1.0, 0.0)
    upper = jnp.where(member & (at < half), 1.0, 0.0)
    lower = jnp.where(member & (at >= half), 1.0, 0.0)

    def dot(a, b):
        return lax.dot_general(a, b, LAST, precision=HIGH, preferred_element_type=jnp.float32)

    def spread(a):
        return jnp.concatenate([a] * (LANES // snaps), axis=0)

    own, fresh, rest = folded[:snaps], folded[snaps : 2 * snaps], folded[2 * snaps :]
    gram = dot(own, every) + dot(lower[:snaps], spread(own))
    cross = dot(every[:snaps], spread(fresh)) + dot(upper[:snaps], spread(rest))
    sums_ref[...] = beside([gram, cross])
    for x in range(nx - OUT_SLOTS, nx):
        sent(x, x % OUT_SLOTS).wait()


def beside(squares):
    lane = iota(1)
    snaps = squares[0].shape[0]
    blocks = [square[i : i + ROWS] for square in squares for i in range(0, snaps, ROWS)]
    packed = jnp.zeros((ROWS, LANES), jnp.float32)
    for i, block in enumerate(blocks):
        packed = jnp.where(lane // snaps == i, block, packed)
    return packed


def step_and_sums(planes, base, pieces, diff, z_halo):
    total, cols, snaps, height, _ = planes.shape
    nx, ny, nz = diff.shape
    half = snaps * ROWS
    tiles = ny // ROWS
    anywhere, inside = pl.BlockSpec(memory_space=pl.ANY), pl.BlockSpec(memory_space=pltpu.VMEM)
    z_shape = z_halo[0].shape
    return pl.pallas_call(
        step_kernel,
        in_specs=[inside] * 6,
        out_specs=[anywhere, inside],
        out_shape=[
            jax.ShapeDtypeStruct((snaps, nx, ny, nz), jnp.float32),
            jax.ShapeDtypeStruct((ROWS, LANES), jnp.float32),
        ],
        scratch_shapes=[
            pltpu.VMEM((nx, 2 * z_shape[1], ROWS, LANES), jnp.float32),
            pltpu.VMEM((snaps * tiles, ROWS, LANES), jnp.float32),
            pltpu.VMEM((OUT_SLOTS, snaps, ny, nz), jnp.float32),
            pltpu.VMEM((2,) + pieces.shape[1:], jnp.bfloat16),
            pltpu.VMEM((3 * half, 2 * half), jnp.float32),
            pltpu.SemaphoreType.DMA((OUT_SLOTS,)),
        ],
        compiler_params=pltpu.CompilerParams(vmem_limit_bytes=5 << 20),
        cost_estimate=SMALL,
        name="step_and_sums",
    )(planes, base, pieces, diff, *z_halo)


def halo_terms(side, value, line):
    row = iota(0)
    sign = 1.0 - 2.0 * side
    factor = jnp.broadcast_to(line, (ROWS, LANES)) + sign * 1.2 / 12
    near = jnp.where(row % 2 == side, factor, 0.0) * pltpu.roll(value, 1 if side else ROWS - 1, 0)
    return near - sign * (0.15 / 12) * value


def extra_kernel(sums, lower, own, diff, sums_ref, mine, delta):
    nx, groups, _, nz = own.shape
    snaps = 4 * groups
    half = 2 * snaps

    def pieces(tiles):
        both = jnp.concatenate(tiles, axis=0)
        high = both.astype(jnp.bfloat16)
        return high, (both - high.astype(jnp.float32)).astype(jnp.bfloat16)

    for x in range(nx):
        for c in range(nz // LANES):
            part = slice(c * LANES, (c + 1) * LANES)
            under = [lower[x, group, :, part] for group in range(groups)]
            over = [own[x, group, :, part] for group in range(groups)]
            lines = diff[x, :1, part], lower[nx, x // ROWS, x % ROWS : x % ROWS + 1, part]
            for side in range(2):
                here, there = ((over, under), (under, over))[side]
                column = slice((2 * x + side) * nz + c * LANES, (2 * x + side) * nz + (c + 1) * LANES)
                high, low = pieces([halo_terms(side, value, lines[side]) for value in there])
                delta[:half, column] = high
                delta[half:, column] = low
                high, low = pieces(here)
                mine[:half, column] = high
                mine[half:, column] = low
    product = lax.dot_general(mine[...], delta[...], LAST, preferred_element_type=jnp.float32)
    same = (
        lax.broadcasted_iota(jnp.int32, product.shape, 0) % 2
        == lax.broadcasted_iota(jnp.int32, product.shape, 1) % 2
    )
    at = lax.broadcasted_iota(jnp.int32, (LANES, 2 * half), 1)
    to = lax.broadcasted_iota(jnp.int32, (LANES, 2 * half), 0)
    member = jnp.where((at % half) // 2 == to % snaps, 1.0, 0.0)
    masked = jnp.where(same, product, 0.0)
    extra = jnp.dot(member[:snaps], masked, precision=HIGH)
    extra = lax.dot_general(extra, member, LAST, precision=HIGH, preferred_element_type=jnp.float32)
    total = sums[...] + beside([jnp.zeros_like(extra), extra])
    folded = pltpu.roll(pltpu.roll(total, LANES // 2, 1), ROWS // 2, 0)
    total = jnp.where(iota(1) < LANES // 2, total, folded)
    sums_ref[...] = jnp.broadcast_to(total[None, : ROWS // 2], sums_ref.shape)


def extra_sums(sums, lower, own, diff, copies):
    nx, groups, _, nz = own.shape
    inside = pl.BlockSpec(memory_space=pltpu.VMEM)
    pieces = pltpu.VMEM((16 * groups, nx * 2 * nz), jnp.bfloat16)
    return pl.pallas_call(
        extra_kernel,
        in_specs=[inside] * 4,
        out_specs=inside,
        out_shape=jax.ShapeDtypeStruct((copies, ROWS // 2, LANES), jnp.float32),
        scratch_shapes=[pieces, pieces],
        compiler_params=pltpu.CompilerParams(vmem_limit_bytes=5 << 20),
        cost_estimate=SMALL,
        name="extra_sums",
    )(sums, lower, own, diff)


def fix_kernel(partial, lower, upper, diff, out_hbm, edge, new, in_sems, sems):
    nx, _, snaps, _, nz = edge.shape
    ny = diff.shape[1]
    row = iota(0)

    def fetch(x):
        return [
            pltpu.make_async_copy(partial.at[:, x, :ROWS], edge.at[x, 0], in_sems.at[2 * x]),
            pltpu.make_async_copy(partial.at[:, x, ny - ROWS :], edge.at[x, 1], in_sems.at[2 * x + 1]),
        ]

    for x in range(nx):
        for copy in fetch(x):
            copy.start()

    def sent(x):
        return [
            pltpu.make_async_copy(new.at[x, 0], out_hbm.at[:, x, :ROWS], sems.at[2 * x]),
            pltpu.make_async_copy(new.at[x, 1], out_hbm.at[:, x, ny - ROWS :], sems.at[2 * x + 1]),
        ]

    def fix(x, _):
        for copy in fetch(x):
            copy.wait()
        for side in range(2):
            halo = (lower, upper)[side]
            for c in range(nz // LANES):
                part = slice(c * LANES, (c + 1) * LANES)
                line = diff[x, ny - 1 :, part] if side else diff[x, :1, part]
                for group in range(snaps // 4):
                    terms = halo_terms(side, halo[x, group, :, part], line)
                    for place in range(4):
                        snap = 4 * group + place
                        turn = (6 * side + ROWS - 2 * place) % ROWS
                        mask = row >= ROWS - 2 if side else row < 2
                        term = jnp.where(mask, pltpu.roll(terms, turn, 0), 0.0)
                        new[x, side, snap, :, part] = edge[x, side, snap, :, part] + term
        for copy in sent(x):
            copy.start()
        return 0

    lax.fori_loop(0, nx, fix, 0)
    for x in range(nx):
        for copy in sent(x):
            copy.wait()


def fix_rows(partial, y_halo, diff):
    snaps, nx, _, nz = partial.shape
    edge = pltpu.VMEM((nx, 2, snaps, ROWS, nz), jnp.float32)
    done = pltpu.SemaphoreType.DMA((2 * nx,))
    anywhere, inside = pl.BlockSpec(memory_space=pl.ANY), pl.BlockSpec(memory_space=pltpu.VMEM)
    return pl.pallas_call(
        fix_kernel,
        in_specs=[anywhere] + [inside] * 3,
        out_specs=anywhere,
        out_shape=jax.ShapeDtypeStruct(partial.shape, jnp.float32),
        scratch_shapes=[edge, edge, done, done],
        input_output_aliases={0: 0},
        compiler_params=pltpu.CompilerParams(vmem_limit_bytes=10 << 20),
        cost_estimate=SMALL,
        name="fix_rows",
    )(partial, *y_halo, diff)


def spectral_kernel(
    ncell, sums_ref, reduced_ref, sigmas_ref
):
    count = sigmas_ref.shape[1]
    slots = count // 2
    row, lane = iota(0), iota(1)
    total = sums_ref[0]
    for i in range(1, sums_ref.shape[0]):
        total = total + sums_ref[i]
    total = total * (1.0 / ncell)
    total = jnp.concatenate([total, total], axis=0)
    total = jnp.where(row < ROWS // 2, total, pltpu.roll(total, LANES // 2, 1))

    def whole(tile, at):
        return jnp.broadcast_to(tile[at : at + 1], (ROWS, LANES))

    def shift(x, turn):
        return pltpu.roll(x, turn % ROWS, 0)

    gram = [
        [jnp.broadcast_to(total[:, part * count + j : part * count + j + 1], (ROWS, LANES)) for part in range(2)]
        for j in range(count)
    ]
    diagonal = [whole(gram[j][j // ROWS], j % ROWS) for j in range(count)]
    while len(diagonal) > 1:
        diagonal = [a + b for a, b in zip(diagonal[::2], diagonal[1::2])]
    unit = count / diagonal[0]
    gram = [[unit * part for part in column] for column in gram]
    rows = []
    inverse = [jnp.where(lane == row + count + part * ROWS, 1.0, 0.0) for part in range(2)]
    for j in range(count):
        part, at = divmod(j, ROWS)
        scale = 1.0 / jnp.sqrt(whole(gram[j][part], at))
        column = [jnp.where(row + i * ROWS >= j, gram[j][i] * scale, 0.0) for i in range(2)]
        for m in range(j + 1, count):
            factor = whole(column[m // ROWS], m % ROWS)
            gram[m] = [gram[m][i] - column[i] * factor for i in range(2)]
        line = whole(inverse[part], at) * scale
        for i in range(2):
            index = row + i * ROWS
            inverse[i] = jnp.where(
                index == j, line, inverse[i] - jnp.where(index > j, column[i], 0.0) * line
            )
        rows += column

    back = jnp.zeros((ROWS, LANES), jnp.float32)
    for i in range(slots):
        back = jnp.where(row == i, whole(inverse[1], ROWS - 1 - i), back)
    first = jnp.where(lane < count, jnp.where(lane == row, 1.0, 0.0), inverse[0])
    second = jnp.where(lane < count, jnp.where(lane == count - 1 - row, 1.0, 0.0), back)

    def join(a, b, turn):
        mask = (row & turn) == 0
        return jnp.where(mask, a, b) + jnp.where(mask, shift(a, -turn), shift(b, turn))

    def gather(parts):
        level = [join(parts[i], parts[i + 4], 4) for i in range(4)]
        level = [join(level[i], level[i + 2], 2) for i in range(2)]
        return join(level[0], level[1], 1)

    def norms(rows, players):
        return gather([rows[2 * p] * rows[2 * p] + rows[2 * p + 1] * rows[2 * p + 1] for p in players])

    heads, tails = list(range(slots)), list(range(count - 1, slots - 1, -1))

    def move(top, low):
        return (
            jnp.where(row == 0, top, shift(jnp.where(row == 0, low, top), 1)),
            jnp.where(row == ROWS - 1, top, shift(low, -1)),
        )

    def sweep(_, carry):
        rows, first, second = list(carry[:-2]), carry[-2], carry[-1]
        players = list(range(count))
        app, aqq = norms(rows, heads), norms(rows, tails)
        for turn in range(count - 1):
            pairs = [(players[i], players[count - 1 - i]) for i in range(slots)]
            apq = gather(
                [rows[2 * p] * rows[2 * q] + rows[2 * p + 1] * rows[2 * q + 1] for p, q in pairs]
            )
            tau = aqq - app
            twice = 2.0 * apq
            square = tau * tau + twice * twice
            turned = square > 0
            inverted = lax.rsqrt(square)
            doubled = jnp.where(turned, 0.5 + 0.5 * jnp.abs(tau) * inverted, 1.0)
            scaled = lax.rsqrt(doubled)
            cosine = doubled * scaled
            half_sine = jnp.where(turned, 0.5 * jnp.where(tau >= 0, twice, -twice) * inverted, 0.0)
            sine = half_sine * scaled
            tangent = sine * scaled
            for i, (p, q) in enumerate(pairs):
                c, s = whole(cosine, i), whole(sine, i)
                for k in range(2):
                    a, b = rows[2 * p + k], rows[2 * q + k]
                    rows[2 * p + k], rows[2 * q + k] = c * a - s * b, s * a + c * b
            first, second = move(cosine * first - sine * second, sine * first + cosine * second)
            app, aqq = move(app - tangent * apq, aqq + tangent * apq)
            players = [players[0], players[-1]] + players[1:-1]
        return (*rows, first, second)

    carry = lax.fori_loop(0, SWEEPS, sweep, (*rows, first, second))
    rows, first, second = carry[:-2], carry[-2], carry[-1]
    lam = [norms(rows, heads), norms(rows, tails)]
    index = [row, count - 1 - row]
    above = [jnp.zeros((ROWS, LANES), jnp.int32)] * 2
    ahead = [jnp.zeros((ROWS, LANES), jnp.int32)] * 2
    for p in range(count):
        other = whole(lam[0], p) if p < slots else whole(lam[1], count - 1 - p)
        for i in range(2):
            larger = other > lam[i]
            above[i] = above[i] + jnp.where(larger, 1, 0)
            ahead[i] = ahead[i] + jnp.where(larger | ((other == lam[i]) & (p < index[i])), 1, 0)
    keep = [jnp.where(a < RANK, 1.0, 0.0) for a in above]
    ordered = jnp.where(ahead[0] == lane, lam[0], 0.0) + jnp.where(ahead[1] == lane, lam[1], 0.0)
    ordered = jnp.sum(ordered, axis=0, keepdims=True)
    sigmas_ref[...] = jnp.sqrt(ordered / unit[:1])[:, :count]

    weight = [keep[i] / lam[i] for i in range(2)]
    weighted = [first * weight[0], second * weight[1]]
    tail = [jnp.zeros((ROWS, LANES), jnp.float32)] * 2
    for p in range(count):
        line = whole(weighted[0], p) if p < slots else whole(weighted[1], count - 1 - p)
        tail = [tail[k] + rows[2 * p + k] * line for k in range(2)]

    def dot(a, b, dims):
        return lax.dot_general(a, b, dims, precision=HIGH, preferred_element_type=jnp.float32)

    def tall(tiles, offset):
        blank = jnp.zeros((ROWS, LANES), jnp.float32)
        stack = [blank] * (offset // ROWS) + tiles
        return jnp.concatenate(stack + [blank] * (LANES // ROWS - len(stack)), axis=0)

    head = dot(
        jnp.concatenate([first, second], axis=0),
        jnp.concatenate([first * keep[0], second * keep[1]], axis=0),
        FIRST,
    )[:count]
    cross = [
        jnp.where(lane < count, pltpu.roll(total, LANES - (2 + i) * count, 1), 0.0) for i in range(2)
    ]
    plain = (((1,), (0,)), ((), ()))
    middle = dot(head * unit[:1, :1], tall(cross, count), plain)
    reduced_ref[...] = dot(middle, tall(tail, 0), plain)[:, :count]


def spectral(sums, count, ncell):
    return pl.pallas_call(
        functools.partial(spectral_kernel, ncell),
        out_shape=[
            jax.ShapeDtypeStruct((count, count), jnp.float32),
            jax.ShapeDtypeStruct((1, count), jnp.float32),
        ],
        compiler_params=pltpu.CompilerParams(vmem_limit_bytes=4 << 20),
        cost_estimate=SMALL,
        name="spectral",
    )(sums)


def inside_vmem(array):
    return pltpu.with_memory_space_constraint(array, pltpu.VMEM)


def shards(snapshots, diffusivity):
    snaps, nx, ny, nz = snapshots.shape
    copies = lax.axis_size(AXES)
    snapshots = pltpu.with_memory_space_constraint(snapshots, pltpu.HBM)
    diffusivity = pltpu.with_memory_space_constraint(diffusivity, pltpu.HBM)
    planes, factors, x_edge, y_low, y_high, z_low, z_high = pack_edges(snapshots, diffusivity)
    planes, factors = inside_vmem(planes), inside_vmem(factors)
    y_below, y_above = neighbours(y_low, y_high, "gy")
    z_halo = neighbours(z_low, z_high, "gz")
    if lax.axis_size("gx") == 2:
        x_halo = (lax.ppermute(x_edge, "gx", [(0, 1), (1, 0)]),) * 2
        x_places = (2, 0)
    else:
        x_halo = neighbours(x_edge[:2], x_edge[2:], "gx")
        x_places = (0, 0)
    planes, base, pieces = own_terms(planes, x_halo, x_places, factors)
    kept = [inside_vmem(planes), inside_vmem(base), inside_vmem(pieces), factors]
    partial, sums = step_and_sums(*kept, [inside_vmem(array) for array in z_halo])
    sums = extra_sums(sums, y_below, y_low, factors, copies)
    shifted = fix_rows(partial, (y_below, y_above), factors)
    sums = lax.all_to_all(sums, AXES, 0, 0, tiled=True)
    ncell = float(nx * ny * nz * copies)
    reduced, sigmas = spectral(sums, snaps, ncell)
    return shifted, reduced, sigmas.reshape(snaps)


def solution(mesh):
    placed = (P(None, "gx", "gy", "gz"), P("gx", "gy", "gz"))
    return jax.shard_map(
        shards,
        mesh=mesh,
        in_specs=placed,
        out_specs=(P(None, "gx", "gy", "gz"), P(), P()),
        check_vma=False,
    )
```

```python
import functools

import jax
import jax.numpy as jnp
from jax import lax
from jax.experimental import pallas as pl
from jax.experimental.pallas import tpu as pltpu
from jax.sharding import PartitionSpec as P

RANK = 12
SWEEPS = 6
ROWS = 8
LANES = 128
AXES = ("gx", "gy", "gz")
HIGH = lax.Precision.HIGHEST
LAST = (((1,), (1,)), ((), ()))
FIRST = (((0,), (0,)), ((), ()))


OUT_SLOTS = 4
SMALL = pl.CostEstimate(flops=1024, bytes_accessed=1024, transcendentals=0)


def ring(axis, by=1):
    count = lax.axis_size(axis)
    return [(i, (i + by) % count) for i in range(count)]


def neighbours(low_edge, high_edge, axis):
    return lax.ppermute(high_edge, axis, ring(axis)), lax.ppermute(low_edge, axis, ring(axis, -1))


def iota(dim):
    return lax.broadcasted_iota(jnp.int32, (ROWS, LANES), dim)


def split(first, second):
    both = jnp.concatenate([first, second], axis=0)
    high = both.astype(jnp.bfloat16)
    return high, (both - high.astype(jnp.float32)).astype(jnp.bfloat16)


def edges_kernel(x_hbm, diff_hbm, planes, diff, xedge_ref, ylow_ref, yhigh_ref, zlow_ref, zhigh_ref, sems):
    total, cols, snaps, height, _ = planes.shape
    nx, ny = total - 4, height - 2 * ROWS
    tiles, groups = ny // ROWS, snaps // 4
    row, lane = iota(0), iota(1)

    def fetch(i, c):
        return pltpu.make_async_copy(
            x_hbm.at[:, i, :, c * LANES : (c + 1) * LANES],
            planes.at[i + 2, c, :, ROWS : ROWS + ny],
            sems.at[i * cols + c],
        )

    for i in range(nx):
        for c in range(cols):
            fetch(i, c).start()
    factors = pltpu.make_async_copy(diff_hbm, diff, sems.at[nx * cols])
    factors.start()
    blank = jnp.zeros((snaps, ROWS, LANES), jnp.float32)

    def clear(i, _):
        for c in range(cols):
            planes[i, c, :, :ROWS] = blank
            planes[i, c, :, ROWS + ny :] = blank
        return 0

    lax.fori_loop(0, total, clear, 0)

    def plane(x):
        for group in range(zlow_ref.shape[1]):
            low = jnp.zeros((ROWS, LANES), jnp.float32)
            high = jnp.zeros((ROWS, LANES), jnp.float32)
            for place in range(min(LANES // 2, snaps * tiles - group * (LANES // 2))):
                snap, tile = divmod(group * (LANES // 2) + place, tiles)
                rows = slice((tile + 1) * ROWS, (tile + 2) * ROWS)
                here = (lane >> 1) == place
                low = jnp.where(here, pltpu.roll(planes[x + 2, 0, snap, rows], 2 * place, 1), low)
                turn = (2 * place + 2) % LANES
                high = jnp.where(here, pltpu.roll(planes[x + 2, cols - 1, snap, rows], turn, 1), high)
            zlow_ref[x, group] = low
            zhigh_ref[x, group] = high
        for c in range(cols):
            part = slice(c * LANES, (c + 1) * LANES)
            for group in range(groups):
                low = jnp.zeros((ROWS, LANES), jnp.float32)
                high = jnp.zeros((ROWS, LANES), jnp.float32)
                for place in range(4):
                    here = (row >> 1) == place
                    first = planes[x + 2, c, 4 * group + place, ROWS : 2 * ROWS]
                    last = planes[x + 2, c, 4 * group + place, ny : ny + ROWS]
                    low = jnp.where(here, pltpu.roll(first, 2 * place, 0), low)
                    high = jnp.where(here, pltpu.roll(last, (2 * place + 2) % ROWS, 0), high)
                ylow_ref[x, group, :, part] = low
                yhigh_ref[x, group, :, part] = high

    def two(i, _):
        for x in (2 * i, 2 * i + 1):
            for c in range(cols):
                pltpu.make_async_copy(
                    x_hbm.at[:, 0, :, :LANES], planes.at[x + 2, c, :, ROWS : ROWS + ny], sems.at[x * cols + c]
                ).wait()
        plane(2 * i)
        plane(2 * i + 1)

        @pl.when((i == 0) | (i == nx // 2 - 1))
        def _():
            place = jnp.where(i == 0, 0, 2)
            for k in range(2):
                for c in range(cols):
                    xedge_ref[place + k, :, :, c * LANES : (c + 1) * LANES] = planes[
                        2 * i + 2 + k, c, :, ROWS : ROWS + ny
                    ]

        return 0

    lax.fori_loop(0, nx // 2, two, 0)
    factors.wait()
    for group in range(groups):
        for c in range(cols):
            part = slice(c * LANES, (c + 1) * LANES)
            last = jnp.zeros((ROWS, LANES), jnp.float32)
            for i in range(min(ROWS, nx - group * ROWS)):
                line = jnp.broadcast_to(diff[group * ROWS + i, ny - 1 :, part], (ROWS, LANES))
                last = jnp.where(row == i, line, last)
            yhigh_ref[nx, group, :, part] = last


def pack_edges(x, diff):
    snaps, nx, ny, nz = x.shape
    cols = nz // LANES
    groups = -(-snaps * (ny // ROWS) * 2 // LANES)
    z_edge = jax.ShapeDtypeStruct((nx, groups, ROWS, LANES), jnp.float32)
    anywhere, inside = pl.BlockSpec(memory_space=pl.ANY), pl.BlockSpec(memory_space=pltpu.VMEM)
    return pl.pallas_call(
        edges_kernel,
        in_specs=[anywhere] * 2,
        out_specs=[inside] * 7,
        out_shape=[
            pltpu.VMEM((nx + 4, cols, snaps, ny + 2 * ROWS, LANES), jnp.float32),
            pltpu.VMEM(diff.shape, jnp.float32),
            jax.ShapeDtypeStruct((4, snaps, ny, nz), jnp.float32),
            jax.ShapeDtypeStruct((nx, snaps // 4, ROWS, nz), jnp.float32),
            jax.ShapeDtypeStruct((nx + 1, snaps // 4, ROWS, nz), jnp.float32),
            z_edge,
            z_edge,
        ],
        scratch_shapes=[pltpu.SemaphoreType.DMA((nx * cols + 1,))],
        compiler_params=pltpu.CompilerParams(vmem_limit_bytes=5 << 20),
        cost_estimate=SMALL,
        name="pack_edges",
    )(x, diff)


def base_kernel(x_places, _, xlow_hbm, xhigh_hbm, diff, planes, base, right, sems):
    nx, snaps, ny, nz = base.shape
    cols = nz // LANES

    def fetch(i, c):
        source = xlow_hbm.at[x_places[0] + i] if i < 2 else xhigh_hbm.at[x_places[1] + i - 2]
        return pltpu.make_async_copy(
            source.at[:, :, c * LANES : (c + 1) * LANES],
            planes.at[i if i < 2 else nx + i, c, :, ROWS : ROWS + ny],
            sems.at[i * cols + c],
        )

    copies = [fetch(i, c) for i in range(4) for c in range(cols)]
    for copy in copies:
        copy.start()

    def plane(x, _):
        for t in range(ny // ROWS):
            rows = slice(t * ROWS, (t + 1) * ROWS)
            for c in range(nz // LANES):
                part = slice(c * LANES, (c + 1) * LANES)
                factor = diff[x, rows, part]
                keep, more, less = 1.0 - 6.0 * factor, factor + 1.2 / 12, factor - 1.2 / 12
                for pair in range(snaps // 2):
                    own = []
                    for snap in (2 * pair, 2 * pair + 1):

                        def at(dy):
                            return planes[x + 2, c, snap, (t + 1) * ROWS + dy : (t + 2) * ROWS + dy]

                        far = (0.15 / 12) * (at(2) - at(-2))
                        base[x, snap, rows, part] = (keep * at(0) + far) + (less * at(1) + more * at(-1))
                        own.append(at(0))
                    high, low = split(*own)
                    right[x, t, 0, pair, :, part] = high
                    right[x, t, 1, pair, :, part] = low
        return 0

    lax.fori_loop(0, nx, plane, 0)
    for copy in copies:
        copy.wait()


def own_terms(planes, x_halo, x_places, diff):
    snaps = planes.shape[2]
    nx, ny, nz = diff.shape
    anywhere, inside = pl.BlockSpec(memory_space=pl.ANY), pl.BlockSpec(memory_space=pltpu.VMEM)
    return pl.pallas_call(
        functools.partial(base_kernel, x_places),
        in_specs=[inside, anywhere, anywhere, inside],
        out_specs=[inside] * 3,
        out_shape=[
            pltpu.VMEM(planes.shape, jnp.float32),
            pltpu.VMEM((nx, snaps, ny, nz), jnp.float32),
            pltpu.VMEM((nx, ny // ROWS, 2, snaps // 2, 2 * ROWS, nz), jnp.bfloat16),
        ],
        scratch_shapes=[pltpu.SemaphoreType.DMA((4 * (nz // LANES),))],
        input_output_aliases={0: 0},
        cost_estimate=SMALL,
        compiler_params=pltpu.CompilerParams(vmem_limit_bytes=5 << 20),
        name="own_terms",
    )(planes, *x_halo, diff)


def step_kernel(
    planes, base, right, diff, zlow, zhigh,
    out_hbm, sums_ref, rims, rim_tiles, out, left_even, left_odd, acc, out_sems,
):
    nx, ny, nz = diff.shape
    snaps = planes.shape[2]
    tiles, cols = ny // ROWS, nz // LANES
    half = snaps * ROWS
    row, lane = iota(0), iota(1)

    acc[...] = jnp.zeros_like(acc)
    left_odd[...] = jnp.zeros_like(left_odd)

    slots = LANES // 4
    at = lax.broadcasted_iota(jnp.int32, (2 * LANES, 2 * LANES), 0)
    to = lax.broadcasted_iota(jnp.int32, (2 * LANES, 2 * LANES), 1)
    origin = 2 * (to // 4) + to % 2 + jnp.where(to % 4 < 2, 0, LANES)
    take = jnp.where(at == origin, 1.0, 0.0)
    for group in range(zlow.shape[1]):
        both = jnp.concatenate([zlow[:, group], zhigh[:, group]], axis=-1).reshape(nx * ROWS, 2 * LANES)
        moved = jnp.dot(both, take, precision=HIGH)
        for part in range(2):
            rims[:, 2 * group + part] = moved[:, part * LANES : (part + 1) * LANES].reshape(nx, ROWS, LANES)

    def multiply(x, left):
        def wide(pieces):
            return jnp.concatenate([pieces[t].reshape(2 * half, nz) for t in range(tiles)], axis=1)

        both, fresh = wide(right.at[x]), wide(left)
        acc[:half] += lax.dot_general(both[:half], both, LAST, preferred_element_type=jnp.float32)
        acc[half:] += lax.dot_general(fresh, both, LAST, preferred_element_type=jnp.float32)

    def advance(x, odd, place, snap, t, c):
        rows, part = slice(t * ROWS, (t + 1) * ROWS), slice(c * LANES, (c + 1) * LANES)

        def at(plane, c=c):
            return planes[x + plane, c, snap, (t + 1) * ROWS : (t + 2) * ROWS]

        u = at(2)
        rim = rim_tiles[odd, snap * tiles + t]
        after = rim if c == cols - 1 else at(2, c + 1)
        before = rim if c == 0 else at(2, c - 1)
        zp1 = pltpu.roll(jnp.where(lane == 0, after, u), LANES - 1, 1)
        zp2 = pltpu.roll(jnp.where(lane < 2, after, u), LANES - 2, 1)
        zm1 = pltpu.roll(jnp.where(lane == LANES - 1, before, u), 1, 1)
        zm2 = pltpu.roll(jnp.where(lane >= LANES - 2, before, u), 2, 1)
        xp1, xp2, xm1, xm2 = at(3), at(4), at(1), at(0)
        around = (xp1 + xm1) + (zp1 + zm1)
        zd = 8.0 * (zp1 - zm1) - (zp2 - zm2)
        xd = 8.0 * (xp1 - xm1) - (xp2 - xm2)
        new = (base[x, snap, rows, part] + diff[x, rows, part] * around) - (
            (0.3 / 12 + 0.02 / 12 * u) * zd + (0.2 / 12) * xd
        )
        out[place, snap, rows, part] = new
        return new

    def sent(x, place):
        return pltpu.make_async_copy(out.at[place], out_hbm.at[:, x], out_sems.at[place])

    def spread_rims(x, odd):
        for i in range(snaps * tiles):
            turn = (LANES - 4 * (i % slots) - 2) % LANES
            rim_tiles[odd, i] = pltpu.roll(rims[x, i // slots], turn, 1)

    def plane(x, odd, left, other):
        place = lax.rem(x, OUT_SLOTS)
        multiply(jnp.maximum(x - 1, 0), other)
        for t in range(tiles):
            for c in range(cols):
                part = slice(c * LANES, (c + 1) * LANES)
                for pair in range(snaps // 2):
                    high, low = split(advance(x, odd, place, 2 * pair, t, c), advance(x, odd, place, 2 * pair + 1, t, c))
                    left[t, 0, pair, :, part] = high
                    left[t, 1, pair, :, part] = low

    def two(i, _):
        x = 2 * i

        @pl.when(x >= OUT_SLOTS)
        def _():
            for k in range(2):
                sent(x + k - OUT_SLOTS, lax.rem(x + k, OUT_SLOTS)).wait()

        spread_rims(x, 0)
        spread_rims(x + 1, 1)
        plane(x, 0, left_even, left_odd)
        acc[...] = jnp.where(i == 0, 0.0, acc[...])
        plane(x + 1, 1, left_odd, left_even)
        for k in range(2):
            sent(x + k, lax.rem(x + k, OUT_SLOTS)).start()
        return 0

    lax.fori_loop(0, nx // 2, two, 0)
    multiply(nx - 1, left_odd)

    same = (
        lax.broadcasted_iota(jnp.int32, acc.shape, 0) % ROWS
        == lax.broadcasted_iota(jnp.int32, acc.shape, 1) % ROWS
    )
    folded = jnp.where(same, acc[...], 0.0).reshape(3 * snaps, ROWS, 2 * half).sum(axis=1)
    at = lax.broadcasted_iota(jnp.int32, (LANES, 2 * half), 1)
    to = lax.broadcasted_iota(jnp.int32, (LANES, 2 * half), 0)
    member = (at % half) // ROWS == to % snaps
    every = jnp.where(member, 1.0, 0.0)
    upper = jnp.where(member & (at < half), 1.0, 0.0)
    lower = jnp.where(member & (at >= half), 1.0, 0.0)

    def dot(a, b):
        return lax.dot_general(a, b, LAST, precision=HIGH, preferred_element_type=jnp.float32)

    def spread(a):
        return jnp.concatenate([a] * (LANES // snaps), axis=0)

    own, fresh, rest = folded[:snaps], folded[snaps : 2 * snaps], folded[2 * snaps :]
    gram = dot(own, every) + dot(lower[:snaps], spread(own))
    cross = dot(every[:snaps], spread(fresh)) + dot(upper[:snaps], spread(rest))
    sums_ref[...] = beside([gram, cross])
    for x in range(nx - OUT_SLOTS, nx):
        sent(x, x % OUT_SLOTS).wait()


def beside(squares):
    lane = iota(1)
    snaps = squares[0].shape[0]
    blocks = [square[i : i + ROWS] for square in squares for i in range(0, snaps, ROWS)]
    packed = jnp.zeros((ROWS, LANES), jnp.float32)
    for i, block in enumerate(blocks):
        packed = jnp.where(lane // snaps == i, block, packed)
    return packed


def step_and_sums(planes, base, pieces, diff, z_halo):
    total, cols, snaps, height, _ = planes.shape
    nx, ny, nz = diff.shape
    half = snaps * ROWS
    tiles = ny // ROWS
    anywhere, inside = pl.BlockSpec(memory_space=pl.ANY), pl.BlockSpec(memory_space=pltpu.VMEM)
    z_shape = z_halo[0].shape
    return pl.pallas_call(
        step_kernel,
        in_specs=[inside] * 6,
        out_specs=[anywhere, inside],
        out_shape=[
            jax.ShapeDtypeStruct((snaps, nx, ny, nz), jnp.float32),
            jax.ShapeDtypeStruct((ROWS, LANES), jnp.float32),
        ],
        scratch_shapes=[
            pltpu.VMEM((nx, 2 * z_shape[1], ROWS, LANES), jnp.float32),
            pltpu.VMEM((2, snaps * tiles, ROWS, LANES), jnp.float32),
            pltpu.VMEM((OUT_SLOTS, snaps, ny, nz), jnp.float32),
            pltpu.VMEM(pieces.shape[1:], jnp.bfloat16),
            pltpu.VMEM(pieces.shape[1:], jnp.bfloat16),
            pltpu.VMEM((3 * half, 2 * half), jnp.float32),
            pltpu.SemaphoreType.DMA((OUT_SLOTS,)),
        ],
        compiler_params=pltpu.CompilerParams(vmem_limit_bytes=5 << 20),
        cost_estimate=SMALL,
        name="step_and_sums",
    )(planes, base, pieces, diff, *z_halo)


def halo_terms(side, value, line):
    row = iota(0)
    sign = 1.0 - 2.0 * side
    factor = jnp.broadcast_to(line, (ROWS, LANES)) + sign * 1.2 / 12
    near = jnp.where(row % 2 == side, factor, 0.0) * pltpu.roll(value, 1 if side else ROWS - 1, 0)
    return near - sign * (0.15 / 12) * value


def extra_kernel(sums, lower, own, diff, sums_ref, mine, delta):
    nx, groups, _, nz = own.shape
    snaps = 4 * groups
    half = 2 * snaps

    def pieces(tiles):
        both = jnp.concatenate(tiles, axis=0)
        high = both.astype(jnp.bfloat16)
        return high, (both - high.astype(jnp.float32)).astype(jnp.bfloat16)

    for x in range(nx):
        for c in range(nz // LANES):
            part = slice(c * LANES, (c + 1) * LANES)
            under = [lower[x, group, :, part] for group in range(groups)]
            over = [own[x, group, :, part] for group in range(groups)]
            lines = diff[x, :1, part], lower[nx, x // ROWS, x % ROWS : x % ROWS + 1, part]
            for side in range(2):
                here, there = ((over, under), (under, over))[side]
                column = slice((2 * x + side) * nz + c * LANES, (2 * x + side) * nz + (c + 1) * LANES)
                high, low = pieces([halo_terms(side, value, lines[side]) for value in there])
                delta[:half, column] = high
                delta[half:, column] = low
                high, low = pieces(here)
                mine[:half, column] = high
                mine[half:, column] = low
    product = lax.dot_general(mine[...], delta[...], LAST, preferred_element_type=jnp.float32)
    same = (
        lax.broadcasted_iota(jnp.int32, product.shape, 0) % 2
        == lax.broadcasted_iota(jnp.int32, product.shape, 1) % 2
    )
    at = lax.broadcasted_iota(jnp.int32, (LANES, 2 * half), 1)
    to = lax.broadcasted_iota(jnp.int32, (LANES, 2 * half), 0)
    member = jnp.where((at % half) // 2 == to % snaps, 1.0, 0.0)
    masked = jnp.where(same, product, 0.0)
    extra = jnp.dot(member[:snaps], masked, precision=HIGH)
    extra = lax.dot_general(extra, member, LAST, precision=HIGH, preferred_element_type=jnp.float32)
    total = sums[...] + beside([jnp.zeros_like(extra), extra])
    folded = pltpu.roll(pltpu.roll(total, LANES // 2, 1), ROWS // 2, 0)
    total = jnp.where(iota(1) < LANES // 2, total, folded)
    sums_ref[...] = jnp.broadcast_to(total[None, : ROWS // 2], sums_ref.shape)


def extra_sums(sums, lower, own, diff, copies):
    nx, groups, _, nz = own.shape
    inside = pl.BlockSpec(memory_space=pltpu.VMEM)
    pieces = pltpu.VMEM((16 * groups, nx * 2 * nz), jnp.bfloat16)
    return pl.pallas_call(
        extra_kernel,
        in_specs=[inside] * 4,
        out_specs=inside,
        out_shape=jax.ShapeDtypeStruct((copies, ROWS // 2, LANES), jnp.float32),
        scratch_shapes=[pieces, pieces],
        compiler_params=pltpu.CompilerParams(vmem_limit_bytes=5 << 20),
        cost_estimate=SMALL,
        name="extra_sums",
    )(sums, lower, own, diff)


def fix_kernel(partial, lower, upper, diff, out_hbm, edge, new, in_sems, sems):
    nx, _, snaps, _, nz = edge.shape
    ny = diff.shape[1]
    row = iota(0)

    def fetch(x):
        return [
            pltpu.make_async_copy(partial.at[:, x, :ROWS], edge.at[x, 0], in_sems.at[2 * x]),
            pltpu.make_async_copy(partial.at[:, x, ny - ROWS :], edge.at[x, 1], in_sems.at[2 * x + 1]),
        ]

    for x in range(nx):
        for copy in fetch(x):
            copy.start()

    def sent(x):
        return [
            pltpu.make_async_copy(new.at[x, 0], out_hbm.at[:, x, :ROWS], sems.at[2 * x]),
            pltpu.make_async_copy(new.at[x, 1], out_hbm.at[:, x, ny - ROWS :], sems.at[2 * x + 1]),
        ]

    def fix(x, _):
        for copy in fetch(x):
            copy.wait()
        for side in range(2):
            halo = (lower, upper)[side]
            for c in range(nz // LANES):
                part = slice(c * LANES, (c + 1) * LANES)
                line = diff[x, ny - 1 :, part] if side else diff[x, :1, part]
                for group in range(snaps // 4):
                    terms = halo_terms(side, halo[x, group, :, part], line)
                    for place in range(4):
                        snap = 4 * group + place
                        turn = (6 * side + ROWS - 2 * place) % ROWS
                        mask = row >= ROWS - 2 if side else row < 2
                        term = jnp.where(mask, pltpu.roll(terms, turn, 0), 0.0)
                        new[x, side, snap, :, part] = edge[x, side, snap, :, part] + term
        for copy in sent(x):
            copy.start()
        return 0

    lax.fori_loop(0, nx, fix, 0)
    for x in range(nx):
        for copy in sent(x):
            copy.wait()


def fix_rows(partial, y_halo, diff):
    snaps, nx, _, nz = partial.shape
    edge = pltpu.VMEM((nx, 2, snaps, ROWS, nz), jnp.float32)
    done = pltpu.SemaphoreType.DMA((2 * nx,))
    anywhere, inside = pl.BlockSpec(memory_space=pl.ANY), pl.BlockSpec(memory_space=pltpu.VMEM)
    return pl.pallas_call(
        fix_kernel,
        in_specs=[anywhere] + [inside] * 3,
        out_specs=anywhere,
        out_shape=jax.ShapeDtypeStruct(partial.shape, jnp.float32),
        scratch_shapes=[edge, edge, done, done],
        input_output_aliases={0: 0},
        compiler_params=pltpu.CompilerParams(vmem_limit_bytes=10 << 20),
        cost_estimate=SMALL,
        name="fix_rows",
    )(partial, *y_halo, diff)


def spectral_kernel(
    ncell, sums_ref, reduced_ref, sigmas_ref
):
    count = sigmas_ref.shape[1]
    slots = count // 2
    row, lane = iota(0), iota(1)
    total = sums_ref[0]
    for i in range(1, sums_ref.shape[0]):
        total = total + sums_ref[i]
    total = total * (1.0 / ncell)
    total = jnp.concatenate([total, total], axis=0)
    total = jnp.where(row < ROWS // 2, total, pltpu.roll(total, LANES // 2, 1))

    def whole(tile, at):
        return jnp.broadcast_to(tile[at : at + 1], (ROWS, LANES))

    def shift(x, turn):
        return pltpu.roll(x, turn % ROWS, 0)

    gram = [
        [jnp.broadcast_to(total[:, part * count + j : part * count + j + 1], (ROWS, LANES)) for part in range(2)]
        for j in range(count)
    ]
    diagonal = [whole(gram[j][j // ROWS], j % ROWS) for j in range(count)]
    while len(diagonal) > 1:
        diagonal = [a + b for a, b in zip(diagonal[::2], diagonal[1::2])]
    unit = count / diagonal[0]
    gram = [[unit * part for part in column] for column in gram]
    rows = []
    inverse = [jnp.where(lane == row + count + part * ROWS, 1.0, 0.0) for part in range(2)]
    for j in range(count):
        part, at = divmod(j, ROWS)
        scale = lax.rsqrt(whole(gram[j][part], at))
        column = [jnp.where(row + i * ROWS >= j, gram[j][i] * scale, 0.0) for i in range(2)]
        for m in range(j + 1, count):
            factor = whole(column[m // ROWS], m % ROWS)
            gram[m] = [gram[m][i] - column[i] * factor for i in range(2)]
        line = whole(inverse[part], at) * scale
        for i in range(2):
            index = row + i * ROWS
            inverse[i] = jnp.where(
                index == j, line, inverse[i] - jnp.where(index > j, column[i], 0.0) * line
            )
        rows += column

    back = jnp.zeros((ROWS, LANES), jnp.float32)
    for i in range(slots):
        back = jnp.where(row == i, whole(inverse[1], ROWS - 1 - i), back)
    first = jnp.where(lane < count, jnp.where(lane == row, 1.0, 0.0), inverse[0])
    second = jnp.where(lane < count, jnp.where(lane == count - 1 - row, 1.0, 0.0), back)

    def join(a, b, turn):
        mask = (row & turn) == 0
        return jnp.where(mask, a, b) + jnp.where(mask, shift(a, -turn), shift(b, turn))

    def gather(parts):
        level = [join(parts[i], parts[i + 4], 4) for i in range(4)]
        level = [join(level[i], level[i + 2], 2) for i in range(2)]
        return join(level[0], level[1], 1)

    def norms(rows, players):
        return gather([rows[2 * p] * rows[2 * p] + rows[2 * p + 1] * rows[2 * p + 1] for p in players])

    heads, tails = list(range(slots)), list(range(count - 1, slots - 1, -1))

    def move(top, low):
        return (
            jnp.where(row == 0, top, shift(jnp.where(row == 0, low, top), 1)),
            jnp.where(row == ROWS - 1, top, shift(low, -1)),
        )

    def sweep(_, carry):
        rows, first, second = list(carry[:-2]), carry[-2], carry[-1]
        players = list(range(count))
        app, aqq = norms(rows, heads), norms(rows, tails)
        for turn in range(count - 1):
            pairs = [(players[i], players[count - 1 - i]) for i in range(slots)]
            apq = gather(
                [rows[2 * p] * rows[2 * q] + rows[2 * p + 1] * rows[2 * q + 1] for p, q in pairs]
            )
            tau = aqq - app
            twice = 2.0 * apq
            square = tau * tau + twice * twice
            turned = square > 0
            inverted = lax.rsqrt(square)
            doubled = jnp.where(turned, 0.5 + 0.5 * jnp.abs(tau) * inverted, 1.0)
            scaled = lax.rsqrt(doubled)
            cosine = doubled * scaled
            half_sine = jnp.where(turned, 0.5 * jnp.where(tau >= 0, twice, -twice) * inverted, 0.0)
            sine = half_sine * scaled
            tangent = sine * scaled
            for i, (p, q) in enumerate(pairs):
                c, s = whole(cosine, i), whole(sine, i)
                for k in range(2):
                    a, b = rows[2 * p + k], rows[2 * q + k]
                    rows[2 * p + k], rows[2 * q + k] = c * a - s * b, s * a + c * b
            first, second = move(cosine * first - sine * second, sine * first + cosine * second)
            app, aqq = move(app - tangent * apq, aqq + tangent * apq)
            players = [players[0], players[-1]] + players[1:-1]
        return (*rows, first, second)

    carry = lax.fori_loop(0, SWEEPS, sweep, (*rows, first, second))
    rows, first, second = carry[:-2], carry[-2], carry[-1]
    lam = [norms(rows, heads), norms(rows, tails)]
    index = [row, count - 1 - row]
    above = [jnp.zeros((ROWS, LANES), jnp.int32)] * 2
    ahead = [jnp.zeros((ROWS, LANES), jnp.int32)] * 2
    for p in range(count):
        other = whole(lam[0], p) if p < slots else whole(lam[1], count - 1 - p)
        for i in range(2):
            larger = other > lam[i]
            above[i] = above[i] + jnp.where(larger, 1, 0)
            ahead[i] = ahead[i] + jnp.where(larger | ((other == lam[i]) & (p < index[i])), 1, 0)
    keep = [jnp.where(a < RANK, 1.0, 0.0) for a in above]
    ordered = jnp.where(ahead[0] == lane, lam[0], 0.0) + jnp.where(ahead[1] == lane, lam[1], 0.0)
    ordered = jnp.sum(ordered, axis=0, keepdims=True)
    sigmas_ref[...] = jnp.sqrt(ordered / unit[:1])[:, :count]

    weight = [keep[i] / lam[i] for i in range(2)]
    weighted = [first * weight[0], second * weight[1]]
    tail = [jnp.zeros((ROWS, LANES), jnp.float32)] * 2
    for p in range(count):
        line = whole(weighted[0], p) if p < slots else whole(weighted[1], count - 1 - p)
        tail = [tail[k] + rows[2 * p + k] * line for k in range(2)]

    def dot(a, b, dims):
        return lax.dot_general(a, b, dims, precision=HIGH, preferred_element_type=jnp.float32)

    def tall(tiles, offset):
        blank = jnp.zeros((ROWS, LANES), jnp.float32)
        stack = [blank] * (offset // ROWS) + tiles
        return jnp.concatenate(stack + [blank] * (LANES // ROWS - len(stack)), axis=0)

    head = dot(
        jnp.concatenate([first, second], axis=0),
        jnp.concatenate([first * keep[0], second * keep[1]], axis=0),
        FIRST,
    )[:count]
    cross = [
        jnp.where(lane < count, pltpu.roll(total, LANES - (2 + i) * count, 1), 0.0) for i in range(2)
    ]
    plain = (((1,), (0,)), ((), ()))
    behind = dot(tall(cross, count), tall(tail, 0), plain)
    reduced_ref[...] = dot(head * unit[:1, :1], behind, plain)[:, :count]


def spectral(sums, count, ncell):
    return pl.pallas_call(
        functools.partial(spectral_kernel, ncell),
        out_shape=[
            jax.ShapeDtypeStruct((count, count), jnp.float32),
            jax.ShapeDtypeStruct((1, count), jnp.float32),
        ],
        compiler_params=pltpu.CompilerParams(vmem_limit_bytes=4 << 20),
        cost_estimate=SMALL,
        name="spectral",
    )(sums)


def inside_vmem(array):
    return pltpu.with_memory_space_constraint(array, pltpu.VMEM)


def shards(snapshots, diffusivity):
    snaps, nx, ny, nz = snapshots.shape
    copies = lax.axis_size(AXES)
    snapshots = pltpu.with_memory_space_constraint(snapshots, pltpu.HBM)
    diffusivity = pltpu.with_memory_space_constraint(diffusivity, pltpu.HBM)
    planes, factors, x_edge, y_low, y_high, z_low, z_high = pack_edges(snapshots, diffusivity)
    planes, factors = inside_vmem(planes), inside_vmem(factors)
    y_below, y_above = neighbours(y_low, y_high, "gy")
    z_halo = neighbours(z_low, z_high, "gz")
    if lax.axis_size("gx") == 2:
        x_halo = (lax.ppermute(x_edge, "gx", [(0, 1), (1, 0)]),) * 2
        x_places = (2, 0)
    else:
        x_halo = neighbours(x_edge[:2], x_edge[2:], "gx")
        x_places = (0, 0)
    planes, base, pieces = own_terms(planes, x_halo, x_places, factors)
    kept = [inside_vmem(planes), inside_vmem(base), inside_vmem(pieces), factors]
    partial, sums = step_and_sums(*kept, [inside_vmem(array) for array in z_halo])
    sums = extra_sums(sums, y_below, y_low, factors, copies)
    shifted = fix_rows(partial, (y_below, y_above), factors)
    sums = lax.all_to_all(sums, AXES, 0, 0, tiled=True)
    ncell = float(nx * ny * nz * copies)
    reduced, sigmas = spectral(sums, snaps, ncell)
    return shifted, reduced, sigmas.reshape(snaps)


def solution(mesh):
    placed = (P(None, "gx", "gy", "gz"), P("gx", "gy", "gz"))
    return jax.shard_map(
        shards,
        mesh=mesh,
        in_specs=placed,
        out_specs=(P(None, "gx", "gy", "gz"), P(), P()),
        check_vma=False,
    )
```

```python
import functools

import jax
import jax.numpy as jnp
from jax import lax
from jax.experimental import pallas as pl
from jax.experimental.pallas import tpu as pltpu
from jax.sharding import PartitionSpec as P

RANK = 12
SWEEPS = 6
ROWS = 8
LANES = 128
AXES = ("gx", "gy", "gz")
HIGH = lax.Precision.HIGHEST
LAST = (((1,), (1,)), ((), ()))
FIRST = (((0,), (0,)), ((), ()))


OUT_SLOTS = 4
SMALL = pl.CostEstimate(flops=1024, bytes_accessed=1024, transcendentals=0)


def ring(axis, by=1):
    count = lax.axis_size(axis)
    return [(i, (i + by) % count) for i in range(count)]


def neighbours(low_edge, high_edge, axis):
    return lax.ppermute(high_edge, axis, ring(axis)), lax.ppermute(low_edge, axis, ring(axis, -1))


def iota(dim):
    return lax.broadcasted_iota(jnp.int32, (ROWS, LANES), dim)


def split(first, second):
    both = jnp.concatenate([first, second], axis=0)
    high = both.astype(jnp.bfloat16)
    return high, (both - high.astype(jnp.float32)).astype(jnp.bfloat16)


def edges_kernel(x_hbm, diff_hbm, planes, diff, xedge_ref, ylow_ref, yhigh_ref, zlow_ref, zhigh_ref, sems):
    total, cols, snaps, height, _ = planes.shape
    nx, ny = total - 4, height - 2 * ROWS
    tiles, groups = ny // ROWS, snaps // 4
    row, lane = iota(0), iota(1)

    def fetch(i, c):
        return pltpu.make_async_copy(
            x_hbm.at[:, i, :, c * LANES : (c + 1) * LANES],
            planes.at[i + 2, c, :, ROWS : ROWS + ny],
            sems.at[i * cols + c],
        )

    for i in range(nx):
        for c in range(cols):
            fetch(i, c).start()
    factors = pltpu.make_async_copy(diff_hbm, diff, sems.at[nx * cols])
    factors.start()
    blank = jnp.zeros((snaps, ROWS, LANES), jnp.float32)

    def clear(i, _):
        for c in range(cols):
            planes[i, c, :, :ROWS] = blank
            planes[i, c, :, ROWS + ny :] = blank
        return 0

    lax.fori_loop(0, total, clear, 0)

    def plane(x):
        for group in range(zlow_ref.shape[1]):
            low = jnp.zeros((ROWS, LANES), jnp.float32)
            high = jnp.zeros((ROWS, LANES), jnp.float32)
            for place in range(min(LANES // 2, snaps * tiles - group * (LANES // 2))):
                snap, tile = divmod(group * (LANES // 2) + place, tiles)
                rows = slice((tile + 1) * ROWS, (tile + 2) * ROWS)
                here = (lane >> 1) == place
                low = jnp.where(here, pltpu.roll(planes[x + 2, 0, snap, rows], 2 * place, 1), low)
                turn = (2 * place + 2) % LANES
                high = jnp.where(here, pltpu.roll(planes[x + 2, cols - 1, snap, rows], turn, 1), high)
            zlow_ref[x, group] = low
            zhigh_ref[x, group] = high
        for c in range(cols):
            part = slice(c * LANES, (c + 1) * LANES)
            for group in range(groups):
                low = jnp.zeros((ROWS, LANES), jnp.float32)
                high = jnp.zeros((ROWS, LANES), jnp.float32)
                for place in range(4):
                    here = (row >> 1) == place
                    first = planes[x + 2, c, 4 * group + place, ROWS : 2 * ROWS]
                    last = planes[x + 2, c, 4 * group + place, ny : ny + ROWS]
                    low = jnp.where(here, pltpu.roll(first, 2 * place, 0), low)
                    high = jnp.where(here, pltpu.roll(last, (2 * place + 2) % ROWS, 0), high)
                ylow_ref[x, group, :, part] = low
                yhigh_ref[x, group, :, part] = high

    def two(i, _):
        for x in (2 * i, 2 * i + 1):
            for c in range(cols):
                pltpu.make_async_copy(
                    x_hbm.at[:, 0, :, :LANES], planes.at[x + 2, c, :, ROWS : ROWS + ny], sems.at[x * cols + c]
                ).wait()
        plane(2 * i)
        plane(2 * i + 1)

        @pl.when((i == 0) | (i == nx // 2 - 1))
        def _():
            place = jnp.where(i == 0, 0, 2)
            for k in range(2):
                for c in range(cols):
                    xedge_ref[place + k, :, :, c * LANES : (c + 1) * LANES] = planes[
                        2 * i + 2 + k, c, :, ROWS : ROWS + ny
                    ]

        return 0

    lax.fori_loop(0, nx // 2, two, 0)
    factors.wait()
    for group in range(groups):
        for c in range(cols):
            part = slice(c * LANES, (c + 1) * LANES)
            last = jnp.zeros((ROWS, LANES), jnp.float32)
            for i in range(min(ROWS, nx - group * ROWS)):
                line = jnp.broadcast_to(diff[group * ROWS + i, ny - 1 :, part], (ROWS, LANES))
                last = jnp.where(row == i, line, last)
            yhigh_ref[nx, group, :, part] = last


def pack_edges(x, diff):
    snaps, nx, ny, nz = x.shape
    cols = nz // LANES
    groups = -(-snaps * (ny // ROWS) * 2 // LANES)
    z_edge = jax.ShapeDtypeStruct((nx, groups, ROWS, LANES), jnp.float32)
    anywhere, inside = pl.BlockSpec(memory_space=pl.ANY), pl.BlockSpec(memory_space=pltpu.VMEM)
    return pl.pallas_call(
        edges_kernel,
        in_specs=[anywhere] * 2,
        out_specs=[inside] * 7,
        out_shape=[
            pltpu.VMEM((nx + 4, cols, snaps, ny + 2 * ROWS, LANES), jnp.float32),
            pltpu.VMEM(diff.shape, jnp.float32),
            jax.ShapeDtypeStruct((4, snaps, ny, nz), jnp.float32),
            jax.ShapeDtypeStruct((nx, snaps // 4, ROWS, nz), jnp.float32),
            jax.ShapeDtypeStruct((nx + 1, snaps // 4, ROWS, nz), jnp.float32),
            z_edge,
            z_edge,
        ],
        scratch_shapes=[pltpu.SemaphoreType.DMA((nx * cols + 1,))],
        compiler_params=pltpu.CompilerParams(vmem_limit_bytes=5 << 20),
        cost_estimate=SMALL,
        name="pack_edges",
    )(x, diff)


def base_kernel(x_places, _, xlow_hbm, xhigh_hbm, diff, planes, base, right, sems):
    nx, snaps, ny, nz = base.shape
    cols = nz // LANES

    def fetch(i, c):
        source = xlow_hbm.at[x_places[0] + i] if i < 2 else xhigh_hbm.at[x_places[1] + i - 2]
        return pltpu.make_async_copy(
            source.at[:, :, c * LANES : (c + 1) * LANES],
            planes.at[i if i < 2 else nx + i, c, :, ROWS : ROWS + ny],
            sems.at[i * cols + c],
        )

    copies = [fetch(i, c) for i in range(4) for c in range(cols)]
    for copy in copies:
        copy.start()

    def plane(x, _):
        for t in range(ny // ROWS):
            rows = slice(t * ROWS, (t + 1) * ROWS)
            for c in range(nz // LANES):
                part = slice(c * LANES, (c + 1) * LANES)
                factor = diff[x, rows, part]
                keep, more, less = 1.0 - 6.0 * factor, factor + 1.2 / 12, factor - 1.2 / 12
                for pair in range(snaps // 2):
                    own = []
                    for snap in (2 * pair, 2 * pair + 1):

                        def at(dy):
                            return planes[x + 2, c, snap, (t + 1) * ROWS + dy : (t + 2) * ROWS + dy]

                        far = (0.15 / 12) * (at(2) - at(-2))
                        base[x, snap, rows, part] = (keep * at(0) + far) + (less * at(1) + more * at(-1))
                        own.append(at(0))
                    high, low = split(*own)
                    right[x, t, 0, pair, :, part] = high
                    right[x, t, 1, pair, :, part] = low
        return 0

    lax.fori_loop(0, nx, plane, 0)
    for copy in copies:
        copy.wait()


def own_terms(planes, x_halo, x_places, diff):
    snaps = planes.shape[2]
    nx, ny, nz = diff.shape
    anywhere, inside = pl.BlockSpec(memory_space=pl.ANY), pl.BlockSpec(memory_space=pltpu.VMEM)
    return pl.pallas_call(
        functools.partial(base_kernel, x_places),
        in_specs=[inside, anywhere, anywhere, inside],
        out_specs=[inside] * 3,
        out_shape=[
            pltpu.VMEM(planes.shape, jnp.float32),
            pltpu.VMEM((nx, snaps, ny, nz), jnp.float32),
            pltpu.VMEM((nx, ny // ROWS, 2, snaps // 2, 2 * ROWS, nz), jnp.bfloat16),
        ],
        scratch_shapes=[pltpu.SemaphoreType.DMA((4 * (nz // LANES),))],
        input_output_aliases={0: 0},
        cost_estimate=SMALL,
        compiler_params=pltpu.CompilerParams(vmem_limit_bytes=5 << 20),
        name="own_terms",
    )(planes, *x_halo, diff)


def step_kernel(
    planes, base, right, diff, zlow, zhigh,
    out_hbm, sums_ref, rims, rim_tiles, out, left_even, left_odd, acc, out_sems,
):
    nx, ny, nz = diff.shape
    snaps = planes.shape[2]
    tiles, cols = ny // ROWS, nz // LANES
    half = snaps * ROWS
    row, lane = iota(0), iota(1)

    acc[...] = jnp.zeros_like(acc)
    left_odd[...] = jnp.zeros_like(left_odd)

    slots = LANES // 4
    at = lax.broadcasted_iota(jnp.int32, (2 * LANES, 2 * LANES), 0)
    to = lax.broadcasted_iota(jnp.int32, (2 * LANES, 2 * LANES), 1)
    origin = 2 * (to // 4) + to % 2 + jnp.where(to % 4 < 2, 0, LANES)
    take = jnp.where(at == origin, 1.0, 0.0)
    for group in range(zlow.shape[1]):
        both = jnp.concatenate([zlow[:, group], zhigh[:, group]], axis=-1).reshape(nx * ROWS, 2 * LANES)
        moved = jnp.dot(both, take, precision=HIGH)
        for part in range(2):
            rims[:, 2 * group + part] = moved[:, part * LANES : (part + 1) * LANES].reshape(nx, ROWS, LANES)

    def multiply(x, left):
        def wide(pieces):
            return jnp.concatenate([pieces[t].reshape(2 * half, nz) for t in range(tiles)], axis=1)

        both, fresh = wide(right.at[x]), wide(left)
        acc[:half] += lax.dot_general(both[:half], both, LAST, preferred_element_type=jnp.float32)
        acc[half:] += lax.dot_general(fresh, both, LAST, preferred_element_type=jnp.float32)

    def advance(x, odd, place, snap, t, c):
        rows, part = slice(t * ROWS, (t + 1) * ROWS), slice(c * LANES, (c + 1) * LANES)

        def at(plane, c=c):
            return planes[x + plane, c, snap, (t + 1) * ROWS : (t + 2) * ROWS]

        u = at(2)
        rim = rim_tiles[odd, snap * tiles + t]
        after = rim if c == cols - 1 else at(2, c + 1)
        before = rim if c == 0 else at(2, c - 1)
        zp1 = pltpu.roll(jnp.where(lane == 0, after, u), LANES - 1, 1)
        zp2 = pltpu.roll(jnp.where(lane < 2, after, u), LANES - 2, 1)
        zm1 = pltpu.roll(jnp.where(lane == LANES - 1, before, u), 1, 1)
        zm2 = pltpu.roll(jnp.where(lane >= LANES - 2, before, u), 2, 1)
        xp1, xp2, xm1, xm2 = at(3), at(4), at(1), at(0)
        around = (xp1 + xm1) + (zp1 + zm1)
        zd = 8.0 * (zp1 - zm1) - (zp2 - zm2)
        xd = 8.0 * (xp1 - xm1) - (xp2 - xm2)
        new = (base[x, snap, rows, part] + diff[x, rows, part] * around) - (
            (0.3 / 12 + 0.02 / 12 * u) * zd + (0.2 / 12) * xd
        )
        out[place, snap, rows, part] = new
        return new

    def sent(x, place):
        return pltpu.make_async_copy(out.at[place], out_hbm.at[:, x], out_sems.at[place])

    def spread_rims(x, odd):
        for i in range(snaps * tiles):
            turn = (LANES - 4 * (i % slots) - 2) % LANES
            rim_tiles[odd, i] = pltpu.roll(rims[x, i // slots], turn, 1)

    def plane(x, odd, left, other):
        place = lax.rem(x, OUT_SLOTS)
        multiply(jnp.maximum(x - 1, 0), other)
        for t in range(tiles):
            for c in range(cols):
                part = slice(c * LANES, (c + 1) * LANES)
                for pair in range(snaps // 2):
                    high, low = split(advance(x, odd, place, 2 * pair, t, c), advance(x, odd, place, 2 * pair + 1, t, c))
                    left[t, 0, pair, :, part] = high
                    left[t, 1, pair, :, part] = low

    def two(i, _):
        x = 2 * i

        @pl.when(x >= OUT_SLOTS)
        def _():
            for k in range(2):
                sent(x + k - OUT_SLOTS, lax.rem(x + k, OUT_SLOTS)).wait()

        spread_rims(x, 0)
        spread_rims(x + 1, 1)
        plane(x, 0, left_even, left_odd)
        acc[...] = jnp.where(i == 0, 0.0, acc[...])
        plane(x + 1, 1, left_odd, left_even)
        for k in range(2):
            sent(x + k, lax.rem(x + k, OUT_SLOTS)).start()
        return 0

    lax.fori_loop(0, nx // 2, two, 0)
    multiply(nx - 1, left_odd)

    same = (
        lax.broadcasted_iota(jnp.int32, acc.shape, 0) % ROWS
        == lax.broadcasted_iota(jnp.int32, acc.shape, 1) % ROWS
    )
    folded = jnp.where(same, acc[...], 0.0).reshape(3 * snaps, ROWS, 2 * half).sum(axis=1)
    at = lax.broadcasted_iota(jnp.int32, (LANES, 2 * half), 1)
    to = lax.broadcasted_iota(jnp.int32, (LANES, 2 * half), 0)
    member = (at % half) // ROWS == to % snaps
    every = jnp.where(member, 1.0, 0.0)
    upper = jnp.where(member & (at < half), 1.0, 0.0)
    lower = jnp.where(member & (at >= half), 1.0, 0.0)

    def dot(a, b):
        return lax.dot_general(a, b, LAST, precision=HIGH, preferred_element_type=jnp.float32)

    def spread(a):
        return jnp.concatenate([a] * (LANES // snaps), axis=0)

    own, fresh, rest = folded[:snaps], folded[snaps : 2 * snaps], folded[2 * snaps :]
    gram = dot(own, every) + dot(lower[:snaps], spread(own))
    cross = dot(every[:snaps], spread(fresh)) + dot(upper[:snaps], spread(rest))
    sums_ref[...] = beside([gram, cross])
    for x in range(nx - OUT_SLOTS, nx):
        sent(x, x % OUT_SLOTS).wait()


def beside(squares):
    lane = iota(1)
    snaps = squares[0].shape[0]
    blocks = [square[i : i + ROWS] for square in squares for i in range(0, snaps, ROWS)]
    packed = jnp.zeros((ROWS, LANES), jnp.float32)
    for i, block in enumerate(blocks):
        packed = jnp.where(lane // snaps == i, block, packed)
    return packed


def step_and_sums(planes, base, pieces, diff, z_halo):
    total, cols, snaps, height, _ = planes.shape
    nx, ny, nz = diff.shape
    half = snaps * ROWS
    tiles = ny // ROWS
    anywhere, inside = pl.BlockSpec(memory_space=pl.ANY), pl.BlockSpec(memory_space=pltpu.VMEM)
    z_shape = z_halo[0].shape
    return pl.pallas_call(
        step_kernel,
        in_specs=[inside] * 6,
        out_specs=[anywhere, inside],
        out_shape=[
            jax.ShapeDtypeStruct((snaps, nx, ny, nz), jnp.float32),
            jax.ShapeDtypeStruct((ROWS, LANES), jnp.float32),
        ],
        scratch_shapes=[
            pltpu.VMEM((nx, 2 * z_shape[1], ROWS, LANES), jnp.float32),
            pltpu.VMEM((2, snaps * tiles, ROWS, LANES), jnp.float32),
            pltpu.VMEM((OUT_SLOTS, snaps, ny, nz), jnp.float32),
            pltpu.VMEM(pieces.shape[1:], jnp.bfloat16),
            pltpu.VMEM(pieces.shape[1:], jnp.bfloat16),
            pltpu.VMEM((3 * half, 2 * half), jnp.float32),
            pltpu.SemaphoreType.DMA((OUT_SLOTS,)),
        ],
        compiler_params=pltpu.CompilerParams(vmem_limit_bytes=5 << 20),
        cost_estimate=SMALL,
        name="step_and_sums",
    )(planes, base, pieces, diff, *z_halo)


def halo_terms(side, value, line):
    row = iota(0)
    sign = 1.0 - 2.0 * side
    factor = jnp.broadcast_to(line, (ROWS, LANES)) + sign * 1.2 / 12
    near = jnp.where(row % 2 == side, factor, 0.0) * pltpu.roll(value, 1 if side else ROWS - 1, 0)
    return near - sign * (0.15 / 12) * value


def extra_kernel(sums, lower, own, diff, sums_ref, mine, delta):
    nx, groups, _, nz = own.shape
    snaps = 4 * groups
    half = 2 * snaps

    def pieces(tiles):
        both = jnp.concatenate(tiles, axis=0)
        high = both.astype(jnp.bfloat16)
        return high, (both - high.astype(jnp.float32)).astype(jnp.bfloat16)

    for x in range(nx):
        for c in range(nz // LANES):
            part = slice(c * LANES, (c + 1) * LANES)
            under = [lower[x, group, :, part] for group in range(groups)]
            over = [own[x, group, :, part] for group in range(groups)]
            lines = diff[x, :1, part], lower[nx, x // ROWS, x % ROWS : x % ROWS + 1, part]
            for side in range(2):
                here, there = ((over, under), (under, over))[side]
                column = slice((2 * x + side) * nz + c * LANES, (2 * x + side) * nz + (c + 1) * LANES)
                high, low = pieces([halo_terms(side, value, lines[side]) for value in there])
                delta[:half, column] = high
                delta[half:, column] = low
                high, low = pieces(here)
                mine[:half, column] = high
                mine[half:, column] = low
    product = lax.dot_general(mine[...], delta[...], LAST, preferred_element_type=jnp.float32)
    same = (
        lax.broadcasted_iota(jnp.int32, product.shape, 0) % 2
        == lax.broadcasted_iota(jnp.int32, product.shape, 1) % 2
    )
    at = lax.broadcasted_iota(jnp.int32, (LANES, 2 * half), 1)
    to = lax.broadcasted_iota(jnp.int32, (LANES, 2 * half), 0)
    member = jnp.where((at % half) // 2 == to % snaps, 1.0, 0.0)
    masked = jnp.where(same, product, 0.0)
    extra = jnp.dot(member[:snaps], masked, precision=HIGH)
    extra = lax.dot_general(extra, member, LAST, precision=HIGH, preferred_element_type=jnp.float32)
    total = sums[...] + beside([jnp.zeros_like(extra), extra])
    folded = pltpu.roll(pltpu.roll(total, LANES // 2, 1), ROWS // 2, 0)
    total = jnp.where(iota(1) < LANES // 2, total, folded)
    sums_ref[...] = jnp.broadcast_to(total[None, : ROWS // 2], sums_ref.shape)


def extra_sums(sums, lower, own, diff, copies):
    nx, groups, _, nz = own.shape
    inside = pl.BlockSpec(memory_space=pltpu.VMEM)
    pieces = pltpu.VMEM((16 * groups, nx * 2 * nz), jnp.bfloat16)
    return pl.pallas_call(
        extra_kernel,
        in_specs=[inside] * 4,
        out_specs=inside,
        out_shape=jax.ShapeDtypeStruct((copies, ROWS // 2, LANES), jnp.float32),
        scratch_shapes=[pieces, pieces],
        compiler_params=pltpu.CompilerParams(vmem_limit_bytes=5 << 20),
        cost_estimate=SMALL,
        name="extra_sums",
    )(sums, lower, own, diff)


def fix_kernel(partial, lower, upper, diff, out_hbm, edge, new, in_sems, sems):
    nx, _, snaps, _, nz = edge.shape
    ny = diff.shape[1]
    row = iota(0)

    def fetch(x):
        return [
            pltpu.make_async_copy(partial.at[:, x, :ROWS], edge.at[x, 0], in_sems.at[2 * x]),
            pltpu.make_async_copy(partial.at[:, x, ny - ROWS :], edge.at[x, 1], in_sems.at[2 * x + 1]),
        ]

    for x in range(nx):
        for copy in fetch(x):
            copy.start()

    def sent(x):
        return [
            pltpu.make_async_copy(new.at[x, 0], out_hbm.at[:, x, :ROWS], sems.at[2 * x]),
            pltpu.make_async_copy(new.at[x, 1], out_hbm.at[:, x, ny - ROWS :], sems.at[2 * x + 1]),
        ]

    def fix(x, _):
        for copy in fetch(x):
            copy.wait()
        for side in range(2):
            halo = (lower, upper)[side]
            for c in range(nz // LANES):
                part = slice(c * LANES, (c + 1) * LANES)
                line = diff[x, ny - 1 :, part] if side else diff[x, :1, part]
                for group in range(snaps // 4):
                    terms = halo_terms(side, halo[x, group, :, part], line)
                    for place in range(4):
                        snap = 4 * group + place
                        turn = (6 * side + ROWS - 2 * place) % ROWS
                        mask = row >= ROWS - 2 if side else row < 2
                        term = jnp.where(mask, pltpu.roll(terms, turn, 0), 0.0)
                        new[x, side, snap, :, part] = edge[x, side, snap, :, part] + term
        for copy in sent(x):
            copy.start()
        return 0

    lax.fori_loop(0, nx, fix, 0)
    for x in range(nx):
        for copy in sent(x):
            copy.wait()


def fix_rows(partial, y_halo, diff):
    snaps, nx, _, nz = partial.shape
    edge = pltpu.VMEM((nx, 2, snaps, ROWS, nz), jnp.float32)
    done = pltpu.SemaphoreType.DMA((2 * nx,))
    anywhere, inside = pl.BlockSpec(memory_space=pl.ANY), pl.BlockSpec(memory_space=pltpu.VMEM)
    return pl.pallas_call(
        fix_kernel,
        in_specs=[anywhere] + [inside] * 3,
        out_specs=anywhere,
        out_shape=jax.ShapeDtypeStruct(partial.shape, jnp.float32),
        scratch_shapes=[edge, edge, done, done],
        input_output_aliases={0: 0},
        compiler_params=pltpu.CompilerParams(vmem_limit_bytes=10 << 20),
        cost_estimate=SMALL,
        name="fix_rows",
    )(partial, *y_halo, diff)


def spectral_kernel(
    ncell, sums_ref, reduced_ref, sigmas_ref
):
    count = sigmas_ref.shape[1]
    slots = count // 2
    row, lane = iota(0), iota(1)
    total = sums_ref[0]
    for i in range(1, sums_ref.shape[0]):
        total = total + sums_ref[i]
    total = total * (1.0 / ncell)
    total = jnp.concatenate([total, total], axis=0)
    total = jnp.where(row < ROWS // 2, total, pltpu.roll(total, LANES // 2, 1))

    def whole(tile, at):
        return jnp.broadcast_to(tile[at : at + 1], (ROWS, LANES))

    def shift(x, turn):
        return pltpu.roll(x, turn % ROWS, 0)

    gram = [
        [jnp.broadcast_to(total[:, part * count + j : part * count + j + 1], (ROWS, LANES)) for part in range(2)]
        for j in range(count)
    ]
    diagonal = [whole(gram[j][j // ROWS], j % ROWS) for j in range(count)]
    while len(diagonal) > 1:
        diagonal = [a + b for a, b in zip(diagonal[::2], diagonal[1::2])]
    unit = count / diagonal[0]
    gram = [[unit * part for part in column] for column in gram]
    rows = []
    inverse = [jnp.where(lane == row + count + part * ROWS, 1.0, 0.0) for part in range(2)]
    for j in range(count):
        part, at = divmod(j, ROWS)
        scale = lax.rsqrt(whole(gram[j][part], at))
        column = [jnp.where(row + i * ROWS >= j, gram[j][i] * scale, 0.0) for i in range(2)]
        for m in range(j + 1, count):
            factor = whole(column[m // ROWS], m % ROWS)
            gram[m] = [gram[m][i] - column[i] * factor for i in range(2)]
        line = whole(inverse[part], at) * scale
        for i in range(2):
            index = row + i * ROWS
            inverse[i] = jnp.where(
                index == j, line, inverse[i] - jnp.where(index > j, column[i], 0.0) * line
            )
        rows += column

    back = jnp.zeros((ROWS, LANES), jnp.float32)
    for i in range(slots):
        back = jnp.where(row == i, whole(inverse[1], ROWS - 1 - i), back)
    first = jnp.where(lane < count, jnp.where(lane == row, 1.0, 0.0), inverse[0])
    second = jnp.where(lane < count, jnp.where(lane == count - 1 - row, 1.0, 0.0), back)

    def join(a, b, turn):
        mask = (row & turn) == 0
        return jnp.where(mask, a, b) + jnp.where(mask, shift(a, -turn), shift(b, turn))

    def gather(parts):
        level = [join(parts[i], parts[i + 4], 4) for i in range(4)]
        level = [join(level[i], level[i + 2], 2) for i in range(2)]
        return join(level[0], level[1], 1)

    def norms(rows, players):
        return gather([rows[2 * p] * rows[2 * p] + rows[2 * p + 1] * rows[2 * p + 1] for p in players])

    heads, tails = list(range(slots)), list(range(count - 1, slots - 1, -1))

    def move(top, low):
        return (
            jnp.where(row == 0, top, shift(jnp.where(row == 0, low, top), 1)),
            jnp.where(row == ROWS - 1, top, shift(low, -1)),
        )

    def sweep(_, carry):
        rows, first, second = list(carry[:-2]), carry[-2], carry[-1]
        players = list(range(count))
        app, aqq = norms(rows, heads), norms(rows, tails)
        for turn in range(count - 1):
            pairs = [(players[i], players[count - 1 - i]) for i in range(slots)]
            apq = gather(
                [rows[2 * p] * rows[2 * q] + rows[2 * p + 1] * rows[2 * q + 1] for p, q in pairs]
            )
            tau = aqq - app
            twice = 2.0 * apq
            square = tau * tau + twice * twice
            turned = square > 0
            inverted = lax.rsqrt(square)
            doubled = jnp.where(turned, 0.5 + 0.5 * jnp.abs(tau) * inverted, 1.0)
            scaled = lax.rsqrt(doubled)
            cosine = doubled * scaled
            half_sine = jnp.where(turned, 0.5 * jnp.where(tau >= 0, twice, -twice) * inverted, 0.0)
            sine = half_sine * scaled
            tangent = sine * scaled
            for i, (p, q) in enumerate(pairs):
                c, s = whole(cosine, i), whole(sine, i)
                for k in range(2):
                    a, b = rows[2 * p + k], rows[2 * q + k]
                    rows[2 * p + k], rows[2 * q + k] = c * a - s * b, s * a + c * b
            first, second = move(cosine * first - sine * second, sine * first + cosine * second)
            app, aqq = move(app - tangent * apq, aqq + tangent * apq)
            players = [players[0], players[-1]] + players[1:-1]
        return (*rows, first, second)

    carry = lax.fori_loop(0, SWEEPS, sweep, (*rows, first, second), unroll=2)
    rows, first, second = carry[:-2], carry[-2], carry[-1]
    lam = [norms(rows, heads), norms(rows, tails)]
    index = [row, count - 1 - row]
    above = [jnp.zeros((ROWS, LANES), jnp.int32)] * 2
    ahead = [jnp.zeros((ROWS, LANES), jnp.int32)] * 2
    for p in range(count):
        other = whole(lam[0], p) if p < slots else whole(lam[1], count - 1 - p)
        for i in range(2):
            larger = other > lam[i]
            above[i] = above[i] + jnp.where(larger, 1, 0)
            ahead[i] = ahead[i] + jnp.where(larger | ((other == lam[i]) & (p < index[i])), 1, 0)
    keep = [jnp.where(a < RANK, 1.0, 0.0) for a in above]
    ordered = jnp.where(ahead[0] == lane, lam[0], 0.0) + jnp.where(ahead[1] == lane, lam[1], 0.0)
    ordered = jnp.sum(ordered, axis=0, keepdims=True)
    sigmas_ref[...] = jnp.sqrt(ordered / unit[:1])[:, :count]

    weight = [keep[i] / lam[i] for i in range(2)]
    weighted = [first * weight[0], second * weight[1]]
    tail = [jnp.zeros((ROWS, LANES), jnp.float32)] * 2
    for p in range(count):
        line = whole(weighted[0], p) if p < slots else whole(weighted[1], count - 1 - p)
        tail = [tail[k] + rows[2 * p + k] * line for k in range(2)]

    def dot(a, b, dims):
        return lax.dot_general(a, b, dims, precision=HIGH, preferred_element_type=jnp.float32)

    def tall(tiles, offset):
        blank = jnp.zeros((ROWS, LANES), jnp.float32)
        stack = [blank] * (offset // ROWS) + tiles
        return jnp.concatenate(stack + [blank] * (LANES // ROWS - len(stack)), axis=0)

    head = dot(
        jnp.concatenate([first, second], axis=0),
        jnp.concatenate([first * keep[0], second * keep[1]], axis=0),
        FIRST,
    )[:count]
    cross = [
        jnp.where(lane < count, pltpu.roll(total, LANES - (2 + i) * count, 1), 0.0) for i in range(2)
    ]
    plain = (((1,), (0,)), ((), ()))
    behind = dot(tall(cross, count), tall(tail, 0), plain)
    reduced_ref[...] = dot(head * unit[:1, :1], behind, plain)[:, :count]


def spectral(sums, count, ncell):
    return pl.pallas_call(
        functools.partial(spectral_kernel, ncell),
        out_shape=[
            jax.ShapeDtypeStruct((count, count), jnp.float32),
            jax.ShapeDtypeStruct((1, count), jnp.float32),
        ],
        compiler_params=pltpu.CompilerParams(vmem_limit_bytes=4 << 20),
        cost_estimate=SMALL,
        name="spectral",
    )(sums)


def inside_vmem(array):
    return pltpu.with_memory_space_constraint(array, pltpu.VMEM)


def shards(snapshots, diffusivity):
    snaps, nx, ny, nz = snapshots.shape
    copies = lax.axis_size(AXES)
    snapshots = pltpu.with_memory_space_constraint(snapshots, pltpu.HBM)
    diffusivity = pltpu.with_memory_space_constraint(diffusivity, pltpu.HBM)
    planes, factors, x_edge, y_low, y_high, z_low, z_high = pack_edges(snapshots, diffusivity)
    planes, factors = inside_vmem(planes), inside_vmem(factors)
    y_below, y_above = neighbours(y_low, y_high, "gy")
    z_halo = neighbours(z_low, z_high, "gz")
    if lax.axis_size("gx") == 2:
        x_halo = (lax.ppermute(x_edge, "gx", [(0, 1), (1, 0)]),) * 2
        x_places = (2, 0)
    else:
        x_halo = neighbours(x_edge[:2], x_edge[2:], "gx")
        x_places = (0, 0)
    planes, base, pieces = own_terms(planes, x_halo, x_places, factors)
    kept = [inside_vmem(planes), inside_vmem(base), inside_vmem(pieces), factors]
    partial, sums = step_and_sums(*kept, [inside_vmem(array) for array in z_halo])
    sums = extra_sums(sums, y_below, y_low, factors, copies)
    shifted = fix_rows(partial, (y_below, y_above), factors)
    sums = lax.all_to_all(sums, AXES, 0, 0, tiled=True)
    ncell = float(nx * ny * nz * copies)
    reduced, sigmas = spectral(sums, snaps, ncell)
    return shifted, reduced, sigmas.reshape(snaps)


def solution(mesh):
    placed = (P(None, "gx", "gy", "gz"), P("gx", "gy", "gz"))
    return jax.shard_map(
        shards,
        mesh=mesh,
        in_specs=placed,
        out_specs=(P(None, "gx", "gy", "gz"), P(), P()),
        check_vma=False,
    )
```
